32 devices in a mesh: replica: 4 (over x, core), expert: 8 (over z, y).
Axes of the slice: x: 2, y: 2, z: 4, core: 2. Of those that a mesh axis runs over, the one named last changes fastest.
Arguments:
- tokens: bfloat16 [4096, 2048], P(('replica', 'expert')), may hold values from -6 to 6
- routing: int32 [4096, 8], P(('replica', 'expert')), may hold values from 0 to 7, all different within a row; in each aligned block of 128 rows (0 to 127, 128 to 255, ...) at most 128 rows name the same one
- gate_scores: float32 [4096, 8], P(('replica', 'expert')), may hold values from 0.1 to 1
- cotangent: bfloat16 [4096, 2048], P(('replica', 'expert')), may hold values from -48 to 48
- w_gate: bfloat16 [4, 8, 2048, 384], P('replica', 'expert'), may hold values from -6 to 6
- w_up: bfloat16 [4, 8, 2048, 384], P('replica', 'expert'), may hold values from -6 to 6
- w_down: bfloat16 [4, 8, 384, 2048], P('replica', 'expert'), may hold values from -6 to 6
- mom_gate: bfloat16 [4, 8, 2048, 384], P('replica', 'expert'), may hold values from -3 to 3
- mom_up: bfloat16 [4, 8, 2048, 384], P('replica', 'expert'), may hold values from -3 to 3
- mom_down: bfloat16 [4, 8, 384, 2048], P('replica', 'expert'), may hold values from -3 to 3
- gossip_round: int32 [8], P('expert'), may hold values from 0 to 1
Outputs:
- layer_out: bfloat16 [4096, 2048], P(('replica', 'expert'))
- token_grad: bfloat16 [4096, 2048], P(('replica', 'expert'))
- new_gate: bfloat16 [4, 8, 2048, 384], P('replica', 'expert')
- new_up: bfloat16 [4, 8, 2048, 384], P('replica', 'expert')
- new_down: bfloat16 [4, 8, 384, 2048], P('replica', 'expert')
- new_mom_gate: bfloat16 [4, 8, 2048, 384], P('replica', 'expert')
- new_mom_up: bfloat16 [4, 8, 2048, 384], P('replica', 'expert')
- new_mom_down: bfloat16 [4, 8, 384, 2048], P('replica', 'expert')
The draws below stay inside these ranges and needn't reach their ends.
Inputs may be any that keep to these rules, and one draw needn't show every extreme that they name: `routing`: each token names 8 different experts; among the 128 tokens of one source no expert is named more than 128 times, a bound that some block reaches. `gossip_round`: each expert's round value names the bit distance of that expert's partner in this round.
All inputs are finite; a program needn't handle non-finite values.
Results may differ from the reference program's by a relative error of at most 0.0064.
Values may be sent and summed in bfloat16 or wider, within the bound.
No kernel may reach another device: no remote copies, remote signals or barrier semaphores. Data moves between devices by JAX's collectives and lax.ppermute only.
A program may use at most 192 MiB of HBM per device.

```python
import math
import jax
import jax.numpy as jnp
import numpy as np
from jax import lax

D = 2048
F = 384
TOPK = 8
TOK_DEV = 128
EXPERTS = 8
CAP = 128
TOKENS = 4096
N_REPLICA = 4


def plant(result, key, smallest, high):
    longest = result.shape.index(max(result.shape))
    spots = []
    for shift in (0, 1):
        where = [jax.random.randint(jax.random.fold_in(key, axis), (), 0, length) for axis, length in enumerate(result.shape)]
        where[longest] = (where[longest] + shift) % result.shape[longest]
        spots.append(tuple(where))
    return result.at[spots[0]].set(smallest).at[spots[1]].set(high)


def shard_levels(stream_key, dims, shards, low, high):
    def one(position, blocks):
        heights = jax.random.uniform(jax.random.fold_in(jax.random.fold_in(stream_key, 6), position), (blocks,), jnp.float32, low / len(shards), high / len(shards))
        return jnp.repeat(jnp.exp(heights), dims[position] // blocks).reshape((-1,) + (1,) * (len(dims) - position - 1))

    gain = one(*shards[0])
    for cut in shards[1:]:
        gain = gain * one(*cut)
    return gain


def assign_block(own_key, own, number, rows, amount, top, limit, slope):
    order = jax.random.permutation(own_key, amount)
    packed, common = portions_of(amount, rows * top, limit, slope, True), portions_of(amount, rows * top, limit, slope, False)
    places = jnp.arange(amount)

    def named(tallies, offset_by):
        used = int((tallies > 0).sum())
        fixed = max(1, used // 4)
        shifted = fixed + (places - fixed + offset_by * (used - fixed)) % max(1, amount - fixed)
        return jnp.zeros((amount,), jnp.int32).at[order[jnp.where(places < fixed, places, shifted)]].set(jnp.asarray(tallies, jnp.int32))

    tallies = jnp.where(number % 4 == 0, named(packed, number // 4), named(common, number - number // 4 - 1))
    mixed = jax.random.permutation(jax.random.fold_in(own, 3), amount)
    source_of, taker = mixed[0:amount // 2 * 2:2], mixed[1:amount // 2 * 2:2]
    slack = jnp.minimum(tallies[source_of] - 1, limit - tallies[taker]) // 2
    slack = jnp.where((source_of == order[0]) | (taker == order[0]) | (tallies[taker] == 0), 0, jnp.maximum(slack, 0))
    shifted = jax.random.randint(jax.random.fold_in(own, 4), (amount // 2,), 0, 1 << 20) % (slack + 1)
    tallies = tallies.at[source_of].add(-shifted).at[taker].add(shifted)
    items = jnp.searchsorted(jnp.cumsum(tallies), jnp.arange(rows * top), side="right").astype(jnp.int32)
    grid = items.reshape(top, rows).T
    grid = grid[jax.random.permutation(jax.random.fold_in(own, 1), rows)]
    offset_by = jax.random.randint(jax.random.fold_in(own, 2), (rows, 1), 0, top)
    return jnp.take_along_axis(grid, (jnp.arange(top)[None, :] + offset_by) % top, axis=1)


def portions_of(number_of, total, bound, lean, full):
    loads = [(1 << 20) // math.isqrt(standing ** lean) + 1 for standing in range(1, number_of + 1)]
    largest = bound if full else min(bound, max(-(-total // number_of), total * loads[0] // sum(loads)))
    least = 1 if total - largest >= number_of - 1 else 0
    holding, spare = [largest] + [least] * (number_of - 1), total - largest - least * (number_of - 1)
    while spare > 0:
        free = [i for i in range(1, number_of) if holding[i] < largest] or [i for i in range(1, number_of) if holding[i] < bound]
        whole, remaining = sum([loads[i] for i in free]), spare
        for i in free:
            extra = min(bound - holding[i], max(1, remaining * loads[i] // whole), spare)
            holding[i] = holding[i] + extra
            spare = spare - extra
    return np.array(holding)


def noise(stream_key, dims, deviation, most, cuts=(), held_as=jnp.bfloat16):
    entries = jax.random.normal(stream_key, dims, jnp.float32) * deviation
    if len(cuts) > 0:
        entries = shard_levels(stream_key, dims, cuts, -0.22, 0.18) * entries
    return jnp.clip(entries, min=-most, max=most).astype(held_as)


def setup_inputs(seed: int = 0) -> dict:
    streams_of = jax.random.split(jax.random.key(seed), 12)
    tokens = noise(streams_of[0], (TOKENS, D), 1.0, 6.0, ((0, 32),))
    routing_keys = jax.random.split(jax.random.fold_in(streams_of[1], 1), TOKENS // TOK_DEV)
    routing_turns = jax.random.permutation(jax.random.fold_in(streams_of[1], 3), TOKENS // TOK_DEV)
    routing = jax.vmap(lambda own, number: assign_block(jax.random.fold_in(streams_of[1], 2), own, number, TOK_DEV, EXPERTS, TOPK, CAP, 2))(routing_keys, routing_turns).reshape((TOKENS, TOPK))
    gate_scores = jnp.clip(jnp.exp(math.log(1.0) - 2.3025851 * jax.random.uniform(streams_of[2], (TOKENS, TOPK), jnp.float32) ** shard_levels(streams_of[2], (TOKENS, TOPK), ((0, 32),), -0.2, 0.2)), 0.1, 1.0)
    cotangent = noise(streams_of[3], (TOKENS, D), 8.0, 48.0, ((0, 32),))
    w_gate = noise(streams_of[4], (N_REPLICA, EXPERTS, D, F), 1.0, 6.0, ((0, 4), (1, 8)))
    w_up = noise(streams_of[5], (N_REPLICA, EXPERTS, D, F), 1.0, 6.0, ((0, 4), (1, 8)))
    w_down = noise(streams_of[6], (N_REPLICA, EXPERTS, F, D), 1.0, 6.0, ((0, 4), (1, 8)))
    mom_gate = noise(streams_of[7], (N_REPLICA, EXPERTS, D, F), 0.5, 3.0, ((0, 4), (1, 8)))
    mom_up = noise(streams_of[8], (N_REPLICA, EXPERTS, D, F), 0.5, 3.0, ((0, 4), (1, 8)))
    mom_down = noise(streams_of[9], (N_REPLICA, EXPERTS, F, D), 0.5, 3.0, ((0, 4), (1, 8)))
    gossip_round = plant(jax.random.randint(streams_of[10], (EXPERTS,), 0, 2), jax.random.fold_in(streams_of[10], 1), 0, 1).astype(jnp.int32)
    return dict(tokens=tokens, routing=routing, gate_scores=gate_scores, cotangent=cotangent, w_gate=w_gate, w_up=w_up, w_down=w_down, mom_gate=mom_gate, mom_up=mom_up, mom_down=mom_down, gossip_round=gossip_round)


momentum_beta = 0.9
learn_rate = 0.1


def expert_forward(rows_in, weight_gate, weight_up, weight_down):
    scale_in = rows_in.shape[1] ** -0.5
    scale_hidden = weight_gate.shape[1] ** -0.5
    gate_pre = jnp.dot(rows_in, weight_gate, preferred_element_type=jnp.float32) * scale_in
    up_pre = jnp.dot(rows_in, weight_up, preferred_element_type=jnp.float32) * scale_in
    sigmoid_gate = jax.nn.sigmoid(gate_pre)
    activation = (gate_pre * sigmoid_gate * up_pre).astype(jnp.bfloat16)
    produced = (jnp.dot(activation, weight_down, preferred_element_type=jnp.float32) * scale_hidden).astype(jnp.bfloat16)
    return gate_pre, up_pre, sigmoid_gate, activation, produced


def expert_backward(rows_in, rows_grad, weight_gate, weight_up, weight_down, gate_pre, up_pre, sigmoid_gate, activation):
    scale_in = rows_in.shape[1] ** -0.5
    scale_hidden = weight_gate.shape[1] ** -0.5
    inner_dims = (((1,), (1,)), ((), ()))
    outer_dims = (((0,), (0,)), ((), ()))
    grad_act = lax.dot_general(rows_grad, weight_down, inner_dims, preferred_element_type=jnp.float32) * scale_hidden
    grad_gate_pre = (grad_act * up_pre * sigmoid_gate * (1.0 + gate_pre * (1.0 - sigmoid_gate))).astype(jnp.bfloat16)
    grad_up_pre = (grad_act * gate_pre * sigmoid_gate).astype(jnp.bfloat16)
    grad_down = lax.dot_general(activation, rows_grad, outer_dims, preferred_element_type=jnp.float32) * scale_hidden
    grad_gate = lax.dot_general(rows_in, grad_gate_pre, outer_dims, preferred_element_type=jnp.float32) * scale_in
    grad_up = lax.dot_general(rows_in, grad_up_pre, outer_dims, preferred_element_type=jnp.float32) * scale_in
    back_sum = lax.dot_general(grad_gate_pre, weight_gate, inner_dims, preferred_element_type=jnp.float32)
    back_sum = back_sum + lax.dot_general(grad_up_pre, weight_up, inner_dims, preferred_element_type=jnp.float32)
    rows_back = (back_sum * scale_in).astype(jnp.bfloat16)
    return rows_back, grad_gate, grad_up, grad_down


def momentum_step(weight, moment, gradient):
    moment_new = momentum_beta * moment.astype(jnp.float32) + gradient
    weight_new = (weight.astype(jnp.float32) - learn_rate * moment_new).astype(jnp.bfloat16)
    return weight_new, moment_new.astype(jnp.bfloat16)


def reference(tokens, routing, gate_scores, cotangent, w_gate, w_up, w_down, mom_gate, mom_up, mom_down, gossip_round):
    sources = EXPERTS
    pair_count = TOK_DEV * TOPK
    outs_list = []
    grads_list = []
    local_lists = [[], [], [], [], [], []]
    token_of = jnp.arange(pair_count, dtype=jnp.int32) // TOPK
    source_ids = jnp.broadcast_to(jnp.arange(sources, dtype=jnp.int32)[:, None], (sources, pair_count))
    for replica_id in range(N_REPLICA):
        first = replica_id * sources * TOK_DEV
        tok_block = tokens[first:first + sources * TOK_DEV].reshape(sources, TOK_DEV, D)
        cot_block = cotangent[first:first + sources * TOK_DEV].reshape(sources, TOK_DEV, D)
        scores = gate_scores[first:first + sources * TOK_DEV].reshape(sources, TOK_DEV, TOPK)
        gate_share = (scores / jnp.sum(scores, axis=2, keepdims=True)).reshape(sources, pair_count)
        expert_ids = routing[first:first + sources * TOK_DEV].reshape(sources, pair_count)
        member = (expert_ids[:, :, None] == jnp.arange(EXPERTS, dtype=jnp.int32)[None, None, :]).astype(jnp.int32)
        earlier = jnp.sum((jnp.cumsum(member, axis=1) - member) * member, axis=2).astype(jnp.int32)
        pair_rows = tok_block[:, token_of]
        pair_grad = (gate_share[:, :, None] * cot_block[:, token_of].astype(jnp.float32)).astype(jnp.bfloat16)
        buffer_x = jnp.zeros((EXPERTS, sources, CAP, D), jnp.bfloat16).at[expert_ids, source_ids, earlier].set(pair_rows)
        buffer_g = jnp.zeros((EXPERTS, sources, CAP, D), jnp.bfloat16).at[expert_ids, source_ids, earlier].set(pair_grad)
        buffer_x = buffer_x.reshape(EXPERTS, sources * CAP, D)
        buffer_g = buffer_g.reshape(EXPERTS, sources * CAP, D)

        def per_expert(items):
            rows_in, rows_grad, weight_gate, weight_up, weight_down, moment_gate, moment_up, moment_down = items
            gate_pre, up_pre, sigmoid_gate, activation, produced = expert_forward(rows_in, weight_gate, weight_up, weight_down)
            rows_back, grad_gate, grad_up, grad_down = expert_backward(rows_in, rows_grad, weight_gate, weight_up, weight_down, gate_pre, up_pre, sigmoid_gate, activation)
            gate_new, gate_moment = momentum_step(weight_gate, moment_gate, grad_gate)
            up_new, up_moment = momentum_step(weight_up, moment_up, grad_up)
            down_new, down_moment = momentum_step(weight_down, moment_down, grad_down)
            return produced, rows_back, gate_new, up_new, down_new, gate_moment, up_moment, down_moment

        results = lax.map(per_expert, (buffer_x, buffer_g, w_gate[replica_id], w_up[replica_id], w_down[replica_id], mom_gate[replica_id], mom_up[replica_id], mom_down[replica_id]))
        produced_all = results[0].reshape(EXPERTS, sources, CAP, D)
        back_all = results[1].reshape(EXPERTS, sources, CAP, D)
        picked = produced_all[expert_ids, source_ids, earlier].astype(jnp.float32)
        picked_back = back_all[expert_ids, source_ids, earlier].astype(jnp.float32)
        mixed_rows = jnp.sum((picked * gate_share[:, :, None]).reshape(sources, TOK_DEV, TOPK, D), axis=2)
        back_rows = jnp.sum(picked_back.reshape(sources, TOK_DEV, TOPK, D), axis=2)
        outs_list.append(mixed_rows.astype(jnp.bfloat16).reshape(sources * TOK_DEV, D))
        grads_list.append(back_rows.astype(jnp.bfloat16).reshape(sources * TOK_DEV, D))
        for index_item in range(6):
            local_lists[index_item].append(results[2 + index_item])
    layer_out = jnp.concatenate(outs_list, axis=0)
    token_grad = jnp.concatenate(grads_list, axis=0)
    bit_count = N_REPLICA.bit_length() - 1
    bit_now = (gossip_round % bit_count).astype(jnp.int32)
    replica_ids = jnp.arange(N_REPLICA, dtype=jnp.int32)[:, None]
    partner_ids = jnp.bitwise_xor(replica_ids, jnp.left_shift(jnp.ones((), jnp.int32), bit_now)[None, :]).astype(jnp.int32)
    expert_index = jnp.broadcast_to(jnp.arange(EXPERTS, dtype=jnp.int32)[None, :], (N_REPLICA, EXPERTS))
    averaged = []
    for index_item in range(3):
        stacked_local = jnp.stack(local_lists[index_item], axis=0)
        partner_w = stacked_local[partner_ids, expert_index]
        averaged.append(((stacked_local.astype(jnp.float32) + partner_w.astype(jnp.float32)) * 0.5).astype(jnp.bfloat16))
    moments = [jnp.stack(local_lists[3 + index_item], axis=0) for index_item in range(3)]
    return (layer_out, token_grad, averaged[0], averaged[1], averaged[2], moments[0], moments[1], moments[2])
```

```python
import jax
import jax.numpy as jnp
from jax import lax
from jax.sharding import PartitionSpec as P

momentum_beta = 0.9
learn_rate = 0.1


def partner_2(value, axis, stride):
    mask = 2**stride
    pairs = [(source, source ^ mask) for source in range(lax.axis_size(axis))]
    return lax.ppermute(value, axis, pairs)


def expert_forward(rows_in, weight_gate, weight_up, weight_down):
    scale_in = rows_in.shape[1] ** (-0.5)
    scale_hidden = weight_gate.shape[1] ** (-0.5)
    gate_pre = jnp.dot(rows_in, weight_gate, preferred_element_type=jnp.float32) * scale_in
    up_pre = jnp.dot(rows_in, weight_up, preferred_element_type=jnp.float32) * scale_in
    sigmoid_gate = jax.nn.sigmoid(gate_pre)
    activation = (gate_pre * sigmoid_gate * up_pre).astype(jnp.bfloat16)
    produced = (
        jnp.dot(activation, weight_down, preferred_element_type=jnp.float32) * scale_hidden
    ).astype(jnp.bfloat16)
    return (gate_pre, up_pre, sigmoid_gate, activation, produced)


def expert_backward(
    rows_in,
    rows_grad,
    weight_gate,
    weight_up,
    weight_down,
    gate_pre,
    up_pre,
    sigmoid_gate,
    activation,
):
    scale_in = rows_in.shape[1] ** (-0.5)
    scale_hidden = weight_gate.shape[1] ** (-0.5)
    inner_dims = (((1,), (1,)), ((), ()))
    outer_dims = (((0,), (0,)), ((), ()))
    grad_act = (
        lax.dot_general(rows_grad, weight_down, inner_dims, preferred_element_type=jnp.float32)
        * scale_hidden
    )
    grad_gate_pre = (
        grad_act * up_pre * sigmoid_gate * (1.0 + gate_pre * (1.0 - sigmoid_gate))
    ).astype(jnp.bfloat16)
    grad_up_pre = (grad_act * gate_pre * sigmoid_gate).astype(jnp.bfloat16)
    grad_down = (
        lax.dot_general(activation, rows_grad, outer_dims, preferred_element_type=jnp.float32)
        * scale_hidden
    )
    grad_gate = (
        lax.dot_general(rows_in, grad_gate_pre, outer_dims, preferred_element_type=jnp.float32)
        * scale_in
    )
    grad_up = (
        lax.dot_general(rows_in, grad_up_pre, outer_dims, preferred_element_type=jnp.float32)
        * scale_in
    )
    back_sum = lax.dot_general(
        grad_gate_pre, weight_gate, inner_dims, preferred_element_type=jnp.float32
    )
    back_sum = back_sum + lax.dot_general(
        grad_up_pre, weight_up, inner_dims, preferred_element_type=jnp.float32
    )
    rows_back = (back_sum * scale_in).astype(jnp.bfloat16)
    return (rows_back, grad_gate, grad_up, grad_down)


def momentum_step(weight, moment, gradient):
    moment_new = momentum_beta * moment.astype(jnp.float32) + gradient
    weight_new = (weight.astype(jnp.float32) - learn_rate * moment_new).astype(jnp.bfloat16)
    return (weight_new, moment_new.astype(jnp.bfloat16))


def per_device_routed(
    tokens,
    routing,
    gate_scores,
    cotangent,
    w_gate,
    w_up,
    w_down,
    mom_gate,
    mom_up,
    mom_down,
    gossip_round,
):
    tok_rows, feature_width = tokens.shape
    top_count = routing.shape[1]
    experts = lax.axis_size("expert")
    capacity = max(2, min(tok_rows, tok_rows * top_count // experts + 8))
    gate_share = gate_scores / jnp.sum(gate_scores, axis=1, keepdims=True)
    expert_ids = routing.reshape(-1)
    member = (expert_ids[:, None] == jnp.arange(experts, dtype=jnp.int32)[None, :]).astype(
        jnp.int32
    )
    earlier = jnp.sum((jnp.cumsum(member, axis=0) - member) * member, axis=1)
    target = expert_ids * capacity + earlier
    source = jnp.arange(expert_ids.shape[0], dtype=jnp.int32) // top_count
    send_rows = (
        jnp.zeros((experts * capacity, feature_width), jnp.bfloat16).at[target].set(tokens[source])
    )
    weighted = (gate_share.reshape(-1)[:, None] * cotangent[source].astype(jnp.float32)).astype(
        jnp.bfloat16
    )
    send_grad = (
        jnp.zeros((experts * capacity, feature_width), jnp.bfloat16).at[target].set(weighted)
    )
    arrived = lax.all_to_all(
        send_rows.reshape(experts, capacity, feature_width),
        "expert",
        split_axis=0,
        concat_axis=0,
        tiled=True,
    ).reshape(-1, feature_width)
    arrived_grad = lax.all_to_all(
        send_grad.reshape(experts, capacity, feature_width),
        "expert",
        split_axis=0,
        concat_axis=0,
        tiled=True,
    ).reshape(-1, feature_width)
    weight_gate = w_gate[0, 0]
    weight_up = w_up[0, 0]
    weight_down = w_down[0, 0]
    gate_pre, up_pre, sigmoid_gate, activation, produced = expert_forward(
        arrived, weight_gate, weight_up, weight_down
    )
    returned = lax.all_to_all(
        produced.reshape(experts, capacity, feature_width),
        "expert",
        split_axis=0,
        concat_axis=0,
        tiled=True,
    ).reshape(-1, feature_width)
    picked = returned[target].astype(jnp.float32) * gate_share.reshape(-1)[:, None]
    layer_out = jnp.sum(picked.reshape(tok_rows, top_count, feature_width), axis=1).astype(
        jnp.bfloat16
    )
    rows_back, grad_gate, grad_up, grad_down = expert_backward(
        arrived,
        arrived_grad,
        weight_gate,
        weight_up,
        weight_down,
        gate_pre,
        up_pre,
        sigmoid_gate,
        activation,
    )
    returned_grad = lax.all_to_all(
        rows_back.reshape(experts, capacity, feature_width),
        "expert",
        split_axis=0,
        concat_axis=0,
        tiled=True,
    ).reshape(-1, feature_width)
    picked_back = returned_grad[target].astype(jnp.float32)
    token_grad = jnp.sum(picked_back.reshape(tok_rows, top_count, feature_width), axis=1).astype(
        jnp.bfloat16
    )
    gate_new, gate_moment = momentum_step(weight_gate, mom_gate[0, 0], grad_gate)
    up_new, up_moment = momentum_step(weight_up, mom_up[0, 0], grad_up)
    down_new, down_moment = momentum_step(weight_down, mom_down[0, 0], grad_down)
    hidden_width = weight_gate.shape[1]
    stacked = jnp.stack([gate_new, up_new, down_new.reshape(feature_width, hidden_width)], axis=0)
    bit_count = lax.axis_size("replica").bit_length() - 1
    bit_now = gossip_round[0] % bit_count
    partner = stacked
    for bit_index in range(bit_count):
        swapped = partner_2(stacked, "replica", bit_index)
        partner = jnp.where(bit_now == bit_index, swapped, partner)
    averaged = ((stacked.astype(jnp.float32) + partner.astype(jnp.float32)) * 0.5).astype(
        jnp.bfloat16
    )
    new_gate = averaged[0][None, None]
    new_up = averaged[1][None, None]
    new_down = averaged[2].reshape(hidden_width, feature_width)[None, None]
    return (
        layer_out,
        token_grad,
        new_gate,
        new_up,
        new_down,
        gate_moment[None, None],
        up_moment[None, None],
        down_moment[None, None],
    )


def per_device_dense(
    tokens,
    routing,
    gate_scores,
    cotangent,
    w_gate,
    w_up,
    w_down,
    mom_gate,
    mom_up,
    mom_down,
    gossip_round,
):
    tok_rows, feature_width = tokens.shape
    experts = lax.axis_size("expert")
    me = lax.axis_index("expert")
    weight_gate = w_gate[0, 0]
    weight_up = w_up[0, 0]
    weight_down = w_down[0, 0]
    hidden_width = weight_gate.shape[1]
    scale_in = feature_width ** (-0.5)
    scale_hidden = hidden_width ** (-0.5)
    inner_dims = (((1,), (1,)), ((), ()))
    outer_dims = (((0,), (0,)), ((), ()))
    gate_share = gate_scores / jnp.sum(gate_scores, axis=1, keepdims=True)
    names = routing[:, :, None] == jnp.arange(experts, dtype=jnp.int32)[None, None, :]
    share_by_expert = jnp.sum(jnp.where(names, gate_share[:, :, None], 0.0), axis=1)
    shares = lax.all_gather(share_by_expert, "expert", axis=0, tiled=True)
    share = jnp.sum(
        jnp.where(jnp.arange(experts, dtype=jnp.int32)[None, :] == me, shares, 0.0),
        axis=1,
        keepdims=True,
    )
    rows_in = lax.all_gather(tokens, "expert", axis=0, tiled=True)
    rows_cot = lax.all_gather(cotangent, "expert", axis=0, tiled=True)

    gate_pre = jnp.dot(rows_in, weight_gate, preferred_element_type=jnp.float32) * scale_in
    up_pre = jnp.dot(rows_in, weight_up, preferred_element_type=jnp.float32) * scale_in
    sigmoid_gate = jax.nn.sigmoid(gate_pre)
    activation = (gate_pre * sigmoid_gate * up_pre * share).astype(jnp.bfloat16)
    part_out = (
        jnp.dot(activation, weight_down, preferred_element_type=jnp.float32) * scale_hidden
    ).astype(jnp.bfloat16)
    layer_out = lax.psum_scatter(part_out, "expert", scatter_dimension=0, tiled=True)

    grad_down = (
        lax.dot_general(activation, rows_cot, outer_dims, preferred_element_type=jnp.float32)
        * scale_hidden
    )
    grad_act = lax.dot_general(
        rows_cot, weight_down, inner_dims, preferred_element_type=jnp.float32
    ) * (share * scale_hidden)
    grad_gate_pre = (
        grad_act * up_pre * sigmoid_gate * (1.0 + gate_pre * (1.0 - sigmoid_gate))
    ).astype(jnp.bfloat16)
    grad_up_pre = (grad_act * gate_pre * sigmoid_gate).astype(jnp.bfloat16)
    grad_gate = (
        lax.dot_general(rows_in, grad_gate_pre, outer_dims, preferred_element_type=jnp.float32)
        * scale_in
    )
    grad_up = (
        lax.dot_general(rows_in, grad_up_pre, outer_dims, preferred_element_type=jnp.float32)
        * scale_in
    )
    back_sum = lax.dot_general(
        grad_gate_pre, weight_gate, inner_dims, preferred_element_type=jnp.float32
    )
    back_sum = back_sum + lax.dot_general(
        grad_up_pre, weight_up, inner_dims, preferred_element_type=jnp.float32
    )
    part_back = (back_sum * scale_in).astype(jnp.bfloat16)
    token_grad = lax.psum_scatter(part_back, "expert", scatter_dimension=0, tiled=True)

    bit_count = lax.axis_size("replica").bit_length() - 1
    bit_now = gossip_round[0] % bit_count

    def averaged(local):
        partner = local
        for bit_index in range(bit_count):
            swapped = partner_2(local, "replica", bit_index)
            partner = jnp.where(bit_now == bit_index, swapped, partner)
        mean = (local.astype(jnp.float32) + partner.astype(jnp.float32)) * 0.5
        return mean.astype(jnp.bfloat16)[None, None]

    down_new, down_moment = momentum_step(weight_down, mom_down[0, 0], grad_down)
    gate_new, gate_moment = momentum_step(weight_gate, mom_gate[0, 0], grad_gate)
    up_new, up_moment = momentum_step(weight_up, mom_up[0, 0], grad_up)
    new_down = averaged(down_new)
    new_gate = averaged(gate_new)
    new_up = averaged(up_new)
    return (
        layer_out,
        token_grad,
        new_gate,
        new_up,
        new_down,
        gate_moment[None, None],
        up_moment[None, None],
        down_moment[None, None],
    )


def per_device(tokens, routing, *others):
    if routing.shape[1] == lax.axis_size("expert"):
        return per_device_dense(tokens, routing, *others)
    return per_device_routed(tokens, routing, *others)


def solution(mesh):
    placed = (
        P(("replica", "expert"), None),
        P(("replica", "expert"), None),
        P(("replica", "expert"), None),
        P(("replica", "expert"), None),
        P("replica", "expert", None, None),
        P("replica", "expert", None, None),
        P("replica", "expert", None, None),
        P("replica", "expert", None, None),
        P("replica", "expert", None, None),
        P("replica", "expert", None, None),
        P("expert"),
    )
    return jax.shard_map(
        per_device,
        mesh=mesh,
        in_specs=placed,
        out_specs=(
            P(("replica", "expert"), None),
            P(("replica", "expert"), None),
            P("replica", "expert", None, None),
            P("replica", "expert", None, None),
            P("replica", "expert", None, None),
            P("replica", "expert", None, None),
            P("replica", "expert", None, None),
            P("replica", "expert", None, None),
        ),
        check_vma=False,
    )
```

```python
import jax
import jax.numpy as jnp
from jax import lax
from jax.sharding import PartitionSpec as P

momentum_beta = 0.9
learn_rate = 0.1


def partner_2(value, axis, stride):
    mask = 2**stride
    pairs = [(source, source ^ mask) for source in range(lax.axis_size(axis))]
    return lax.ppermute(value, axis, pairs)


def expert_forward(rows_in, weight_gate, weight_up, weight_down):
    scale_in = rows_in.shape[1] ** (-0.5)
    scale_hidden = weight_gate.shape[1] ** (-0.5)
    gate_pre = jnp.dot(rows_in, weight_gate, preferred_element_type=jnp.float32) * scale_in
    up_pre = jnp.dot(rows_in, weight_up, preferred_element_type=jnp.float32) * scale_in
    sigmoid_gate = jax.nn.sigmoid(gate_pre)
    activation = (gate_pre * sigmoid_gate * up_pre).astype(jnp.bfloat16)
    produced = (
        jnp.dot(activation, weight_down, preferred_element_type=jnp.float32) * scale_hidden
    ).astype(jnp.bfloat16)
    return (gate_pre, up_pre, sigmoid_gate, activation, produced)


def expert_backward(
    rows_in,
    rows_grad,
    weight_gate,
    weight_up,
    weight_down,
    gate_pre,
    up_pre,
    sigmoid_gate,
    activation,
):
    scale_in = rows_in.shape[1] ** (-0.5)
    scale_hidden = weight_gate.shape[1] ** (-0.5)
    inner_dims = (((1,), (1,)), ((), ()))
    outer_dims = (((0,), (0,)), ((), ()))
    grad_act = (
        lax.dot_general(rows_grad, weight_down, inner_dims, preferred_element_type=jnp.float32)
        * scale_hidden
    )
    grad_gate_pre = (
        grad_act * up_pre * sigmoid_gate * (1.0 + gate_pre * (1.0 - sigmoid_gate))
    ).astype(jnp.bfloat16)
    grad_up_pre = (grad_act * gate_pre * sigmoid_gate).astype(jnp.bfloat16)
    grad_down = (
        lax.dot_general(activation, rows_grad, outer_dims, preferred_element_type=jnp.float32)
        * scale_hidden
    )
    grad_gate = (
        lax.dot_general(rows_in, grad_gate_pre, outer_dims, preferred_element_type=jnp.float32)
        * scale_in
    )
    grad_up = (
        lax.dot_general(rows_in, grad_up_pre, outer_dims, preferred_element_type=jnp.float32)
        * scale_in
    )
    back_sum = lax.dot_general(
        grad_gate_pre, weight_gate, inner_dims, preferred_element_type=jnp.float32
    )
    back_sum = back_sum + lax.dot_general(
        grad_up_pre, weight_up, inner_dims, preferred_element_type=jnp.float32
    )
    rows_back = (back_sum * scale_in).astype(jnp.bfloat16)
    return (rows_back, grad_gate, grad_up, grad_down)


def momentum_step(weight, moment, gradient):
    moment_new = momentum_beta * moment.astype(jnp.float32) + gradient
    weight_new = (weight.astype(jnp.float32) - learn_rate * moment_new).astype(jnp.bfloat16)
    return (weight_new, moment_new.astype(jnp.bfloat16))


def per_device_routed(
    tokens,
    routing,
    gate_scores,
    cotangent,
    w_gate,
    w_up,
    w_down,
    mom_gate,
    mom_up,
    mom_down,
    gossip_round,
):
    tok_rows, feature_width = tokens.shape
    top_count = routing.shape[1]
    experts = lax.axis_size("expert")
    capacity = max(2, min(tok_rows, tok_rows * top_count // experts + 8))
    gate_share = gate_scores / jnp.sum(gate_scores, axis=1, keepdims=True)
    expert_ids = routing.reshape(-1)
    member = (expert_ids[:, None] == jnp.arange(experts, dtype=jnp.int32)[None, :]).astype(
        jnp.int32
    )
    earlier = jnp.sum((jnp.cumsum(member, axis=0) - member) * member, axis=1)
    target = expert_ids * capacity + earlier
    source = jnp.arange(expert_ids.shape[0], dtype=jnp.int32) // top_count
    send_rows = (
        jnp.zeros((experts * capacity, feature_width), jnp.bfloat16).at[target].set(tokens[source])
    )
    weighted = (gate_share.reshape(-1)[:, None] * cotangent[source].astype(jnp.float32)).astype(
        jnp.bfloat16
    )
    send_grad = (
        jnp.zeros((experts * capacity, feature_width), jnp.bfloat16).at[target].set(weighted)
    )
    arrived = lax.all_to_all(
        send_rows.reshape(experts, capacity, feature_width),
        "expert",
        split_axis=0,
        concat_axis=0,
        tiled=True,
    ).reshape(-1, feature_width)
    arrived_grad = lax.all_to_all(
        send_grad.reshape(experts, capacity, feature_width),
        "expert",
        split_axis=0,
        concat_axis=0,
        tiled=True,
    ).reshape(-1, feature_width)
    weight_gate = w_gate[0, 0]
    weight_up = w_up[0, 0]
    weight_down = w_down[0, 0]
    gate_pre, up_pre, sigmoid_gate, activation, produced = expert_forward(
        arrived, weight_gate, weight_up, weight_down
    )
    returned = lax.all_to_all(
        produced.reshape(experts, capacity, feature_width),
        "expert",
        split_axis=0,
        concat_axis=0,
        tiled=True,
    ).reshape(-1, feature_width)
    picked = returned[target].astype(jnp.float32) * gate_share.reshape(-1)[:, None]
    layer_out = jnp.sum(picked.reshape(tok_rows, top_count, feature_width), axis=1).astype(
        jnp.bfloat16
    )
    rows_back, grad_gate, grad_up, grad_down = expert_backward(
        arrived,
        arrived_grad,
        weight_gate,
        weight_up,
        weight_down,
        gate_pre,
        up_pre,
        sigmoid_gate,
        activation,
    )
    returned_grad = lax.all_to_all(
        rows_back.reshape(experts, capacity, feature_width),
        "expert",
        split_axis=0,
        concat_axis=0,
        tiled=True,
    ).reshape(-1, feature_width)
    picked_back = returned_grad[target].astype(jnp.float32)
    token_grad = jnp.sum(picked_back.reshape(tok_rows, top_count, feature_width), axis=1).astype(
        jnp.bfloat16
    )
    gate_new, gate_moment = momentum_step(weight_gate, mom_gate[0, 0], grad_gate)
    up_new, up_moment = momentum_step(weight_up, mom_up[0, 0], grad_up)
    down_new, down_moment = momentum_step(weight_down, mom_down[0, 0], grad_down)
    hidden_width = weight_gate.shape[1]
    stacked = jnp.stack([gate_new, up_new, down_new.reshape(feature_width, hidden_width)], axis=0)
    bit_count = lax.axis_size("replica").bit_length() - 1
    bit_now = gossip_round[0] % bit_count
    partner = stacked
    for bit_index in range(bit_count):
        swapped = partner_2(stacked, "replica", bit_index)
        partner = jnp.where(bit_now == bit_index, swapped, partner)
    averaged = ((stacked.astype(jnp.float32) + partner.astype(jnp.float32)) * 0.5).astype(
        jnp.bfloat16
    )
    new_gate = averaged[0][None, None]
    new_up = averaged[1][None, None]
    new_down = averaged[2].reshape(hidden_width, feature_width)[None, None]
    return (
        layer_out,
        token_grad,
        new_gate,
        new_up,
        new_down,
        gate_moment[None, None],
        up_moment[None, None],
        down_moment[None, None],
    )


def ring_order(experts):
    return list(range(0, experts, 2)) + list(range(experts - 1, 0, -2))


def ring_hop(value, experts, step):
    order = ring_order(experts)
    pairs = [(order[i], order[(i + step) % experts]) for i in range(experts)]
    return lax.ppermute(value, "expert", pairs)


def ring_gather(own, experts):
    half = own.shape[0] // 2
    last = experts // 2
    blocks = [None] * experts
    blocks[0] = own
    behind = ahead = own
    for step in range(1, last):
        behind = ring_hop(behind, experts, 1)
        ahead = ring_hop(ahead, experts, -1)
        blocks[experts - step] = behind
        blocks[step] = ahead
    top = ring_hop(behind[:half], experts, 1)
    bottom = ring_hop(ahead[half:], experts, -1)
    blocks[last] = jnp.concatenate([top, bottom], axis=0)
    return blocks


def ring_scatter(parts, experts):
    half = parts[0].shape[0] // 2
    last = experts // 2
    f32 = jnp.float32
    forward = ring_hop(parts[last][:half].astype(jnp.bfloat16), experts, 1)
    backward = ring_hop(parts[last][half:].astype(jnp.bfloat16), experts, -1)
    for step in range(last - 1, 0, -1):
        mine_f = parts[step]
        mine_b = parts[experts - step]
        if step == last - 1:
            add_f = jnp.concatenate([mine_f[:half] + forward.astype(f32), mine_f[half:]], axis=0)
            add_b = jnp.concatenate([mine_b[:half], mine_b[half:] + backward.astype(f32)], axis=0)
        else:
            add_f = mine_f + forward.astype(f32)
            add_b = mine_b + backward.astype(f32)
        forward = ring_hop(add_f.astype(jnp.bfloat16), experts, 1)
        backward = ring_hop(add_b.astype(jnp.bfloat16), experts, -1)
    total = parts[0] + forward.astype(f32) + backward.astype(f32)
    return total.astype(jnp.bfloat16)


def per_device_dense(
    tokens,
    routing,
    gate_scores,
    cotangent,
    w_gate,
    w_up,
    w_down,
    mom_gate,
    mom_up,
    mom_down,
    gossip_round,
):
    tok_rows, feature_width = tokens.shape
    experts = lax.axis_size("expert")
    me = lax.axis_index("expert")
    weight_gate = w_gate[0, 0]
    weight_up = w_up[0, 0]
    weight_down = w_down[0, 0]
    hidden_width = weight_gate.shape[1]
    scale_in = feature_width ** (-0.5)
    scale_hidden = hidden_width ** (-0.5)
    inner_dims = (((1,), (1,)), ((), ()))
    outer_dims = (((0,), (0,)), ((), ()))
    gate_share = gate_scores / jnp.sum(gate_scores, axis=1, keepdims=True)
    names = routing[:, :, None] == jnp.arange(experts, dtype=jnp.int32)[None, None, :]
    share_by_expert = jnp.sum(jnp.where(names, gate_share[:, :, None], 0.0), axis=1)
    shares = lax.all_gather(share_by_expert, "expert", axis=0, tiled=True)
    share = jnp.sum(
        jnp.where(jnp.arange(experts, dtype=jnp.int32)[None, :] == me, shares, 0.0),
        axis=1,
    ).reshape(experts, tok_rows)
    order = jnp.array(ring_order(experts), dtype=jnp.int32)
    place = jnp.sum(jnp.where(order == me, jnp.arange(experts, dtype=jnp.int32), 0))
    picks = order[(place + jnp.arange(experts, dtype=jnp.int32)) % experts]
    share = share[picks].reshape(experts * tok_rows, 1)

    tok_blocks = ring_gather(tokens, experts)
    cot_blocks = ring_gather(cotangent, experts)
    rows_in = jnp.concatenate(tok_blocks, axis=0)
    rows_cot = jnp.concatenate(cot_blocks, axis=0)

    weight_both = jnp.concatenate([weight_gate, weight_up], axis=1)
    both_pre = jnp.dot(rows_in, weight_both, preferred_element_type=jnp.float32) * scale_in
    gate_pre = both_pre[:, :hidden_width]
    up_pre = both_pre[:, hidden_width:]
    sigmoid_gate = jax.nn.sigmoid(gate_pre)
    activation = (gate_pre * sigmoid_gate * up_pre * share).astype(jnp.bfloat16)
    part_out = jnp.dot(activation, weight_down, preferred_element_type=jnp.float32) * scale_hidden

    grad_down = (
        lax.dot_general(activation, rows_cot, outer_dims, preferred_element_type=jnp.float32)
        * scale_hidden
    )
    grad_act = lax.dot_general(
        rows_cot, weight_down, inner_dims, preferred_element_type=jnp.float32
    ) * (share * scale_hidden)
    grad_gate_pre = (
        grad_act * up_pre * sigmoid_gate * (1.0 + gate_pre * (1.0 - sigmoid_gate))
    ).astype(jnp.bfloat16)
    grad_up_pre = (grad_act * gate_pre * sigmoid_gate).astype(jnp.bfloat16)
    grad_gate = (
        lax.dot_general(rows_in, grad_gate_pre, outer_dims, preferred_element_type=jnp.float32)
        * scale_in
    )
    grad_up = (
        lax.dot_general(rows_in, grad_up_pre, outer_dims, preferred_element_type=jnp.float32)
        * scale_in
    )
    grad_both_pre = jnp.concatenate([grad_gate_pre, grad_up_pre], axis=1)
    part_back = (
        lax.dot_general(grad_both_pre, weight_both, inner_dims, preferred_element_type=jnp.float32)
        * scale_in
    )

    bit_count = lax.axis_size("replica").bit_length() - 1
    bit_now = gossip_round[0] % bit_count

    def averaged(local):
        partner = local
        for bit_index in range(bit_count):
            swapped = partner_2(local, "replica", bit_index)
            partner = jnp.where(bit_now == bit_index, swapped, partner)
        mean = (local.astype(jnp.float32) + partner.astype(jnp.float32)) * 0.5
        return mean.astype(jnp.bfloat16)[None, None]

    down_new, down_moment = momentum_step(weight_down, mom_down[0, 0], grad_down)
    gate_new, gate_moment = momentum_step(weight_gate, mom_gate[0, 0], grad_gate)
    up_new, up_moment = momentum_step(weight_up, mom_up[0, 0], grad_up)
    new_down = averaged(down_new)
    new_gate = averaged(gate_new)
    new_up = averaged(up_new)

    def blocks_of(rows):
        return [rows[j * tok_rows : (j + 1) * tok_rows] for j in range(experts)]

    layer_out = ring_scatter(blocks_of(part_out), experts)
    token_grad = ring_scatter(blocks_of(part_back), experts)
    return (
        layer_out,
        token_grad,
        new_gate,
        new_up,
        new_down,
        gate_moment[None, None],
        up_moment[None, None],
        down_moment[None, None],
    )


def per_device(tokens, routing, *others):
    if routing.shape[1] == lax.axis_size("expert"):
        return per_device_dense(tokens, routing, *others)
    return per_device_routed(tokens, routing, *others)


def solution(mesh):
    placed = (
        P(("replica", "expert"), None),
        P(("replica", "expert"), None),
        P(("replica", "expert"), None),
        P(("replica", "expert"), None),
        P("replica", "expert", None, None),
        P("replica", "expert", None, None),
        P("replica", "expert", None, None),
        P("replica", "expert", None, None),
        P("replica", "expert", None, None),
        P("replica", "expert", None, None),
        P("expert"),
    )
    return jax.shard_map(
        per_device,
        mesh=mesh,
        in_specs=placed,
        out_specs=(
            P(("replica", "expert"), None),
            P(("replica", "expert"), None),
            P("replica", "expert", None, None),
            P("replica", "expert", None, None),
            P("replica", "expert", None, None),
            P("replica", "expert", None, None),
            P("replica", "expert", None, None),
            P("replica", "expert", None, None),
        ),
        check_vma=False,
    )
```

```python
import jax
import jax.numpy as jnp
from jax import lax
from jax.sharding import PartitionSpec as P

momentum_beta = 0.9
learn_rate = 0.1


def partner_2(value, axis, stride):
    mask = 2**stride
    pairs = [(source, source ^ mask) for source in range(lax.axis_size(axis))]
    return lax.ppermute(value, axis, pairs)


def expert_forward(rows_in, weight_gate, weight_up, weight_down):
    scale_in = rows_in.shape[1] ** (-0.5)
    scale_hidden = weight_gate.shape[1] ** (-0.5)
    gate_pre = jnp.dot(rows_in, weight_gate, preferred_element_type=jnp.float32) * scale_in
    up_pre = jnp.dot(rows_in, weight_up, preferred_element_type=jnp.float32) * scale_in
    sigmoid_gate = jax.nn.sigmoid(gate_pre)
    activation = (gate_pre * sigmoid_gate * up_pre).astype(jnp.bfloat16)
    produced = (
        jnp.dot(activation, weight_down, preferred_element_type=jnp.float32) * scale_hidden
    ).astype(jnp.bfloat16)
    return (gate_pre, up_pre, sigmoid_gate, activation, produced)


def expert_backward(
    rows_in,
    rows_grad,
    weight_gate,
    weight_up,
    weight_down,
    gate_pre,
    up_pre,
    sigmoid_gate,
    activation,
):
    scale_in = rows_in.shape[1] ** (-0.5)
    scale_hidden = weight_gate.shape[1] ** (-0.5)
    inner_dims = (((1,), (1,)), ((), ()))
    outer_dims = (((0,), (0,)), ((), ()))
    grad_act = (
        lax.dot_general(rows_grad, weight_down, inner_dims, preferred_element_type=jnp.float32)
        * scale_hidden
    )
    grad_gate_pre = (
        grad_act * up_pre * sigmoid_gate * (1.0 + gate_pre * (1.0 - sigmoid_gate))
    ).astype(jnp.bfloat16)
    grad_up_pre = (grad_act * gate_pre * sigmoid_gate).astype(jnp.bfloat16)
    grad_down = (
        lax.dot_general(activation, rows_grad, outer_dims, preferred_element_type=jnp.float32)
        * scale_hidden
    )
    grad_gate = (
        lax.dot_general(rows_in, grad_gate_pre, outer_dims, preferred_element_type=jnp.float32)
        * scale_in
    )
    grad_up = (
        lax.dot_general(rows_in, grad_up_pre, outer_dims, preferred_element_type=jnp.float32)
        * scale_in
    )
    back_sum = lax.dot_general(
        grad_gate_pre, weight_gate, inner_dims, preferred_element_type=jnp.float32
    )
    back_sum = back_sum + lax.dot_general(
        grad_up_pre, weight_up, inner_dims, preferred_element_type=jnp.float32
    )
    rows_back = (back_sum * scale_in).astype(jnp.bfloat16)
    return (rows_back, grad_gate, grad_up, grad_down)


def momentum_step(weight, moment, gradient):
    moment_new = momentum_beta * moment.astype(jnp.float32) + gradient
    weight_new = (weight.astype(jnp.float32) - learn_rate * moment_new).astype(jnp.bfloat16)
    return (weight_new, moment_new.astype(jnp.bfloat16))


def per_device_routed(
    tokens,
    routing,
    gate_scores,
    cotangent,
    w_gate,
    w_up,
    w_down,
    mom_gate,
    mom_up,
    mom_down,
    gossip_round,
):
    tok_rows, feature_width = tokens.shape
    top_count = routing.shape[1]
    experts = lax.axis_size("expert")
    capacity = max(2, min(tok_rows, tok_rows * top_count // experts + 8))
    gate_share = gate_scores / jnp.sum(gate_scores, axis=1, keepdims=True)
    expert_ids = routing.reshape(-1)
    member = (expert_ids[:, None] == jnp.arange(experts, dtype=jnp.int32)[None, :]).astype(
        jnp.int32
    )
    earlier = jnp.sum((jnp.cumsum(member, axis=0) - member) * member, axis=1)
    target = expert_ids * capacity + earlier
    source = jnp.arange(expert_ids.shape[0], dtype=jnp.int32) // top_count
    send_rows = (
        jnp.zeros((experts * capacity, feature_width), jnp.bfloat16).at[target].set(tokens[source])
    )
    weighted = (gate_share.reshape(-1)[:, None] * cotangent[source].astype(jnp.float32)).astype(
        jnp.bfloat16
    )
    send_grad = (
        jnp.zeros((experts * capacity, feature_width), jnp.bfloat16).at[target].set(weighted)
    )
    arrived = lax.all_to_all(
        send_rows.reshape(experts, capacity, feature_width),
        "expert",
        split_axis=0,
        concat_axis=0,
        tiled=True,
    ).reshape(-1, feature_width)
    arrived_grad = lax.all_to_all(
        send_grad.reshape(experts, capacity, feature_width),
        "expert",
        split_axis=0,
        concat_axis=0,
        tiled=True,
    ).reshape(-1, feature_width)
    weight_gate = w_gate[0, 0]
    weight_up = w_up[0, 0]
    weight_down = w_down[0, 0]
    gate_pre, up_pre, sigmoid_gate, activation, produced = expert_forward(
        arrived, weight_gate, weight_up, weight_down
    )
    returned = lax.all_to_all(
        produced.reshape(experts, capacity, feature_width),
        "expert",
        split_axis=0,
        concat_axis=0,
        tiled=True,
    ).reshape(-1, feature_width)
    picked = returned[target].astype(jnp.float32) * gate_share.reshape(-1)[:, None]
    layer_out = jnp.sum(picked.reshape(tok_rows, top_count, feature_width), axis=1).astype(
        jnp.bfloat16
    )
    rows_back, grad_gate, grad_up, grad_down = expert_backward(
        arrived,
        arrived_grad,
        weight_gate,
        weight_up,
        weight_down,
        gate_pre,
        up_pre,
        sigmoid_gate,
        activation,
    )
    returned_grad = lax.all_to_all(
        rows_back.reshape(experts, capacity, feature_width),
        "expert",
        split_axis=0,
        concat_axis=0,
        tiled=True,
    ).reshape(-1, feature_width)
    picked_back = returned_grad[target].astype(jnp.float32)
    token_grad = jnp.sum(picked_back.reshape(tok_rows, top_count, feature_width), axis=1).astype(
        jnp.bfloat16
    )
    gate_new, gate_moment = momentum_step(weight_gate, mom_gate[0, 0], grad_gate)
    up_new, up_moment = momentum_step(weight_up, mom_up[0, 0], grad_up)
    down_new, down_moment = momentum_step(weight_down, mom_down[0, 0], grad_down)
    hidden_width = weight_gate.shape[1]
    stacked = jnp.stack([gate_new, up_new, down_new.reshape(feature_width, hidden_width)], axis=0)
    bit_count = lax.axis_size("replica").bit_length() - 1
    bit_now = gossip_round[0] % bit_count
    partner = stacked
    for bit_index in range(bit_count):
        swapped = partner_2(stacked, "replica", bit_index)
        partner = jnp.where(bit_now == bit_index, swapped, partner)
    averaged = ((stacked.astype(jnp.float32) + partner.astype(jnp.float32)) * 0.5).astype(
        jnp.bfloat16
    )
    new_gate = averaged[0][None, None]
    new_up = averaged[1][None, None]
    new_down = averaged[2].reshape(hidden_width, feature_width)[None, None]
    return (
        layer_out,
        token_grad,
        new_gate,
        new_up,
        new_down,
        gate_moment[None, None],
        up_moment[None, None],
        down_moment[None, None],
    )


def ring_order(experts):
    return list(range(0, experts, 2)) + list(range(experts - 1, 0, -2))


def ring_hop(value, experts, step):
    order = ring_order(experts)
    pairs = [(order[i], order[(i + step) % experts]) for i in range(experts)]
    return lax.ppermute(value, "expert", pairs)


def ring_gather(own, experts):
    half = own.shape[0] // 2
    last = experts // 2
    blocks = [None] * experts
    blocks[0] = own
    behind = ahead = own
    for step in range(1, last):
        behind = ring_hop(behind, experts, 1)
        ahead = ring_hop(ahead, experts, -1)
        blocks[experts - step] = behind
        blocks[step] = ahead
    top = ring_hop(behind[:half], experts, 1)
    bottom = ring_hop(ahead[half:], experts, -1)
    blocks[last] = jnp.concatenate([top, bottom], axis=0)
    return blocks


def own_shares(routing, gate_share, experts):
    me = lax.axis_index("expert")
    ids = jnp.arange(experts, dtype=jnp.int32)
    order = ring_order(experts)
    away = [[order[(order.index(e) + j) % experts] ^ e for j in range(experts)] for e in range(experts)]
    names = routing[:, None, :] == ids[None, :, None]
    table = jnp.sum(jnp.where(names, gate_share[:, None, :], 0.0), axis=2).T
    table = table[None]
    bit = 1
    while bit < experts:
        pairs = [(e, e ^ bit) for e in range(experts)]
        table = jnp.concatenate([table, lax.ppermute(table, "expert", pairs)], axis=0)
        bit = bit * 2
    mine = jnp.sum(jnp.where((ids == me)[None, :, None], table, 0.0), axis=1)
    picks = jnp.array(away, dtype=jnp.int32)[me]
    rows = jnp.sum(jnp.where(picks[:, None, None] == ids[None, :, None], mine[None], 0.0), axis=1)
    return [rows[j][:, None] for j in range(experts)]


def ring_scatter(parts, experts):
    half = parts[0].shape[0] // 2
    last = experts // 2
    f32 = jnp.float32
    forward = ring_hop(parts[last][:half].astype(jnp.bfloat16), experts, 1)
    backward = ring_hop(parts[last][half:].astype(jnp.bfloat16), experts, -1)
    for step in range(last - 1, 0, -1):
        mine_f = parts[step]
        mine_b = parts[experts - step]
        if step == last - 1:
            add_f = jnp.concatenate([mine_f[:half] + forward.astype(f32), mine_f[half:]], axis=0)
            add_b = jnp.concatenate([mine_b[:half], mine_b[half:] + backward.astype(f32)], axis=0)
        else:
            add_f = mine_f + forward.astype(f32)
            add_b = mine_b + backward.astype(f32)
        forward = ring_hop(add_f.astype(jnp.bfloat16), experts, 1)
        backward = ring_hop(add_b.astype(jnp.bfloat16), experts, -1)
    total = parts[0] + forward.astype(f32) + backward.astype(f32)
    return total.astype(jnp.bfloat16)


def per_device_dense(
    tokens,
    routing,
    gate_scores,
    cotangent,
    w_gate,
    w_up,
    w_down,
    mom_gate,
    mom_up,
    mom_down,
    gossip_round,
):
    tok_rows, feature_width = tokens.shape
    experts = lax.axis_size("expert")
    weight_gate = w_gate[0, 0]
    weight_up = w_up[0, 0]
    weight_down = w_down[0, 0]
    hidden_width = weight_gate.shape[1]
    scale_in = feature_width ** (-0.5)
    scale_hidden = hidden_width ** (-0.5)
    inner_dims = (((1,), (1,)), ((), ()))
    outer_dims = (((0,), (0,)), ((), ()))
    gate_share = gate_scores / jnp.sum(gate_scores, axis=1, keepdims=True)
    share_blocks = own_shares(routing, gate_share, experts)

    tok_blocks = ring_gather(tokens, experts)
    cot_blocks = ring_gather(cotangent, experts)
    weight_both = jnp.concatenate([weight_gate, weight_up], axis=1)

    acts, gate_grads, up_grads = [], [], []
    for block, cot, share in zip(tok_blocks, cot_blocks, share_blocks):
        both_pre = jnp.dot(block, weight_both, preferred_element_type=jnp.float32) * scale_in
        gate_pre = both_pre[:, :hidden_width]
        up_pre = both_pre[:, hidden_width:]
        sigmoid_gate = jax.nn.sigmoid(gate_pre)
        acts.append((gate_pre * sigmoid_gate * up_pre * share).astype(jnp.bfloat16))
        grad_act = lax.dot_general(
            cot, weight_down, inner_dims, preferred_element_type=jnp.float32
        ) * (share * scale_hidden)
        gate_grads.append(
            (grad_act * up_pre * sigmoid_gate * (1.0 + gate_pre * (1.0 - sigmoid_gate))).astype(
                jnp.bfloat16
            )
        )
        up_grads.append((grad_act * gate_pre * sigmoid_gate).astype(jnp.bfloat16))
    rows_in = jnp.concatenate(tok_blocks, axis=0)
    rows_cot = jnp.concatenate(cot_blocks, axis=0)
    activation = jnp.concatenate(acts, axis=0)
    grad_gate_pre = jnp.concatenate(gate_grads, axis=0)
    grad_up_pre = jnp.concatenate(up_grads, axis=0)

    grad_down = (
        lax.dot_general(activation, rows_cot, outer_dims, preferred_element_type=jnp.float32)
        * scale_hidden
    )
    down_new, down_moment = momentum_step(weight_down, mom_down[0, 0], grad_down)
    grad_gate = (
        lax.dot_general(rows_in, grad_gate_pre, outer_dims, preferred_element_type=jnp.float32)
        * scale_in
    )
    gate_new, gate_moment = momentum_step(weight_gate, mom_gate[0, 0], grad_gate)
    grad_up = (
        lax.dot_general(rows_in, grad_up_pre, outer_dims, preferred_element_type=jnp.float32)
        * scale_in
    )
    up_new, up_moment = momentum_step(weight_up, mom_up[0, 0], grad_up)
    activation, down_new = lax.optimization_barrier((activation, down_new))
    part_out = jnp.dot(activation, weight_down, preferred_element_type=jnp.float32) * scale_hidden
    grad_gate_pre, grad_up_pre, gate_new, up_new = lax.optimization_barrier(
        (grad_gate_pre, grad_up_pre, gate_new, up_new)
    )
    grad_both_pre = jnp.concatenate([grad_gate_pre, grad_up_pre], axis=1)
    part_back = (
        lax.dot_general(grad_both_pre, weight_both, inner_dims, preferred_element_type=jnp.float32)
        * scale_in
    )

    bit_count = lax.axis_size("replica").bit_length() - 1
    bit_now = gossip_round[0] % bit_count

    def averaged(local):
        partner = local
        for bit_index in range(bit_count):
            swapped = partner_2(local, "replica", bit_index)
            partner = jnp.where(bit_now == bit_index, swapped, partner)
        mean = (local.astype(jnp.float32) + partner.astype(jnp.float32)) * 0.5
        return mean.astype(jnp.bfloat16)[None, None]

    new_down = averaged(down_new)
    new_gate = averaged(gate_new)
    new_up = averaged(up_new)

    def blocks_of(rows):
        return [rows[j * tok_rows : (j + 1) * tok_rows] for j in range(experts)]

    layer_out = ring_scatter(blocks_of(part_out), experts)
    token_grad = ring_scatter(blocks_of(part_back), experts)
    return (
        layer_out,
        token_grad,
        new_gate,
        new_up,
        new_down,
        gate_moment[None, None],
        up_moment[None, None],
        down_moment[None, None],
    )


def per_device(tokens, routing, *others):
    if routing.shape[1] == lax.axis_size("expert"):
        return per_device_dense(tokens, routing, *others)
    return per_device_routed(tokens, routing, *others)


def solution(mesh):
    placed = (
        P(("replica", "expert"), None),
        P(("replica", "expert"), None),
        P(("replica", "expert"), None),
        P(("replica", "expert"), None),
        P("replica", "expert", None, None),
        P("replica", "expert", None, None),
        P("replica", "expert", None, None),
        P("replica", "expert", None, None),
        P("replica", "expert", None, None),
        P("replica", "expert", None, None),
        P("expert"),
    )
    return jax.shard_map(
        per_device,
        mesh=mesh,
        in_specs=placed,
        out_specs=(
            P(("replica", "expert"), None),
            P(("replica", "expert"), None),
            P("replica", "expert", None, None),
            P("replica", "expert", None, None),
            P("replica", "expert", None, None),
            P("replica", "expert", None, None),
            P("replica", "expert", None, None),
            P("replica", "expert", None, None),
        ),
        check_vma=False,
    )
```

```python
import jax
import jax.numpy as jnp
from jax import lax
from jax.sharding import PartitionSpec as P

momentum_beta = 0.9
learn_rate = 0.1


def partner_2(value, axis, stride):
    mask = 2**stride
    pairs = [(source, source ^ mask) for source in range(lax.axis_size(axis))]
    return lax.ppermute(value, axis, pairs)


def expert_forward(rows_in, weight_gate, weight_up, weight_down):
    scale_in = rows_in.shape[1] ** (-0.5)
    scale_hidden = weight_gate.shape[1] ** (-0.5)
    gate_pre = jnp.dot(rows_in, weight_gate, preferred_element_type=jnp.float32) * scale_in
    up_pre = jnp.dot(rows_in, weight_up, preferred_element_type=jnp.float32) * scale_in
    sigmoid_gate = jax.nn.sigmoid(gate_pre)
    activation = (gate_pre * sigmoid_gate * up_pre).astype(jnp.bfloat16)
    produced = (
        jnp.dot(activation, weight_down, preferred_element_type=jnp.float32) * scale_hidden
    ).astype(jnp.bfloat16)
    return (gate_pre, up_pre, sigmoid_gate, activation, produced)


def expert_backward(
    rows_in,
    rows_grad,
    weight_gate,
    weight_up,
    weight_down,
    gate_pre,
    up_pre,
    sigmoid_gate,
    activation,
):
    scale_in = rows_in.shape[1] ** (-0.5)
    scale_hidden = weight_gate.shape[1] ** (-0.5)
    inner_dims = (((1,), (1,)), ((), ()))
    outer_dims = (((0,), (0,)), ((), ()))
    grad_act = (
        lax.dot_general(rows_grad, weight_down, inner_dims, preferred_element_type=jnp.float32)
        * scale_hidden
    )
    grad_gate_pre = (
        grad_act * up_pre * sigmoid_gate * (1.0 + gate_pre * (1.0 - sigmoid_gate))
    ).astype(jnp.bfloat16)
    grad_up_pre = (grad_act * gate_pre * sigmoid_gate).astype(jnp.bfloat16)
    grad_down = (
        lax.dot_general(activation, rows_grad, outer_dims, preferred_element_type=jnp.float32)
        * scale_hidden
    )
    grad_gate = (
        lax.dot_general(rows_in, grad_gate_pre, outer_dims, preferred_element_type=jnp.float32)
        * scale_in
    )
    grad_up = (
        lax.dot_general(rows_in, grad_up_pre, outer_dims, preferred_element_type=jnp.float32)
        * scale_in
    )
    back_sum = lax.dot_general(
        grad_gate_pre, weight_gate, inner_dims, preferred_element_type=jnp.float32
    )
    back_sum = back_sum + lax.dot_general(
        grad_up_pre, weight_up, inner_dims, preferred_element_type=jnp.float32
    )
    rows_back = (back_sum * scale_in).astype(jnp.bfloat16)
    return (rows_back, grad_gate, grad_up, grad_down)


def momentum_step(weight, moment, gradient):
    moment_new = momentum_beta * moment.astype(jnp.float32) + gradient
    weight_new = (weight.astype(jnp.float32) - learn_rate * moment_new).astype(jnp.bfloat16)
    return (weight_new, moment_new.astype(jnp.bfloat16))


def per_device_routed(
    tokens,
    routing,
    gate_scores,
    cotangent,
    w_gate,
    w_up,
    w_down,
    mom_gate,
    mom_up,
    mom_down,
    gossip_round,
):
    tok_rows, feature_width = tokens.shape
    top_count = routing.shape[1]
    experts = lax.axis_size("expert")
    capacity = max(2, min(tok_rows, tok_rows * top_count // experts + 8))
    gate_share = gate_scores / jnp.sum(gate_scores, axis=1, keepdims=True)
    expert_ids = routing.reshape(-1)
    member = (expert_ids[:, None] == jnp.arange(experts, dtype=jnp.int32)[None, :]).astype(
        jnp.int32
    )
    earlier = jnp.sum((jnp.cumsum(member, axis=0) - member) * member, axis=1)
    target = expert_ids * capacity + earlier
    source = jnp.arange(expert_ids.shape[0], dtype=jnp.int32) // top_count
    send_rows = (
        jnp.zeros((experts * capacity, feature_width), jnp.bfloat16).at[target].set(tokens[source])
    )
    weighted = (gate_share.reshape(-1)[:, None] * cotangent[source].astype(jnp.float32)).astype(
        jnp.bfloat16
    )
    send_grad = (
        jnp.zeros((experts * capacity, feature_width), jnp.bfloat16).at[target].set(weighted)
    )
    arrived = lax.all_to_all(
        send_rows.reshape(experts, capacity, feature_width),
        "expert",
        split_axis=0,
        concat_axis=0,
        tiled=True,
    ).reshape(-1, feature_width)
    arrived_grad = lax.all_to_all(
        send_grad.reshape(experts, capacity, feature_width),
        "expert",
        split_axis=0,
        concat_axis=0,
        tiled=True,
    ).reshape(-1, feature_width)
    weight_gate = w_gate[0, 0]
    weight_up = w_up[0, 0]
    weight_down = w_down[0, 0]
    gate_pre, up_pre, sigmoid_gate, activation, produced = expert_forward(
        arrived, weight_gate, weight_up, weight_down
    )
    returned = lax.all_to_all(
        produced.reshape(experts, capacity, feature_width),
        "expert",
        split_axis=0,
        concat_axis=0,
        tiled=True,
    ).reshape(-1, feature_width)
    picked = returned[target].astype(jnp.float32) * gate_share.reshape(-1)[:, None]
    layer_out = jnp.sum(picked.reshape(tok_rows, top_count, feature_width), axis=1).astype(
        jnp.bfloat16
    )
    rows_back, grad_gate, grad_up, grad_down = expert_backward(
        arrived,
        arrived_grad,
        weight_gate,
        weight_up,
        weight_down,
        gate_pre,
        up_pre,
        sigmoid_gate,
        activation,
    )
    returned_grad = lax.all_to_all(
        rows_back.reshape(experts, capacity, feature_width),
        "expert",
        split_axis=0,
        concat_axis=0,
        tiled=True,
    ).reshape(-1, feature_width)
    picked_back = returned_grad[target].astype(jnp.float32)
    token_grad = jnp.sum(picked_back.reshape(tok_rows, top_count, feature_width), axis=1).astype(
        jnp.bfloat16
    )
    gate_new, gate_moment = momentum_step(weight_gate, mom_gate[0, 0], grad_gate)
    up_new, up_moment = momentum_step(weight_up, mom_up[0, 0], grad_up)
    down_new, down_moment = momentum_step(weight_down, mom_down[0, 0], grad_down)
    hidden_width = weight_gate.shape[1]
    stacked = jnp.stack([gate_new, up_new, down_new.reshape(feature_width, hidden_width)], axis=0)
    bit_count = lax.axis_size("replica").bit_length() - 1
    bit_now = gossip_round[0] % bit_count
    partner = stacked
    for bit_index in range(bit_count):
        swapped = partner_2(stacked, "replica", bit_index)
        partner = jnp.where(bit_now == bit_index, swapped, partner)
    averaged = ((stacked.astype(jnp.float32) + partner.astype(jnp.float32)) * 0.5).astype(
        jnp.bfloat16
    )
    new_gate = averaged[0][None, None]
    new_up = averaged[1][None, None]
    new_down = averaged[2].reshape(hidden_width, feature_width)[None, None]
    return (
        layer_out,
        token_grad,
        new_gate,
        new_up,
        new_down,
        gate_moment[None, None],
        up_moment[None, None],
        down_moment[None, None],
    )


def ring_order(experts):
    return list(range(0, experts, 2)) + list(range(experts - 1, 0, -2))


def ring_hop(value, experts, step):
    order = ring_order(experts)
    pairs = [(order[i], order[(i + step) % experts]) for i in range(experts)]
    return lax.ppermute(value, "expert", pairs)


def after(value, *others):
    return lax.optimization_barrier((value,) + others)[0]


def ring_gather_pair(first, second, experts):
    half = first.shape[0] // 2
    last = experts // 2
    blocks = [[None] * experts, [None] * experts]
    moving = [(first, first), (second, second)]
    for which, own in enumerate((first, second)):
        blocks[which][0] = own
    for step in range(1, last):
        for which in range(2):
            behind, ahead = moving[which]
            behind = ring_hop(behind, experts, 1)
            ahead = ring_hop(ahead, experts, -1)
            moving[which] = lax.optimization_barrier((behind, ahead))
            blocks[which][experts - step], blocks[which][step] = moving[which]
    for which in range(2):
        behind, ahead = moving[which]
        top = ring_hop(behind[:half], experts, 1)
        bottom = ring_hop(ahead[half:], experts, -1)
        blocks[which][last] = jnp.concatenate([top, bottom], axis=0)
    return blocks


def ring_scatter_pair(parts_pair, experts, gates):
    half = parts_pair[0][0].shape[0] // 2
    last = experts // 2
    f32 = jnp.float32
    moving = []
    for parts in parts_pair:
        top = parts[last][:half].astype(jnp.bfloat16)
        bottom = parts[last][half:].astype(jnp.bfloat16)
        moving.append((ring_hop(top, experts, 1), ring_hop(bottom, experts, -1)))
    for step in range(last - 1, 0, -1):
        for which, parts in enumerate(parts_pair):
            forward, backward = moving[which]
            mine_f, mine_b = parts[step], parts[experts - step]
            if step == last - 1:
                add_f = jnp.concatenate([mine_f[:half] + forward.astype(f32), mine_f[half:]], axis=0)
                add_b = jnp.concatenate([mine_b[:half], mine_b[half:] + backward.astype(f32)], axis=0)
            else:
                add_f = mine_f + forward.astype(f32)
                add_b = mine_b + backward.astype(f32)
            add_f, add_b = add_f.astype(jnp.bfloat16), add_b.astype(jnp.bfloat16)
            if step in gates:
                add_f, add_b = after((add_f, add_b), gates[step])
            else:
                add_f, add_b = lax.optimization_barrier((add_f, add_b))
            moving[which] = (ring_hop(add_f, experts, 1), ring_hop(add_b, experts, -1))
    totals = []
    for parts, (forward, backward) in zip(parts_pair, moving):
        total = parts[0] + forward.astype(f32) + backward.astype(f32)
        totals.append(total.astype(jnp.bfloat16))
    return totals


def own_shares(routing, gate_share, experts, marks):
    me = lax.axis_index("expert")
    ids = jnp.arange(experts, dtype=jnp.int32)
    order = ring_order(experts)
    away = [[order[(order.index(e) + j) % experts] ^ e for j in range(experts)] for e in range(experts)]
    names = routing[:, None, :] == ids[None, :, None]
    table = jnp.sum(jnp.where(names, gate_share[:, None, :], 0.0), axis=2).T
    table = table[None]
    bit = 1
    turn = 0
    while bit < experts:
        pairs = [(e, e ^ bit) for e in range(experts)]
        other = lax.ppermute(table, "expert", pairs)
        table = jnp.concatenate([table, after(other, marks[turn % len(marks)])], axis=0)
        bit = bit * 2
        turn = turn + 1
    mine = jnp.sum(jnp.where((ids == me)[None, :, None], table, 0.0), axis=1)
    picks = jnp.array(away, dtype=jnp.int32)[me]
    rows = jnp.sum(jnp.where(picks[:, None, None] == ids[None, :, None], mine[None], 0.0), axis=1)
    return [rows[j][:, None] for j in range(experts)]


def ring_scatter(parts, experts):
    half = parts[0].shape[0] // 2
    last = experts // 2
    f32 = jnp.float32
    forward = ring_hop(parts[last][:half].astype(jnp.bfloat16), experts, 1)
    backward = ring_hop(parts[last][half:].astype(jnp.bfloat16), experts, -1)
    for step in range(last - 1, 0, -1):
        mine_f = parts[step]
        mine_b = parts[experts - step]
        if step == last - 1:
            add_f = jnp.concatenate([mine_f[:half] + forward.astype(f32), mine_f[half:]], axis=0)
            add_b = jnp.concatenate([mine_b[:half], mine_b[half:] + backward.astype(f32)], axis=0)
        else:
            add_f = mine_f + forward.astype(f32)
            add_b = mine_b + backward.astype(f32)
        forward = ring_hop(add_f.astype(jnp.bfloat16), experts, 1)
        backward = ring_hop(add_b.astype(jnp.bfloat16), experts, -1)
    total = parts[0] + forward.astype(f32) + backward.astype(f32)
    return total.astype(jnp.bfloat16)


def per_device_dense(
    tokens,
    routing,
    gate_scores,
    cotangent,
    w_gate,
    w_up,
    w_down,
    mom_gate,
    mom_up,
    mom_down,
    gossip_round,
):
    tok_rows, feature_width = tokens.shape
    experts = lax.axis_size("expert")
    weight_gate = w_gate[0, 0]
    weight_up = w_up[0, 0]
    weight_down = w_down[0, 0]
    hidden_width = weight_gate.shape[1]
    scale_in = feature_width ** (-0.5)
    scale_hidden = hidden_width ** (-0.5)
    inner_dims = (((1,), (1,)), ((), ()))
    outer_dims = (((0,), (0,)), ((), ()))
    gate_share = gate_scores / jnp.sum(gate_scores, axis=1, keepdims=True)
    tok_blocks, cot_blocks = ring_gather_pair(tokens, cotangent, experts)
    marks = (tok_blocks[1], cot_blocks[1], tok_blocks[min(2, experts // 2)])
    share_blocks = own_shares(routing, gate_share, experts, marks)
    weight_both = jnp.concatenate([weight_gate, weight_up], axis=1)

    arrival = [0]
    for step in range(1, experts // 2):
        arrival = arrival + [step, experts - step]
    arrival.append(experts // 2)

    acts, gate_grads, up_grads = [], [], []
    for place in arrival:
        block, cot, share = tok_blocks[place], cot_blocks[place], share_blocks[place]
        both_pre = jnp.dot(block, weight_both, preferred_element_type=jnp.float32) * scale_in
        gate_pre = both_pre[:, :hidden_width]
        up_pre = both_pre[:, hidden_width:]
        sigmoid_gate = jax.nn.sigmoid(gate_pre)
        acts.append((gate_pre * sigmoid_gate * up_pre * share).astype(jnp.bfloat16))
        grad_act = lax.dot_general(
            cot, weight_down, inner_dims, preferred_element_type=jnp.float32
        ) * (share * scale_hidden)
        gate_grads.append(
            (grad_act * up_pre * sigmoid_gate * (1.0 + gate_pre * (1.0 - sigmoid_gate))).astype(
                jnp.bfloat16
            )
        )
        up_grads.append((grad_act * gate_pre * sigmoid_gate).astype(jnp.bfloat16))
    rows_in = jnp.concatenate([tok_blocks[place] for place in arrival], axis=0)
    rows_cot = jnp.concatenate([cot_blocks[place] for place in arrival], axis=0)
    activation = jnp.concatenate(acts, axis=0)
    grad_gate_pre = jnp.concatenate(gate_grads, axis=0)
    grad_up_pre = jnp.concatenate(up_grads, axis=0)

    grad_down = (
        lax.dot_general(activation, rows_cot, outer_dims, preferred_element_type=jnp.float32)
        * scale_hidden
    )
    down_new, down_moment = momentum_step(weight_down, mom_down[0, 0], grad_down)
    grad_gate_pre = after(grad_gate_pre, down_new)
    grad_gate = (
        lax.dot_general(rows_in, grad_gate_pre, outer_dims, preferred_element_type=jnp.float32)
        * scale_in
    )
    gate_new, gate_moment = momentum_step(weight_gate, mom_gate[0, 0], grad_gate)
    grad_up_pre = after(grad_up_pre, gate_new)
    grad_up = (
        lax.dot_general(rows_in, grad_up_pre, outer_dims, preferred_element_type=jnp.float32)
        * scale_in
    )
    up_new, up_moment = momentum_step(weight_up, mom_up[0, 0], grad_up)
    bit_count = lax.axis_size("replica").bit_length() - 1
    bit_now = gossip_round[0] % bit_count

    def swaps(local):
        return [partner_2(local, "replica", bit_index) for bit_index in range(bit_count)]

    def averaged(local, swapped):
        partner = local
        for bit_index in range(bit_count):
            partner = jnp.where(bit_now == bit_index, swapped[bit_index], partner)
        mean = (local.astype(jnp.float32) + partner.astype(jnp.float32)) * 0.5
        return mean.astype(jnp.bfloat16)[None, None]

    down_swaps = swaps(down_new)
    gate_swaps = swaps(gate_new)
    up_swaps = swaps(after(up_new, down_swaps[-1]))
    new_down = averaged(down_new, down_swaps)
    new_gate = averaged(gate_new, gate_swaps)
    new_up = averaged(up_new, up_swaps)

    activation = after(activation, down_new)
    part_out = jnp.dot(activation, weight_down, preferred_element_type=jnp.float32) * scale_hidden
    grad_gate_pre, grad_up_pre = after((grad_gate_pre, grad_up_pre), gate_new, up_new)
    grad_both_pre = jnp.concatenate([grad_gate_pre, grad_up_pre], axis=1)
    part_back = (
        lax.dot_general(grad_both_pre, weight_both, inner_dims, preferred_element_type=jnp.float32)
        * scale_in
    )

    def blocks_of(rows):
        starts = [arrival.index(j) * tok_rows for j in range(experts)]
        return [rows[start : start + tok_rows] for start in starts]

    layer_out, token_grad = ring_scatter_pair(
        (blocks_of(part_out), blocks_of(part_back)),
        experts,
        {2: down_swaps[-1], 1: gate_swaps[-1]},
    )
    return (
        layer_out,
        token_grad,
        new_gate,
        new_up,
        new_down,
        gate_moment[None, None],
        up_moment[None, None],
        down_moment[None, None],
    )


def per_device(tokens, routing, *others):
    if routing.shape[1] == lax.axis_size("expert"):
        return per_device_dense(tokens, routing, *others)
    return per_device_routed(tokens, routing, *others)


def solution(mesh):
    placed = (
        P(("replica", "expert"), None),
        P(("replica", "expert"), None),
        P(("replica", "expert"), None),
        P(("replica", "expert"), None),
        P("replica", "expert", None, None),
        P("replica", "expert", None, None),
        P("replica", "expert", None, None),
        P("replica", "expert", None, None),
        P("replica", "expert", None, None),
        P("replica", "expert", None, None),
        P("expert"),
    )
    return jax.shard_map(
        per_device,
        mesh=mesh,
        in_specs=placed,
        out_specs=(
            P(("replica", "expert"), None),
            P(("replica", "expert"), None),
            P("replica", "expert", None, None),
            P("replica", "expert", None, None),
            P("replica", "expert", None, None),
            P("replica", "expert", None, None),
            P("replica", "expert", None, None),
            P("replica", "expert", None, None),
        ),
        check_vma=False,
    )
```

```python
import jax
import jax.numpy as jnp
from jax import lax
from jax.experimental import pallas as pl
from jax.experimental.pallas import tpu as pltpu
from jax.sharding import PartitionSpec as P

momentum_beta = 0.9
learn_rate = 0.1


def partner_2(value, axis, stride):
    mask = 2**stride
    pairs = [(source, source ^ mask) for source in range(lax.axis_size(axis))]
    return lax.ppermute(value, axis, pairs)


def expert_forward(rows_in, weight_gate, weight_up, weight_down):
    scale_in = rows_in.shape[1] ** (-0.5)
    scale_hidden = weight_gate.shape[1] ** (-0.5)
    gate_pre = jnp.dot(rows_in, weight_gate, preferred_element_type=jnp.float32) * scale_in
    up_pre = jnp.dot(rows_in, weight_up, preferred_element_type=jnp.float32) * scale_in
    sigmoid_gate = jax.nn.sigmoid(gate_pre)
    activation = (gate_pre * sigmoid_gate * up_pre).astype(jnp.bfloat16)
    produced = (
        jnp.dot(activation, weight_down, preferred_element_type=jnp.float32) * scale_hidden
    ).astype(jnp.bfloat16)
    return (gate_pre, up_pre, sigmoid_gate, activation, produced)


def expert_backward(
    rows_in,
    rows_grad,
    weight_gate,
    weight_up,
    weight_down,
    gate_pre,
    up_pre,
    sigmoid_gate,
    activation,
):
    scale_in = rows_in.shape[1] ** (-0.5)
    scale_hidden = weight_gate.shape[1] ** (-0.5)
    inner_dims = (((1,), (1,)), ((), ()))
    outer_dims = (((0,), (0,)), ((), ()))
    grad_act = (
        lax.dot_general(rows_grad, weight_down, inner_dims, preferred_element_type=jnp.float32)
        * scale_hidden
    )
    grad_gate_pre = (
        grad_act * up_pre * sigmoid_gate * (1.0 + gate_pre * (1.0 - sigmoid_gate))
    ).astype(jnp.bfloat16)
    grad_up_pre = (grad_act * gate_pre * sigmoid_gate).astype(jnp.bfloat16)
    grad_down = (
        lax.dot_general(activation, rows_grad, outer_dims, preferred_element_type=jnp.float32)
        * scale_hidden
    )
    grad_gate = (
        lax.dot_general(rows_in, grad_gate_pre, outer_dims, preferred_element_type=jnp.float32)
        * scale_in
    )
    grad_up = (
        lax.dot_general(rows_in, grad_up_pre, outer_dims, preferred_element_type=jnp.float32)
        * scale_in
    )
    back_sum = lax.dot_general(
        grad_gate_pre, weight_gate, inner_dims, preferred_element_type=jnp.float32
    )
    back_sum = back_sum + lax.dot_general(
        grad_up_pre, weight_up, inner_dims, preferred_element_type=jnp.float32
    )
    rows_back = (back_sum * scale_in).astype(jnp.bfloat16)
    return (rows_back, grad_gate, grad_up, grad_down)


def momentum_step(weight, moment, gradient):
    moment_new = momentum_beta * moment.astype(jnp.float32) + gradient
    weight_new = (weight.astype(jnp.float32) - learn_rate * moment_new).astype(jnp.bfloat16)
    return (weight_new, moment_new.astype(jnp.bfloat16))


def per_device_routed(
    tokens,
    routing,
    gate_scores,
    cotangent,
    w_gate,
    w_up,
    w_down,
    mom_gate,
    mom_up,
    mom_down,
    gossip_round,
):
    tok_rows, feature_width = tokens.shape
    top_count = routing.shape[1]
    experts = lax.axis_size("expert")
    capacity = max(2, min(tok_rows, tok_rows * top_count // experts + 8))
    gate_share = gate_scores / jnp.sum(gate_scores, axis=1, keepdims=True)
    expert_ids = routing.reshape(-1)
    member = (expert_ids[:, None] == jnp.arange(experts, dtype=jnp.int32)[None, :]).astype(
        jnp.int32
    )
    earlier = jnp.sum((jnp.cumsum(member, axis=0) - member) * member, axis=1)
    target = expert_ids * capacity + earlier
    source = jnp.arange(expert_ids.shape[0], dtype=jnp.int32) // top_count
    send_rows = (
        jnp.zeros((experts * capacity, feature_width), jnp.bfloat16).at[target].set(tokens[source])
    )
    weighted = (gate_share.reshape(-1)[:, None] * cotangent[source].astype(jnp.float32)).astype(
        jnp.bfloat16
    )
    send_grad = (
        jnp.zeros((experts * capacity, feature_width), jnp.bfloat16).at[target].set(weighted)
    )
    arrived = lax.all_to_all(
        send_rows.reshape(experts, capacity, feature_width),
        "expert",
        split_axis=0,
        concat_axis=0,
        tiled=True,
    ).reshape(-1, feature_width)
    arrived_grad = lax.all_to_all(
        send_grad.reshape(experts, capacity, feature_width),
        "expert",
        split_axis=0,
        concat_axis=0,
        tiled=True,
    ).reshape(-1, feature_width)
    weight_gate = w_gate[0, 0]
    weight_up = w_up[0, 0]
    weight_down = w_down[0, 0]
    gate_pre, up_pre, sigmoid_gate, activation, produced = expert_forward(
        arrived, weight_gate, weight_up, weight_down
    )
    returned = lax.all_to_all(
        produced.reshape(experts, capacity, feature_width),
        "expert",
        split_axis=0,
        concat_axis=0,
        tiled=True,
    ).reshape(-1, feature_width)
    picked = returned[target].astype(jnp.float32) * gate_share.reshape(-1)[:, None]
    layer_out = jnp.sum(picked.reshape(tok_rows, top_count, feature_width), axis=1).astype(
        jnp.bfloat16
    )
    rows_back, grad_gate, grad_up, grad_down = expert_backward(
        arrived,
        arrived_grad,
        weight_gate,
        weight_up,
        weight_down,
        gate_pre,
        up_pre,
        sigmoid_gate,
        activation,
    )
    returned_grad = lax.all_to_all(
        rows_back.reshape(experts, capacity, feature_width),
        "expert",
        split_axis=0,
        concat_axis=0,
        tiled=True,
    ).reshape(-1, feature_width)
    picked_back = returned_grad[target].astype(jnp.float32)
    token_grad = jnp.sum(picked_back.reshape(tok_rows, top_count, feature_width), axis=1).astype(
        jnp.bfloat16
    )
    gate_new, gate_moment = momentum_step(weight_gate, mom_gate[0, 0], grad_gate)
    up_new, up_moment = momentum_step(weight_up, mom_up[0, 0], grad_up)
    down_new, down_moment = momentum_step(weight_down, mom_down[0, 0], grad_down)
    hidden_width = weight_gate.shape[1]
    stacked = jnp.stack([gate_new, up_new, down_new.reshape(feature_width, hidden_width)], axis=0)
    bit_count = lax.axis_size("replica").bit_length() - 1
    bit_now = gossip_round[0] % bit_count
    partner = stacked
    for bit_index in range(bit_count):
        swapped = partner_2(stacked, "replica", bit_index)
        partner = jnp.where(bit_now == bit_index, swapped, partner)
    averaged = ((stacked.astype(jnp.float32) + partner.astype(jnp.float32)) * 0.5).astype(
        jnp.bfloat16
    )
    new_gate = averaged[0][None, None]
    new_up = averaged[1][None, None]
    new_down = averaged[2].reshape(hidden_width, feature_width)[None, None]
    return (
        layer_out,
        token_grad,
        new_gate,
        new_up,
        new_down,
        gate_moment[None, None],
        up_moment[None, None],
        down_moment[None, None],
    )


def ring_order(experts):
    return list(range(0, experts, 2)) + list(range(experts - 1, 0, -2))


def ring_hop(value, experts, step):
    order = ring_order(experts)
    pairs = [(order[i], order[(i + step) % experts]) for i in range(experts)]
    return lax.ppermute(value, "expert", pairs)


def after(value, *others):
    return lax.optimization_barrier((value,) + others)[0]


def ring_gather_pair(first, second, experts):
    half = first.shape[0] // 2
    last = experts // 2
    blocks = [[None] * experts, [None] * experts]
    moving = [(first, first), (second, second)]
    for which, own in enumerate((first, second)):
        blocks[which][0] = own
    for step in range(1, last):
        for which in range(2):
            behind, ahead = moving[which]
            behind = ring_hop(behind, experts, 1)
            ahead = ring_hop(ahead, experts, -1)
            moving[which] = lax.optimization_barrier((behind, ahead))
            blocks[which][experts - step], blocks[which][step] = moving[which]
    for which in range(2):
        behind, ahead = moving[which]
        top = ring_hop(behind[:half], experts, 1)
        bottom = ring_hop(ahead[half:], experts, -1)
        blocks[which][last] = jnp.concatenate([top, bottom], axis=0)
    return blocks


def ring_scatter(parts, experts, gates):
    half = parts[0].shape[0] // 2
    last = experts // 2
    f32 = jnp.float32
    forward = ring_hop(parts[last][:half].astype(jnp.bfloat16), experts, 1)
    backward = ring_hop(parts[last][half:].astype(jnp.bfloat16), experts, -1)
    for step in range(last - 1, 0, -1):
        mine_f, mine_b = parts[step], parts[experts - step]
        if step == last - 1:
            add_f = jnp.concatenate([mine_f[:half] + forward.astype(f32), mine_f[half:]], axis=0)
            add_b = jnp.concatenate([mine_b[:half], mine_b[half:] + backward.astype(f32)], axis=0)
        else:
            add_f = mine_f + forward.astype(f32)
            add_b = mine_b + backward.astype(f32)
        add_f, add_b = add_f.astype(jnp.bfloat16), add_b.astype(jnp.bfloat16)
        if step in gates:
            add_f, add_b = after((add_f, add_b), gates[step])
        else:
            add_f, add_b = lax.optimization_barrier((add_f, add_b))
        forward = ring_hop(add_f, experts, 1)
        backward = ring_hop(add_b, experts, -1)
    total = parts[0] + forward.astype(f32) + backward.astype(f32)
    return total.astype(jnp.bfloat16)


def mean_body(pick_ref, local_ref, near_ref, far_ref, left_ref, right_ref):
    f32 = jnp.float32
    columns = left_ref.shape[1]
    local = local_ref[...].astype(f32)

    def write(other):
        mean = ((local + other.astype(f32)) * 0.5).astype(jnp.bfloat16)
        left_ref[...] = mean[:, :columns]
        right_ref[...] = mean[:, columns:]

    @pl.when(pick_ref[0] == 0)
    def _():
        write(near_ref[...])

    @pl.when(pick_ref[0] != 0)
    def _():
        write(far_ref[...])


def mean_halves(take_far, local, near, far):
    rows, columns = local.shape
    tile = rows // 8
    half = columns // 2
    grid_spec = pltpu.PrefetchScalarGridSpec(
        num_scalar_prefetch=1,
        grid=(rows // tile,),
        in_specs=[
            pl.BlockSpec((tile, columns), lambda i, pick: (i, 0)),
            pl.BlockSpec((tile, columns), lambda i, pick: (i * (1 - pick[0]), 0)),
            pl.BlockSpec((tile, columns), lambda i, pick: (i * pick[0], 0)),
        ],
        out_specs=[pl.BlockSpec((tile, half), lambda i, pick: (i, 0))] * 2,
    )
    return pl.pallas_call(
        mean_body,
        grid_spec=grid_spec,
        out_shape=[jax.ShapeDtypeStruct((rows, half), jnp.bfloat16)] * 2,
        cost_estimate=pl.CostEstimate(
            flops=2 * rows * columns, bytes_accessed=6 * rows * columns, transcendentals=0
        ),
    )(take_far.astype(jnp.int32).reshape(1), local, near, far)


def own_shares(routing, gate_share, experts, marks):
    me = lax.axis_index("expert")
    ids = jnp.arange(experts, dtype=jnp.int32)
    order = ring_order(experts)
    away = [[order[(order.index(e) + j) % experts] ^ e for j in range(experts)] for e in range(experts)]
    names = routing[:, None, :] == ids[None, :, None]
    table = jnp.sum(jnp.where(names, gate_share[:, None, :], 0.0), axis=2).T
    table = table[None]
    bit = 1
    turn = 0
    while bit < experts:
        pairs = [(e, e ^ bit) for e in range(experts)]
        other = lax.ppermute(table, "expert", pairs)
        table = jnp.concatenate([table, after(other, marks[turn % len(marks)])], axis=0)
        bit = bit * 2
        turn = turn + 1
    mine = jnp.sum(jnp.where((ids == me)[None, :, None], table, 0.0), axis=1)
    picks = jnp.array(away, dtype=jnp.int32)[me]
    rows = jnp.sum(jnp.where(picks[:, None, None] == ids[None, :, None], mine[None], 0.0), axis=1)
    return [rows[j][:, None] for j in range(experts)]


def per_device_dense(
    tokens,
    routing,
    gate_scores,
    cotangent,
    w_gate,
    w_up,
    w_down,
    mom_gate,
    mom_up,
    mom_down,
    gossip_round,
):
    tok_rows, feature_width = tokens.shape
    experts = lax.axis_size("expert")
    weight_gate = w_gate[0, 0]
    weight_up = w_up[0, 0]
    weight_down = w_down[0, 0]
    hidden_width = weight_gate.shape[1]
    scale_in = feature_width ** (-0.5)
    scale_hidden = hidden_width ** (-0.5)
    inner_dims = (((1,), (1,)), ((), ()))
    outer_dims = (((0,), (0,)), ((), ()))
    gate_share = gate_scores / jnp.sum(gate_scores, axis=1, keepdims=True)
    tok_blocks, cot_blocks = ring_gather_pair(tokens, cotangent, experts)
    marks = [cot_blocks[step] for step in range(1, experts // 2)]
    share_blocks = own_shares(routing, gate_share, experts, marks)
    weight_both = jnp.concatenate([weight_gate, weight_up], axis=1)
    mom_both = jnp.concatenate([mom_gate[0, 0], mom_up[0, 0]], axis=1)
    weight_both, mom_both = lax.optimization_barrier((weight_both, mom_both))

    arrival = [0]
    for step in range(1, experts // 2):
        arrival = arrival + [step, experts - step]
    arrival.append(experts // 2)

    acts, gate_grads, up_grads = [], [], []
    for place in arrival:
        block, cot, share = tok_blocks[place], cot_blocks[place], share_blocks[place]
        both_pre = jnp.dot(block, weight_both, preferred_element_type=jnp.float32) * scale_in
        gate_pre = both_pre[:, :hidden_width]
        up_pre = both_pre[:, hidden_width:]
        sigmoid_gate = jax.nn.sigmoid(gate_pre)
        acts.append((gate_pre * sigmoid_gate * up_pre * share).astype(jnp.bfloat16))
        grad_act = lax.dot_general(
            cot, weight_down, inner_dims, preferred_element_type=jnp.float32
        ) * (share * scale_hidden)
        gate_grads.append(
            (grad_act * up_pre * sigmoid_gate * (1.0 + gate_pre * (1.0 - sigmoid_gate))).astype(
                jnp.bfloat16
            )
        )
        up_grads.append((grad_act * gate_pre * sigmoid_gate).astype(jnp.bfloat16))
    rows_in = jnp.concatenate([tok_blocks[place] for place in arrival], axis=0)
    rows_cot = jnp.concatenate([cot_blocks[place] for place in arrival], axis=0)
    activation = jnp.concatenate(acts, axis=0)
    both_grads = [jnp.concatenate(pair, axis=1) for pair in zip(gate_grads, up_grads)]
    grad_both_pre = jnp.concatenate(both_grads, axis=0)

    bit_count = lax.axis_size("replica").bit_length() - 1
    bit_now = gossip_round[0] % bit_count

    def swap(local, bit_index, *others):
        return partner_2(after(local, *others) if others else local, "replica", bit_index)

    def averaged(local, swapped):
        partner = local
        for bit_index in range(bit_count):
            partner = jnp.where(bit_now == bit_index, swapped[bit_index], partner)
        mean = (local.astype(jnp.float32) + partner.astype(jnp.float32)) * 0.5
        return mean.astype(jnp.bfloat16)

    grad_down = (
        lax.dot_general(activation, rows_cot, outer_dims, preferred_element_type=jnp.float32)
        * scale_hidden
    )
    down_new, down_moment = momentum_step(weight_down, mom_down[0, 0], grad_down)
    out_parts = [None] * experts
    back_parts = [None] * experts
    for place, act, both_grad in zip(arrival, acts, both_grads):
        act, both_grad = after((act, both_grad), down_new)
        out_parts[place] = (
            jnp.dot(act, weight_down, preferred_element_type=jnp.float32) * scale_hidden
        )
        back_parts[place] = (
            lax.dot_general(both_grad, weight_both, inner_dims, preferred_element_type=jnp.float32)
            * scale_in
        )
    out_parts = [lax.optimization_barrier(part) for part in out_parts]
    back_parts = [lax.optimization_barrier(part) for part in back_parts]
    first = experts // 2
    grad_both_pre = after(grad_both_pre, out_parts[first], back_parts[first])
    grad_both = (
        lax.dot_general(rows_in, grad_both_pre, outer_dims, preferred_element_type=jnp.float32)
        * scale_in
    )
    both_new, both_moment = momentum_step(weight_both, mom_both, grad_both)
    gate_moment = both_moment[:, :hidden_width]
    up_moment = both_moment[:, hidden_width:]

    far = bit_count - 1
    down_far = swap(down_new, far)
    both_far = swap(both_new, far)
    down_swaps = [swap(down_new, bit_index) for bit_index in range(far)] + [down_far]
    both_swaps = [swap(both_new, bit_index) for bit_index in range(far)] + [both_far]
    new_down = averaged(down_new, down_swaps)
    if bit_count == 2:
        new_gate, new_up = mean_halves(bit_now == far, both_new, *both_swaps)
    else:
        new_both = averaged(both_new, both_swaps)
        new_gate, new_up = new_both[:, :hidden_width], new_both[:, hidden_width:]
    parts = [
        jnp.concatenate([out_part, back_part], axis=0)
        for out_part, back_part in zip(out_parts, back_parts)
    ]
    returns = ring_scatter(parts, experts, {3: both_new, 2: down_far})
    layer_out, token_grad = returns[:tok_rows], returns[tok_rows:]
    return (
        layer_out,
        token_grad,
        new_gate[None, None],
        new_up[None, None],
        new_down[None, None],
        gate_moment[None, None],
        up_moment[None, None],
        down_moment[None, None],
    )


def per_device(tokens, routing, *others):
    if routing.shape[1] == lax.axis_size("expert"):
        return per_device_dense(tokens, routing, *others)
    return per_device_routed(tokens, routing, *others)


def solution(mesh):
    placed = (
        P(("replica", "expert"), None),
        P(("replica", "expert"), None),
        P(("replica", "expert"), None),
        P(("replica", "expert"), None),
        P("replica", "expert", None, None),
        P("replica", "expert", None, None),
        P("replica", "expert", None, None),
        P("replica", "expert", None, None),
        P("replica", "expert", None, None),
        P("replica", "expert", None, None),
        P("expert"),
    )
    return jax.shard_map(
        per_device,
        mesh=mesh,
        in_specs=placed,
        out_specs=(
            P(("replica", "expert"), None),
            P(("replica", "expert"), None),
            P("replica", "expert", None, None),
            P("replica", "expert", None, None),
            P("replica", "expert", None, None),
            P("replica", "expert", None, None),
            P("replica", "expert", None, None),
            P("replica", "expert", None, None),
        ),
        check_vma=False,
    )
```

```python
import jax
import jax.numpy as jnp
from jax import lax
from jax.sharding import PartitionSpec as P

momentum_beta = 0.9
learn_rate = 0.1


def partner_2(value, axis, stride):
    mask = 2**stride
    pairs = [(source, source ^ mask) for source in range(lax.axis_size(axis))]
    return lax.ppermute(value, axis, pairs)


def expert_forward(rows_in, weight_gate, weight_up, weight_down):
    scale_in = rows_in.shape[1] ** (-0.5)
    scale_hidden = weight_gate.shape[1] ** (-0.5)
    gate_pre = jnp.dot(rows_in, weight_gate, preferred_element_type=jnp.float32) * scale_in
    up_pre = jnp.dot(rows_in, weight_up, preferred_element_type=jnp.float32) * scale_in
    sigmoid_gate = jax.nn.sigmoid(gate_pre)
    activation = (gate_pre * sigmoid_gate * up_pre).astype(jnp.bfloat16)
    produced = (
        jnp.dot(activation, weight_down, preferred_element_type=jnp.float32) * scale_hidden
    ).astype(jnp.bfloat16)
    return (gate_pre, up_pre, sigmoid_gate, activation, produced)


def expert_backward(
    rows_in,
    rows_grad,
    weight_gate,
    weight_up,
    weight_down,
    gate_pre,
    up_pre,
    sigmoid_gate,
    activation,
):
    scale_in = rows_in.shape[1] ** (-0.5)
    scale_hidden = weight_gate.shape[1] ** (-0.5)
    inner_dims = (((1,), (1,)), ((), ()))
    outer_dims = (((0,), (0,)), ((), ()))
    grad_act = (
        lax.dot_general(rows_grad, weight_down, inner_dims, preferred_element_type=jnp.float32)
        * scale_hidden
    )
    grad_gate_pre = (
        grad_act * up_pre * sigmoid_gate * (1.0 + gate_pre * (1.0 - sigmoid_gate))
    ).astype(jnp.bfloat16)
    grad_up_pre = (grad_act * gate_pre * sigmoid_gate).astype(jnp.bfloat16)
    grad_down = (
        lax.dot_general(activation, rows_grad, outer_dims, preferred_element_type=jnp.float32)
        * scale_hidden
    )
    grad_gate = (
        lax.dot_general(rows_in, grad_gate_pre, outer_dims, preferred_element_type=jnp.float32)
        * scale_in
    )
    grad_up = (
        lax.dot_general(rows_in, grad_up_pre, outer_dims, preferred_element_type=jnp.float32)
        * scale_in
    )
    back_sum = lax.dot_general(
        grad_gate_pre, weight_gate, inner_dims, preferred_element_type=jnp.float32
    )
    back_sum = back_sum + lax.dot_general(
        grad_up_pre, weight_up, inner_dims, preferred_element_type=jnp.float32
    )
    rows_back = (back_sum * scale_in).astype(jnp.bfloat16)
    return (rows_back, grad_gate, grad_up, grad_down)


def momentum_step(weight, moment, gradient):
    moment_new = momentum_beta * moment.astype(jnp.float32) + gradient
    weight_new = (weight.astype(jnp.float32) - learn_rate * moment_new).astype(jnp.bfloat16)
    return (weight_new, moment_new.astype(jnp.bfloat16))


def per_device_routed(
    tokens,
    routing,
    gate_scores,
    cotangent,
    w_gate,
    w_up,
    w_down,
    mom_gate,
    mom_up,
    mom_down,
    gossip_round,
):
    tok_rows, feature_width = tokens.shape
    top_count = routing.shape[1]
    experts = lax.axis_size("expert")
    capacity = max(2, min(tok_rows, tok_rows * top_count // experts + 8))
    gate_share = gate_scores / jnp.sum(gate_scores, axis=1, keepdims=True)
    expert_ids = routing.reshape(-1)
    member = (expert_ids[:, None] == jnp.arange(experts, dtype=jnp.int32)[None, :]).astype(
        jnp.int32
    )
    earlier = jnp.sum((jnp.cumsum(member, axis=0) - member) * member, axis=1)
    target = expert_ids * capacity + earlier
    source = jnp.arange(expert_ids.shape[0], dtype=jnp.int32) // top_count
    send_rows = (
        jnp.zeros((experts * capacity, feature_width), jnp.bfloat16).at[target].set(tokens[source])
    )
    weighted = (gate_share.reshape(-1)[:, None] * cotangent[source].astype(jnp.float32)).astype(
        jnp.bfloat16
    )
    send_grad = (
        jnp.zeros((experts * capacity, feature_width), jnp.bfloat16).at[target].set(weighted)
    )
    arrived = lax.all_to_all(
        send_rows.reshape(experts, capacity, feature_width),
        "expert",
        split_axis=0,
        concat_axis=0,
        tiled=True,
    ).reshape(-1, feature_width)
    arrived_grad = lax.all_to_all(
        send_grad.reshape(experts, capacity, feature_width),
        "expert",
        split_axis=0,
        concat_axis=0,
        tiled=True,
    ).reshape(-1, feature_width)
    weight_gate = w_gate[0, 0]
    weight_up = w_up[0, 0]
    weight_down = w_down[0, 0]
    gate_pre, up_pre, sigmoid_gate, activation, produced = expert_forward(
        arrived, weight_gate, weight_up, weight_down
    )
    returned = lax.all_to_all(
        produced.reshape(experts, capacity, feature_width),
        "expert",
        split_axis=0,
        concat_axis=0,
        tiled=True,
    ).reshape(-1, feature_width)
    picked = returned[target].astype(jnp.float32) * gate_share.reshape(-1)[:, None]
    layer_out = jnp.sum(picked.reshape(tok_rows, top_count, feature_width), axis=1).astype(
        jnp.bfloat16
    )
    rows_back, grad_gate, grad_up, grad_down = expert_backward(
        arrived,
        arrived_grad,
        weight_gate,
        weight_up,
        weight_down,
        gate_pre,
        up_pre,
        sigmoid_gate,
        activation,
    )
    returned_grad = lax.all_to_all(
        rows_back.reshape(experts, capacity, feature_width),
        "expert",
        split_axis=0,
        concat_axis=0,
        tiled=True,
    ).reshape(-1, feature_width)
    picked_back = returned_grad[target].astype(jnp.float32)
    token_grad = jnp.sum(picked_back.reshape(tok_rows, top_count, feature_width), axis=1).astype(
        jnp.bfloat16
    )
    gate_new, gate_moment = momentum_step(weight_gate, mom_gate[0, 0], grad_gate)
    up_new, up_moment = momentum_step(weight_up, mom_up[0, 0], grad_up)
    down_new, down_moment = momentum_step(weight_down, mom_down[0, 0], grad_down)
    hidden_width = weight_gate.shape[1]
    stacked = jnp.stack([gate_new, up_new, down_new.reshape(feature_width, hidden_width)], axis=0)
    bit_count = lax.axis_size("replica").bit_length() - 1
    bit_now = gossip_round[0] % bit_count
    partner = stacked
    for bit_index in range(bit_count):
        swapped = partner_2(stacked, "replica", bit_index)
        partner = jnp.where(bit_now == bit_index, swapped, partner)
    averaged = ((stacked.astype(jnp.float32) + partner.astype(jnp.float32)) * 0.5).astype(
        jnp.bfloat16
    )
    new_gate = averaged[0][None, None]
    new_up = averaged[1][None, None]
    new_down = averaged[2].reshape(hidden_width, feature_width)[None, None]
    return (
        layer_out,
        token_grad,
        new_gate,
        new_up,
        new_down,
        gate_moment[None, None],
        up_moment[None, None],
        down_moment[None, None],
    )


def ring_order(experts):
    return list(range(0, experts, 2)) + list(range(experts - 1, 0, -2))


def ring_hop(value, experts, step):
    order = ring_order(experts)
    pairs = [(order[i], order[(i + step) % experts]) for i in range(experts)]
    return lax.ppermute(value, "expert", pairs)


def after(value, *others):
    return lax.optimization_barrier((value,) + others)[0]


def ring_gather_pair(first, second, experts):
    half = first.shape[0] // 2
    last = experts // 2
    blocks = [[None] * experts, [None] * experts]
    moving = [(first, first), (second, second)]
    for which, own in enumerate((first, second)):
        blocks[which][0] = own
    for step in range(1, last):
        for which in range(2):
            behind, ahead = moving[which]
            behind = ring_hop(behind, experts, 1)
            ahead = ring_hop(ahead, experts, -1)
            moving[which] = lax.optimization_barrier((behind, ahead))
            blocks[which][experts - step], blocks[which][step] = moving[which]
    for which in range(2):
        behind, ahead = moving[which]
        top = ring_hop(behind[:half], experts, 1)
        bottom = ring_hop(ahead[half:], experts, -1)
        blocks[which][last] = jnp.concatenate([top, bottom], axis=0)
    return blocks


def ring_scatter(parts, experts, gates):
    half = parts[0].shape[0] // 2
    last = experts // 2
    f32 = jnp.float32
    forward = ring_hop(parts[last][:half].astype(jnp.bfloat16), experts, 1)
    backward = ring_hop(parts[last][half:].astype(jnp.bfloat16), experts, -1)
    for step in range(last - 1, 0, -1):
        mine_f, mine_b = parts[step], parts[experts - step]
        if step == last - 1:
            add_f = jnp.concatenate([mine_f[:half] + forward.astype(f32), mine_f[half:]], axis=0)
            add_b = jnp.concatenate([mine_b[:half], mine_b[half:] + backward.astype(f32)], axis=0)
        else:
            add_f = mine_f + forward.astype(f32)
            add_b = mine_b + backward.astype(f32)
        add_f, add_b = add_f.astype(jnp.bfloat16), add_b.astype(jnp.bfloat16)
        if step in gates:
            add_f, add_b = after((add_f, add_b), gates[step])
        else:
            add_f, add_b = lax.optimization_barrier((add_f, add_b))
        forward = ring_hop(add_f, experts, 1)
        backward = ring_hop(add_b, experts, -1)
    total = parts[0] + forward.astype(f32) + backward.astype(f32)
    return total.astype(jnp.bfloat16)


def own_shares(routing, gate_share, experts, marks):
    me = lax.axis_index("expert")
    ids = jnp.arange(experts, dtype=jnp.int32)
    order = ring_order(experts)
    away = [[order[(order.index(e) + j) % experts] ^ e for j in range(experts)] for e in range(experts)]
    names = routing[:, None, :] == ids[None, :, None]
    table = jnp.sum(jnp.where(names, gate_share[:, None, :], 0.0), axis=2).T
    table = table[None]
    bit = 1
    turn = 0
    while bit < experts:
        pairs = [(e, e ^ bit) for e in range(experts)]
        other = lax.ppermute(table, "expert", pairs)
        table = jnp.concatenate([table, after(other, marks[turn % len(marks)])], axis=0)
        bit = bit * 2
        turn = turn + 1
    mine = jnp.sum(jnp.where((ids == me)[None, :, None], table, 0.0), axis=1)
    picks = jnp.array(away, dtype=jnp.int32)[me]
    rows = jnp.sum(jnp.where(picks[:, None, None] == ids[None, :, None], mine[None], 0.0), axis=1)
    return [rows[j][:, None] for j in range(experts)]


def per_device_dense(
    tokens,
    routing,
    gate_scores,
    cotangent,
    w_gate,
    w_up,
    w_down,
    mom_gate,
    mom_up,
    mom_down,
    gossip_round,
):
    tok_rows, feature_width = tokens.shape
    experts = lax.axis_size("expert")
    weight_gate = w_gate[0, 0]
    weight_up = w_up[0, 0]
    weight_down = w_down[0, 0]
    hidden_width = weight_gate.shape[1]
    scale_in = feature_width ** (-0.5)
    scale_hidden = hidden_width ** (-0.5)
    inner_dims = (((1,), (1,)), ((), ()))
    outer_dims = (((0,), (0,)), ((), ()))
    gate_share = gate_scores / jnp.sum(gate_scores, axis=1, keepdims=True)
    tok_blocks, cot_blocks = ring_gather_pair(tokens, cotangent, experts)
    marks = (cot_blocks[1], tok_blocks[min(2, experts // 2)], cot_blocks[min(2, experts // 2)])
    share_blocks = own_shares(routing, gate_share, experts, marks)
    weight_both = jnp.concatenate([weight_gate, weight_up], axis=1)

    arrival = [0]
    for step in range(1, experts // 2):
        arrival = arrival + [step, experts - step]
    arrival.append(experts // 2)

    acts, gate_grads, up_grads = [], [], []
    for place in arrival:
        block, cot, share = tok_blocks[place], cot_blocks[place], share_blocks[place]
        both_pre = jnp.dot(block, weight_both, preferred_element_type=jnp.float32) * scale_in
        gate_pre = both_pre[:, :hidden_width]
        up_pre = both_pre[:, hidden_width:]
        sigmoid_gate = jax.nn.sigmoid(gate_pre)
        acts.append((gate_pre * sigmoid_gate * up_pre * share).astype(jnp.bfloat16))
        grad_act = lax.dot_general(
            cot, weight_down, inner_dims, preferred_element_type=jnp.float32
        ) * (share * scale_hidden)
        gate_grads.append(
            (grad_act * up_pre * sigmoid_gate * (1.0 + gate_pre * (1.0 - sigmoid_gate))).astype(
                jnp.bfloat16
            )
        )
        up_grads.append((grad_act * gate_pre * sigmoid_gate).astype(jnp.bfloat16))
    rows_in = jnp.concatenate([tok_blocks[place] for place in arrival], axis=0)
    rows_cot = jnp.concatenate([cot_blocks[place] for place in arrival], axis=0)
    activation = jnp.concatenate(acts, axis=0)
    both_grads = [jnp.concatenate(pair, axis=1) for pair in zip(gate_grads, up_grads)]
    grad_gate_pre = jnp.concatenate(gate_grads, axis=0)
    grad_up_pre = jnp.concatenate(up_grads, axis=0)

    bit_count = lax.axis_size("replica").bit_length() - 1
    bit_now = gossip_round[0] % bit_count

    def swap(local, bit_index, *others):
        return partner_2(after(local, *others) if others else local, "replica", bit_index)

    def averaged(local, swapped):
        partner = local
        for bit_index in range(bit_count):
            partner = jnp.where(bit_now == bit_index, swapped[bit_index], partner)
        mean = (local.astype(jnp.float32) + partner.astype(jnp.float32)) * 0.5
        return mean.astype(jnp.bfloat16)

    grad_down = (
        lax.dot_general(activation, rows_cot, outer_dims, preferred_element_type=jnp.float32)
        * scale_hidden
    )
    down_new, down_moment = momentum_step(weight_down, mom_down[0, 0], grad_down)
    out_parts = [None] * experts
    back_parts = [None] * experts
    for place, act, both_grad in zip(arrival, acts, both_grads):
        act, both_grad = after((act, both_grad), down_new)
        out_parts[place] = (
            jnp.dot(act, weight_down, preferred_element_type=jnp.float32) * scale_hidden
        )
        back_parts[place] = (
            lax.dot_general(both_grad, weight_both, inner_dims, preferred_element_type=jnp.float32)
            * scale_in
        )
    out_parts = [lax.optimization_barrier(part) for part in out_parts]
    back_parts = [lax.optimization_barrier(part) for part in back_parts]
    first = experts // 2
    grad_gate_pre = after(grad_gate_pre, out_parts[first], back_parts[first])
    grad_gate = (
        lax.dot_general(rows_in, grad_gate_pre, outer_dims, preferred_element_type=jnp.float32)
        * scale_in
    )
    gate_new, gate_moment = momentum_step(weight_gate, mom_gate[0, 0], grad_gate)
    grad_up_pre = after(grad_up_pre, gate_new)
    grad_up = (
        lax.dot_general(rows_in, grad_up_pre, outer_dims, preferred_element_type=jnp.float32)
        * scale_in
    )
    up_new, up_moment = momentum_step(weight_up, mom_up[0, 0], grad_up)

    far = bit_count - 1
    down_far = swap(down_new, far)
    gate_far = swap(gate_new, far)
    up_far = swap(up_new, far, down_far)
    down_swaps = [swap(down_new, bit_index) for bit_index in range(far)] + [down_far]
    gate_swaps = [swap(gate_new, bit_index, down_swaps[0]) for bit_index in range(far)] + [gate_far]
    up_swaps = [swap(up_new, bit_index, gate_swaps[0]) for bit_index in range(far)] + [up_far]
    new_down = averaged(down_new, down_swaps)
    new_gate = averaged(gate_new, gate_swaps)
    new_up = averaged(up_new, up_swaps)

    parts = [
        jnp.concatenate([out_part, back_part], axis=0)
        for out_part, back_part in zip(out_parts, back_parts)
    ]
    returns = ring_scatter(parts, experts, {2: down_far, 1: gate_far})
    layer_out, token_grad = returns[:tok_rows], returns[tok_rows:]
    return (
        layer_out,
        token_grad,
        new_gate[None, None],
        new_up[None, None],
        new_down[None, None],
        gate_moment[None, None],
        up_moment[None, None],
        down_moment[None, None],
    )


def per_device(tokens, routing, *others):
    if routing.shape[1] == lax.axis_size("expert"):
        return per_device_dense(tokens, routing, *others)
    return per_device_routed(tokens, routing, *others)


def solution(mesh):
    placed = (
        P(("replica", "expert"), None),
        P(("replica", "expert"), None),
        P(("replica", "expert"), None),
        P(("replica", "expert"), None),
        P("replica", "expert", None, None),
        P("replica", "expert", None, None),
        P("replica", "expert", None, None),
        P("replica", "expert", None, None),
        P("replica", "expert", None, None),
        P("replica", "expert", None, None),
        P("expert"),
    )
    return jax.shard_map(
        per_device,
        mesh=mesh,
        in_specs=placed,
        out_specs=(
            P(("replica", "expert"), None),
            P(("replica", "expert"), None),
            P("replica", "expert", None, None),
            P("replica", "expert", None, None),
            P("replica", "expert", None, None),
            P("replica", "expert", None, None),
            P("replica", "expert", None, None),
            P("replica", "expert", None, None),
        ),
        check_vma=False,
    )
```

```python
import jax
import jax.numpy as jnp
from jax import lax
from jax.sharding import PartitionSpec as P

momentum_beta = 0.9
learn_rate = 0.1


def partner_2(value, axis, stride):
    mask = 2**stride
    pairs = [(source, source ^ mask) for source in range(lax.axis_size(axis))]
    return lax.ppermute(value, axis, pairs)


def expert_forward(rows_in, weight_gate, weight_up, weight_down):
    scale_in = rows_in.shape[1] ** (-0.5)
    scale_hidden = weight_gate.shape[1] ** (-0.5)
    gate_pre = jnp.dot(rows_in, weight_gate, preferred_element_type=jnp.float32) * scale_in
    up_pre = jnp.dot(rows_in, weight_up, preferred_element_type=jnp.float32) * scale_in
    sigmoid_gate = jax.nn.sigmoid(gate_pre)
    activation = (gate_pre * sigmoid_gate * up_pre).astype(jnp.bfloat16)
    produced = (
        jnp.dot(activation, weight_down, preferred_element_type=jnp.float32) * scale_hidden
    ).astype(jnp.bfloat16)
    return (gate_pre, up_pre, sigmoid_gate, activation, produced)


def expert_backward(
    rows_in,
    rows_grad,
    weight_gate,
    weight_up,
    weight_down,
    gate_pre,
    up_pre,
    sigmoid_gate,
    activation,
):
    scale_in = rows_in.shape[1] ** (-0.5)
    scale_hidden = weight_gate.shape[1] ** (-0.5)
    inner_dims = (((1,), (1,)), ((), ()))
    outer_dims = (((0,), (0,)), ((), ()))
    grad_act = (
        lax.dot_general(rows_grad, weight_down, inner_dims, preferred_element_type=jnp.float32)
        * scale_hidden
    )
    grad_gate_pre = (
        grad_act * up_pre * sigmoid_gate * (1.0 + gate_pre * (1.0 - sigmoid_gate))
    ).astype(jnp.bfloat16)
    grad_up_pre = (grad_act * gate_pre * sigmoid_gate).astype(jnp.bfloat16)
    grad_down = (
        lax.dot_general(activation, rows_grad, outer_dims, preferred_element_type=jnp.float32)
        * scale_hidden
    )
    grad_gate = (
        lax.dot_general(rows_in, grad_gate_pre, outer_dims, preferred_element_type=jnp.float32)
        * scale_in
    )
    grad_up = (
        lax.dot_general(rows_in, grad_up_pre, outer_dims, preferred_element_type=jnp.float32)
        * scale_in
    )
    back_sum = lax.dot_general(
        grad_gate_pre, weight_gate, inner_dims, preferred_element_type=jnp.float32
    )
    back_sum = back_sum + lax.dot_general(
        grad_up_pre, weight_up, inner_dims, preferred_element_type=jnp.float32
    )
    rows_back = (back_sum * scale_in).astype(jnp.bfloat16)
    return (rows_back, grad_gate, grad_up, grad_down)


def momentum_step(weight, moment, gradient):
    moment_new = momentum_beta * moment.astype(jnp.float32) + gradient
    weight_new = (weight.astype(jnp.float32) - learn_rate * moment_new).astype(jnp.bfloat16)
    return (weight_new, moment_new.astype(jnp.bfloat16))


def per_device_routed(
    tokens,
    routing,
    gate_scores,
    cotangent,
    w_gate,
    w_up,
    w_down,
    mom_gate,
    mom_up,
    mom_down,
    gossip_round,
):
    tok_rows, feature_width = tokens.shape
    top_count = routing.shape[1]
    experts = lax.axis_size("expert")
    capacity = max(2, min(tok_rows, tok_rows * top_count // experts + 8))
    gate_share = gate_scores / jnp.sum(gate_scores, axis=1, keepdims=True)
    expert_ids = routing.reshape(-1)
    member = (expert_ids[:, None] == jnp.arange(experts, dtype=jnp.int32)[None, :]).astype(
        jnp.int32
    )
    earlier = jnp.sum((jnp.cumsum(member, axis=0) - member) * member, axis=1)
    target = expert_ids * capacity + earlier
    source = jnp.arange(expert_ids.shape[0], dtype=jnp.int32) // top_count
    send_rows = (
        jnp.zeros((experts * capacity, feature_width), jnp.bfloat16).at[target].set(tokens[source])
    )
    weighted = (gate_share.reshape(-1)[:, None] * cotangent[source].astype(jnp.float32)).astype(
        jnp.bfloat16
    )
    send_grad = (
        jnp.zeros((experts * capacity, feature_width), jnp.bfloat16).at[target].set(weighted)
    )
    arrived = lax.all_to_all(
        send_rows.reshape(experts, capacity, feature_width),
        "expert",
        split_axis=0,
        concat_axis=0,
        tiled=True,
    ).reshape(-1, feature_width)
    arrived_grad = lax.all_to_all(
        send_grad.reshape(experts, capacity, feature_width),
        "expert",
        split_axis=0,
        concat_axis=0,
        tiled=True,
    ).reshape(-1, feature_width)
    weight_gate = w_gate[0, 0]
    weight_up = w_up[0, 0]
    weight_down = w_down[0, 0]
    gate_pre, up_pre, sigmoid_gate, activation, produced = expert_forward(
        arrived, weight_gate, weight_up, weight_down
    )
    returned = lax.all_to_all(
        produced.reshape(experts, capacity, feature_width),
        "expert",
        split_axis=0,
        concat_axis=0,
        tiled=True,
    ).reshape(-1, feature_width)
    picked = returned[target].astype(jnp.float32) * gate_share.reshape(-1)[:, None]
    layer_out = jnp.sum(picked.reshape(tok_rows, top_count, feature_width), axis=1).astype(
        jnp.bfloat16
    )
    rows_back, grad_gate, grad_up, grad_down = expert_backward(
        arrived,
        arrived_grad,
        weight_gate,
        weight_up,
        weight_down,
        gate_pre,
        up_pre,
        sigmoid_gate,
        activation,
    )
    returned_grad = lax.all_to_all(
        rows_back.reshape(experts, capacity, feature_width),
        "expert",
        split_axis=0,
        concat_axis=0,
        tiled=True,
    ).reshape(-1, feature_width)
    picked_back = returned_grad[target].astype(jnp.float32)
    token_grad = jnp.sum(picked_back.reshape(tok_rows, top_count, feature_width), axis=1).astype(
        jnp.bfloat16
    )
    gate_new, gate_moment = momentum_step(weight_gate, mom_gate[0, 0], grad_gate)
    up_new, up_moment = momentum_step(weight_up, mom_up[0, 0], grad_up)
    down_new, down_moment = momentum_step(weight_down, mom_down[0, 0], grad_down)
    hidden_width = weight_gate.shape[1]
    stacked = jnp.stack([gate_new, up_new, down_new.reshape(feature_width, hidden_width)], axis=0)
    bit_count = lax.axis_size("replica").bit_length() - 1
    bit_now = gossip_round[0] % bit_count
    partner = stacked
    for bit_index in range(bit_count):
        swapped = partner_2(stacked, "replica", bit_index)
        partner = jnp.where(bit_now == bit_index, swapped, partner)
    averaged = ((stacked.astype(jnp.float32) + partner.astype(jnp.float32)) * 0.5).astype(
        jnp.bfloat16
    )
    new_gate = averaged[0][None, None]
    new_up = averaged[1][None, None]
    new_down = averaged[2].reshape(hidden_width, feature_width)[None, None]
    return (
        layer_out,
        token_grad,
        new_gate,
        new_up,
        new_down,
        gate_moment[None, None],
        up_moment[None, None],
        down_moment[None, None],
    )


def ring_order(experts):
    return list(range(0, experts, 2)) + list(range(experts - 1, 0, -2))


def ring_hop(value, experts, step):
    order = ring_order(experts)
    pairs = [(order[i], order[(i + step) % experts]) for i in range(experts)]
    return lax.ppermute(value, "expert", pairs)


def after(value, *others):
    return lax.optimization_barrier((value,) + others)[0]


def ring_gather_pair(first, second, experts):
    half = first.shape[0] // 2
    last = experts // 2
    blocks = [[None] * experts, [None] * experts]
    moving = [(first, first), (second, second)]
    for which, own in enumerate((first, second)):
        blocks[which][0] = own
    for step in range(1, last):
        for which in range(2):
            behind, ahead = moving[which]
            behind = ring_hop(behind, experts, 1)
            ahead = ring_hop(ahead, experts, -1)
            moving[which] = lax.optimization_barrier((behind, ahead))
            blocks[which][experts - step], blocks[which][step] = moving[which]
    for which in range(2):
        behind, ahead = moving[which]
        top = ring_hop(behind[:half], experts, 1)
        bottom = ring_hop(ahead[half:], experts, -1)
        blocks[which][last] = jnp.concatenate([top, bottom], axis=0)
    return blocks


def ring_scatter(parts, experts, gate):
    half = parts[0].shape[0] // 2
    last = experts // 2
    f32 = jnp.float32
    forward = ring_hop(parts[last][:half].astype(jnp.bfloat16), experts, 1)
    backward = ring_hop(parts[last][half:].astype(jnp.bfloat16), experts, -1)
    for step in range(last - 1, 0, -1):
        mine_f, mine_b = parts[step], parts[experts - step]
        if step == last - 1:
            add_f = jnp.concatenate([mine_f[:half] + forward.astype(f32), mine_f[half:]], axis=0)
            add_b = jnp.concatenate([mine_b[:half], mine_b[half:] + backward.astype(f32)], axis=0)
        else:
            add_f = mine_f + forward.astype(f32)
            add_b = mine_b + backward.astype(f32)
        add_f, add_b = add_f.astype(jnp.bfloat16), add_b.astype(jnp.bfloat16)
        add_f, add_b = after((add_f, add_b), gate(step, forward, backward))
        forward = ring_hop(add_f, experts, 1)
        backward = ring_hop(add_b, experts, -1)
    total = parts[0] + forward.astype(f32) + backward.astype(f32)
    return total.astype(jnp.bfloat16)


def own_shares(routing, gate_share, experts, marks):
    me = lax.axis_index("expert")
    ids = jnp.arange(experts, dtype=jnp.int32)
    order = ring_order(experts)
    away = [[order[(order.index(e) + j) % experts] ^ e for j in range(experts)] for e in range(experts)]
    names = routing[:, None, :] == ids[None, :, None]
    table = jnp.sum(jnp.where(names, gate_share[:, None, :], 0.0), axis=2).T
    table = table[None]
    bit = 1
    turn = 0
    while bit < experts:
        pairs = [(e, e ^ bit) for e in range(experts)]
        other = lax.ppermute(table, "expert", pairs)
        table = jnp.concatenate([table, after(other, marks[turn % len(marks)])], axis=0)
        bit = bit * 2
        turn = turn + 1
    mine = jnp.sum(jnp.where((ids == me)[None, :, None], table, 0.0), axis=1)
    picks = jnp.array(away, dtype=jnp.int32)[me]
    rows = jnp.sum(jnp.where(picks[:, None, None] == ids[None, :, None], mine[None], 0.0), axis=1)
    return [rows[j][:, None] for j in range(experts)]


def per_device_dense(
    tokens,
    routing,
    gate_scores,
    cotangent,
    w_gate,
    w_up,
    w_down,
    mom_gate,
    mom_up,
    mom_down,
    gossip_round,
):
    tok_rows, feature_width = tokens.shape
    experts = lax.axis_size("expert")
    weight_gate = w_gate[0, 0]
    weight_up = w_up[0, 0]
    weight_down = w_down[0, 0]
    hidden_width = weight_gate.shape[1]
    scale_in = feature_width ** (-0.5)
    scale_hidden = hidden_width ** (-0.5)
    inner_dims = (((1,), (1,)), ((), ()))
    outer_dims = (((0,), (0,)), ((), ()))
    gate_share = gate_scores / jnp.sum(gate_scores, axis=1, keepdims=True)
    tok_blocks, cot_blocks = ring_gather_pair(tokens, cotangent, experts)
    marks = (cot_blocks[1], tok_blocks[min(2, experts // 2)], cot_blocks[min(2, experts // 2)])
    share_blocks = own_shares(routing, gate_share, experts, marks)
    weight_both = jnp.concatenate([weight_gate, weight_up], axis=1)

    arrival = [0]
    for step in range(1, experts // 2):
        arrival = arrival + [step, experts - step]
    arrival.append(experts // 2)

    acts, gate_grads, up_grads = [], [], []
    for place in arrival:
        block, cot, share = tok_blocks[place], cot_blocks[place], share_blocks[place]
        both_pre = jnp.dot(block, weight_both, preferred_element_type=jnp.float32) * scale_in
        gate_pre = both_pre[:, :hidden_width]
        up_pre = both_pre[:, hidden_width:]
        sigmoid_gate = jax.nn.sigmoid(gate_pre)
        acts.append((gate_pre * sigmoid_gate * up_pre * share).astype(jnp.bfloat16))
        grad_act = lax.dot_general(
            cot, weight_down, inner_dims, preferred_element_type=jnp.float32
        ) * (share * scale_hidden)
        gate_grads.append(
            (grad_act * up_pre * sigmoid_gate * (1.0 + gate_pre * (1.0 - sigmoid_gate))).astype(
                jnp.bfloat16
            )
        )
        up_grads.append((grad_act * gate_pre * sigmoid_gate).astype(jnp.bfloat16))
    rows_in = jnp.concatenate([tok_blocks[place] for place in arrival], axis=0)
    rows_cot = jnp.concatenate([cot_blocks[place] for place in arrival], axis=0)
    activation = jnp.concatenate(acts, axis=0)
    both_grads = [jnp.concatenate(pair, axis=1) for pair in zip(gate_grads, up_grads)]
    grad_gate_pre = jnp.concatenate(gate_grads, axis=0)
    grad_up_pre = jnp.concatenate(up_grads, axis=0)

    bit_count = lax.axis_size("replica").bit_length() - 1
    bit_now = gossip_round[0] % bit_count

    def swap(local, bit_index, *others):
        return partner_2(after(local, *others) if others else local, "replica", bit_index)

    def averaged(local, swapped):
        partner = local
        for bit_index in range(bit_count):
            partner = jnp.where(bit_now == bit_index, swapped[bit_index], partner)
        mean = (local.astype(jnp.float32) + partner.astype(jnp.float32)) * 0.5
        return mean.astype(jnp.bfloat16)

    grad_down = (
        lax.dot_general(activation, rows_cot, outer_dims, preferred_element_type=jnp.float32)
        * scale_hidden
    )
    down_new, down_moment = momentum_step(weight_down, mom_down[0, 0], grad_down)
    out_parts = [None] * experts
    back_parts = [None] * experts
    for place, act, both_grad in zip(arrival, acts, both_grads):
        act, both_grad = after((act, both_grad), down_new)
        out_parts[place] = (
            jnp.dot(act, weight_down, preferred_element_type=jnp.float32) * scale_hidden
        )
        back_parts[place] = (
            lax.dot_general(both_grad, weight_both, inner_dims, preferred_element_type=jnp.float32)
            * scale_in
        )
    out_parts = [lax.optimization_barrier(part) for part in out_parts]
    back_parts = [lax.optimization_barrier(part) for part in back_parts]
    first = experts // 2
    grad_gate_pre = after(grad_gate_pre, out_parts[first], back_parts[first])
    grad_gate = (
        lax.dot_general(rows_in, grad_gate_pre, outer_dims, preferred_element_type=jnp.float32)
        * scale_in
    )
    gate_new, gate_moment = momentum_step(weight_gate, mom_gate[0, 0], grad_gate)
    grad_up_pre = after(grad_up_pre, gate_new)
    grad_up = (
        lax.dot_general(rows_in, grad_up_pre, outer_dims, preferred_element_type=jnp.float32)
        * scale_in
    )
    up_new, up_moment = momentum_step(weight_up, mom_up[0, 0], grad_up)

    far = bit_count - 1
    down_far = swap(down_new, far)
    gate_far = swap(gate_new, far)
    up_far = swap(up_new, far, down_far)
    down_swaps = [swap(down_new, bit_index) for bit_index in range(far)] + [down_far]
    gate_swaps = []

    def gate(step, forward, backward):
        if step == 2:
            return (down_swaps, up_new, out_parts, back_parts)
        if step == 1:
            for bit_index in range(far):
                gate_swaps.append(swap(gate_new, bit_index, gate_far, forward, backward))
            gate_swaps.append(gate_far)
            return gate_swaps[0]
        return ()

    parts = [
        jnp.concatenate([out_part, back_part], axis=0)
        for out_part, back_part in zip(out_parts, back_parts)
    ]
    returns = ring_scatter(parts, experts, gate)
    layer_out, token_grad = returns[:tok_rows], returns[tok_rows:]

    up_swaps = [swap(up_new, bit_index, gate_swaps[0]) for bit_index in range(far)] + [up_far]
    new_down = averaged(down_new, down_swaps)
    new_gate = averaged(gate_new, gate_swaps)
    new_up = averaged(up_new, up_swaps)
    return (
        layer_out,
        token_grad,
        new_gate[None, None],
        new_up[None, None],
        new_down[None, None],
        gate_moment[None, None],
        up_moment[None, None],
        down_moment[None, None],
    )


def per_device(tokens, routing, *others):
    if routing.shape[1] == lax.axis_size("expert"):
        return per_device_dense(tokens, routing, *others)
    return per_device_routed(tokens, routing, *others)


def solution(mesh):
    placed = (
        P(("replica", "expert"), None),
        P(("replica", "expert"), None),
        P(("replica", "expert"), None),
        P(("replica", "expert"), None),
        P("replica", "expert", None, None),
        P("replica", "expert", None, None),
        P("replica", "expert", None, None),
        P("replica", "expert", None, None),
        P("replica", "expert", None, None),
        P("replica", "expert", None, None),
        P("expert"),
    )
    return jax.shard_map(
        per_device,
        mesh=mesh,
        in_specs=placed,
        out_specs=(
            P(("replica", "expert"), None),
            P(("replica", "expert"), None),
            P("replica", "expert", None, None),
            P("replica", "expert", None, None),
            P("replica", "expert", None, None),
            P("replica", "expert", None, None),
            P("replica", "expert", None, None),
            P("replica", "expert", None, None),
        ),
        check_vma=False,
    )
```

```python
import jax
import jax.numpy as jnp
from jax import lax
from jax.sharding import PartitionSpec as P

momentum_beta = 0.9
learn_rate = 0.1


def partner_2(value, axis, stride):
    mask = 2**stride
    pairs = [(source, source ^ mask) for source in range(lax.axis_size(axis))]
    return lax.ppermute(value, axis, pairs)


def expert_forward(rows_in, weight_gate, weight_up, weight_down):
    scale_in = rows_in.shape[1] ** (-0.5)
    scale_hidden = weight_gate.shape[1] ** (-0.5)
    gate_pre = jnp.dot(rows_in, weight_gate, preferred_element_type=jnp.float32) * scale_in
    up_pre = jnp.dot(rows_in, weight_up, preferred_element_type=jnp.float32) * scale_in
    sigmoid_gate = jax.nn.sigmoid(gate_pre)
    activation = (gate_pre * sigmoid_gate * up_pre).astype(jnp.bfloat16)
    produced = (
        jnp.dot(activation, weight_down, preferred_element_type=jnp.float32) * scale_hidden
    ).astype(jnp.bfloat16)
    return (gate_pre, up_pre, sigmoid_gate, activation, produced)


def expert_backward(
    rows_in,
    rows_grad,
    weight_gate,
    weight_up,
    weight_down,
    gate_pre,
    up_pre,
    sigmoid_gate,
    activation,
):
    scale_in = rows_in.shape[1] ** (-0.5)
    scale_hidden = weight_gate.shape[1] ** (-0.5)
    inner_dims = (((1,), (1,)), ((), ()))
    outer_dims = (((0,), (0,)), ((), ()))
    grad_act = (
        lax.dot_general(rows_grad, weight_down, inner_dims, preferred_element_type=jnp.float32)
        * scale_hidden
    )
    grad_gate_pre = (
        grad_act * up_pre * sigmoid_gate * (1.0 + gate_pre * (1.0 - sigmoid_gate))
    ).astype(jnp.bfloat16)
    grad_up_pre = (grad_act * gate_pre * sigmoid_gate).astype(jnp.bfloat16)
    grad_down = (
        lax.dot_general(activation, rows_grad, outer_dims, preferred_element_type=jnp.float32)
        * scale_hidden
    )
    grad_gate = (
        lax.dot_general(rows_in, grad_gate_pre, outer_dims, preferred_element_type=jnp.float32)
        * scale_in
    )
    grad_up = (
        lax.dot_general(rows_in, grad_up_pre, outer_dims, preferred_element_type=jnp.float32)
        * scale_in
    )
    back_sum = lax.dot_general(
        grad_gate_pre, weight_gate, inner_dims, preferred_element_type=jnp.float32
    )
    back_sum = back_sum + lax.dot_general(
        grad_up_pre, weight_up, inner_dims, preferred_element_type=jnp.float32
    )
    rows_back = (back_sum * scale_in).astype(jnp.bfloat16)
    return (rows_back, grad_gate, grad_up, grad_down)


def momentum_step(weight, moment, gradient):
    moment_new = momentum_beta * moment.astype(jnp.float32) + gradient
    weight_new = (weight.astype(jnp.float32) - learn_rate * moment_new).astype(jnp.bfloat16)
    return (weight_new, moment_new.astype(jnp.bfloat16))


def per_device_routed(
    tokens,
    routing,
    gate_scores,
    cotangent,
    w_gate,
    w_up,
    w_down,
    mom_gate,
    mom_up,
    mom_down,
    gossip_round,
):
    tok_rows, feature_width = tokens.shape
    top_count = routing.shape[1]
    experts = lax.axis_size("expert")
    capacity = max(2, min(tok_rows, tok_rows * top_count // experts + 8))
    gate_share = gate_scores / jnp.sum(gate_scores, axis=1, keepdims=True)
    expert_ids = routing.reshape(-1)
    member = (expert_ids[:, None] == jnp.arange(experts, dtype=jnp.int32)[None, :]).astype(
        jnp.int32
    )
    earlier = jnp.sum((jnp.cumsum(member, axis=0) - member) * member, axis=1)
    target = expert_ids * capacity + earlier
    source = jnp.arange(expert_ids.shape[0], dtype=jnp.int32) // top_count
    send_rows = (
        jnp.zeros((experts * capacity, feature_width), jnp.bfloat16).at[target].set(tokens[source])
    )
    weighted = (gate_share.reshape(-1)[:, None] * cotangent[source].astype(jnp.float32)).astype(
        jnp.bfloat16
    )
    send_grad = (
        jnp.zeros((experts * capacity, feature_width), jnp.bfloat16).at[target].set(weighted)
    )
    arrived = lax.all_to_all(
        send_rows.reshape(experts, capacity, feature_width),
        "expert",
        split_axis=0,
        concat_axis=0,
        tiled=True,
    ).reshape(-1, feature_width)
    arrived_grad = lax.all_to_all(
        send_grad.reshape(experts, capacity, feature_width),
        "expert",
        split_axis=0,
        concat_axis=0,
        tiled=True,
    ).reshape(-1, feature_width)
    weight_gate = w_gate[0, 0]
    weight_up = w_up[0, 0]
    weight_down = w_down[0, 0]
    gate_pre, up_pre, sigmoid_gate, activation, produced = expert_forward(
        arrived, weight_gate, weight_up, weight_down
    )
    returned = lax.all_to_all(
        produced.reshape(experts, capacity, feature_width),
        "expert",
        split_axis=0,
        concat_axis=0,
        tiled=True,
    ).reshape(-1, feature_width)
    picked = returned[target].astype(jnp.float32) * gate_share.reshape(-1)[:, None]
    layer_out = jnp.sum(picked.reshape(tok_rows, top_count, feature_width), axis=1).astype(
        jnp.bfloat16
    )
    rows_back, grad_gate, grad_up, grad_down = expert_backward(
        arrived,
        arrived_grad,
        weight_gate,
        weight_up,
        weight_down,
        gate_pre,
        up_pre,
        sigmoid_gate,
        activation,
    )
    returned_grad = lax.all_to_all(
        rows_back.reshape(experts, capacity, feature_width),
        "expert",
        split_axis=0,
        concat_axis=0,
        tiled=True,
    ).reshape(-1, feature_width)
    picked_back = returned_grad[target].astype(jnp.float32)
    token_grad = jnp.sum(picked_back.reshape(tok_rows, top_count, feature_width), axis=1).astype(
        jnp.bfloat16
    )
    gate_new, gate_moment = momentum_step(weight_gate, mom_gate[0, 0], grad_gate)
    up_new, up_moment = momentum_step(weight_up, mom_up[0, 0], grad_up)
    down_new, down_moment = momentum_step(weight_down, mom_down[0, 0], grad_down)
    hidden_width = weight_gate.shape[1]
    stacked = jnp.stack([gate_new, up_new, down_new.reshape(feature_width, hidden_width)], axis=0)
    bit_count = lax.axis_size("replica").bit_length() - 1
    bit_now = gossip_round[0] % bit_count
    partner = stacked
    for bit_index in range(bit_count):
        swapped = partner_2(stacked, "replica", bit_index)
        partner = jnp.where(bit_now == bit_index, swapped, partner)
    averaged = ((stacked.astype(jnp.float32) + partner.astype(jnp.float32)) * 0.5).astype(
        jnp.bfloat16
    )
    new_gate = averaged[0][None, None]
    new_up = averaged[1][None, None]
    new_down = averaged[2].reshape(hidden_width, feature_width)[None, None]
    return (
        layer_out,
        token_grad,
        new_gate,
        new_up,
        new_down,
        gate_moment[None, None],
        up_moment[None, None],
        down_moment[None, None],
    )


def ring_order(experts):
    return list(range(0, experts, 2)) + list(range(experts - 1, 0, -2))


def ring_hop(value, experts, step):
    order = ring_order(experts)
    pairs = [(order[i], order[(i + step) % experts]) for i in range(experts)]
    return lax.ppermute(value, "expert", pairs)


def after(value, *others):
    return lax.optimization_barrier((value,) + others)[0]


def ring_gather_pair(first, second, experts):
    half = first.shape[0] // 2
    last = experts // 2
    blocks = [[None] * experts, [None] * experts]
    moving = [(first, first), (second, second)]
    for which, own in enumerate((first, second)):
        blocks[which][0] = own
    for step in range(1, last):
        for which in range(2):
            behind, ahead = moving[which]
            behind = ring_hop(behind, experts, 1)
            ahead = ring_hop(ahead, experts, -1)
            moving[which] = after((behind, ahead), moving[0]) if which else (behind, ahead)
            moving[which] = lax.optimization_barrier(moving[which])
            blocks[which][experts - step], blocks[which][step] = moving[which]
    for which in range(2):
        behind, ahead = moving[which]
        top = ring_hop(behind[:half], experts, 1)
        bottom = ring_hop(ahead[half:], experts, -1)
        blocks[which][last] = jnp.concatenate([top, bottom], axis=0)
    return blocks


def ring_scatter(parts, experts, gate):
    half = parts[0].shape[0] // 2
    last = experts // 2
    f32 = jnp.float32
    forward = ring_hop(parts[last][:half].astype(jnp.bfloat16), experts, 1)
    backward = ring_hop(parts[last][half:].astype(jnp.bfloat16), experts, -1)
    for step in range(last - 1, 0, -1):
        mine_f, mine_b = parts[step], parts[experts - step]
        if step == last - 1:
            add_f = jnp.concatenate([mine_f[:half] + forward.astype(f32), mine_f[half:]], axis=0)
            add_b = jnp.concatenate([mine_b[:half], mine_b[half:] + backward.astype(f32)], axis=0)
        else:
            add_f = mine_f + forward.astype(f32)
            add_b = mine_b + backward.astype(f32)
        add_f, add_b = add_f.astype(jnp.bfloat16), add_b.astype(jnp.bfloat16)
        add_f, add_b = after((add_f, add_b), gate(step, forward, backward))
        forward = ring_hop(add_f, experts, 1)
        backward = ring_hop(add_b, experts, -1)
    total = parts[0] + forward.astype(f32) + backward.astype(f32)
    return total.astype(jnp.bfloat16)


def own_shares(routing, gate_share, experts, marks):
    me = lax.axis_index("expert")
    ids = jnp.arange(experts, dtype=jnp.int32)
    order = ring_order(experts)
    away = [[order[(order.index(e) + j) % experts] ^ e for j in range(experts)] for e in range(experts)]
    names = routing[:, None, :] == ids[None, :, None]
    table = jnp.sum(jnp.where(names, gate_share[:, None, :], 0.0), axis=2).T
    table = table[None]
    bit = 1
    turn = 0
    while bit < experts:
        pairs = [(e, e ^ bit) for e in range(experts)]
        other = lax.ppermute(table, "expert", pairs)
        table = jnp.concatenate([table, after(other, marks[turn % len(marks)])], axis=0)
        bit = bit * 2
        turn = turn + 1
    mine = jnp.sum(jnp.where((ids == me)[None, :, None], table, 0.0), axis=1)
    picks = jnp.array(away, dtype=jnp.int32)[me]
    rows = jnp.sum(jnp.where(picks[:, None, None] == ids[None, :, None], mine[None], 0.0), axis=1)
    return [rows[j][:, None] for j in range(experts)]


def per_device_dense(
    tokens,
    routing,
    gate_scores,
    cotangent,
    w_gate,
    w_up,
    w_down,
    mom_gate,
    mom_up,
    mom_down,
    gossip_round,
):
    tok_rows, feature_width = tokens.shape
    experts = lax.axis_size("expert")
    weight_gate = w_gate[0, 0]
    weight_up = w_up[0, 0]
    weight_down = w_down[0, 0]
    hidden_width = weight_gate.shape[1]
    scale_in = feature_width ** (-0.5)
    scale_hidden = hidden_width ** (-0.5)
    inner_dims = (((1,), (1,)), ((), ()))
    outer_dims = (((0,), (0,)), ((), ()))
    gate_share = gate_scores / jnp.sum(gate_scores, axis=1, keepdims=True)
    tok_blocks, cot_blocks = ring_gather_pair(tokens, cotangent, experts)
    marks = (cot_blocks[1], tok_blocks[min(2, experts // 2)], cot_blocks[min(2, experts // 2)])
    share_blocks = own_shares(routing, gate_share, experts, marks)
    weight_both = jnp.concatenate([weight_gate, weight_up], axis=1)
    mom_both = jnp.concatenate([mom_gate[0, 0], mom_up[0, 0]], axis=1)

    arrival = [0]
    for step in range(1, experts // 2):
        arrival = arrival + [step, experts - step]
    arrival.append(experts // 2)

    acts, gate_grads, up_grads = [], [], []
    for place in arrival:
        block, cot, share = tok_blocks[place], cot_blocks[place], share_blocks[place]
        both_pre = jnp.dot(block, weight_both, preferred_element_type=jnp.float32) * scale_in
        gate_pre = both_pre[:, :hidden_width]
        up_pre = both_pre[:, hidden_width:]
        sigmoid_gate = jax.nn.sigmoid(gate_pre)
        acts.append((gate_pre * sigmoid_gate * up_pre * share).astype(jnp.bfloat16))
        grad_act = lax.dot_general(
            cot, weight_down, inner_dims, preferred_element_type=jnp.float32
        ) * (share * scale_hidden)
        gate_grads.append(
            (grad_act * up_pre * sigmoid_gate * (1.0 + gate_pre * (1.0 - sigmoid_gate))).astype(
                jnp.bfloat16
            )
        )
        up_grads.append((grad_act * gate_pre * sigmoid_gate).astype(jnp.bfloat16))
    rows_in = jnp.concatenate([tok_blocks[place] for place in arrival], axis=0)
    rows_cot = jnp.concatenate([cot_blocks[place] for place in arrival], axis=0)
    activation = jnp.concatenate(acts, axis=0)
    both_grads = [jnp.concatenate(pair, axis=1) for pair in zip(gate_grads, up_grads)]
    grad_both_pre = jnp.concatenate(both_grads, axis=0)

    bit_count = lax.axis_size("replica").bit_length() - 1
    bit_now = gossip_round[0] % bit_count

    def swap(local, bit_index, *others):
        return partner_2(after(local, *others) if others else local, "replica", bit_index)

    def mean(one, other):
        total = one.astype(jnp.float32) + other.astype(jnp.float32)
        return (total * 0.5).astype(jnp.bfloat16)

    def with_near(local, swapped):
        result = local
        for bit_index, value in enumerate(swapped):
            result = jnp.where(bit_now == bit_index, mean(local, value), result)
        return lax.optimization_barrier(result)

    def with_far(base, value):
        return jnp.where(bit_now == bit_count - 1, mean(base, value), base)

    def averaged(local, swapped):
        return with_far(with_near(local, swapped[:-1]), swapped[-1])

    grad_down = (
        lax.dot_general(activation, rows_cot, outer_dims, preferred_element_type=jnp.float32)
        * scale_hidden
    )
    down_new, down_moment = momentum_step(weight_down, mom_down[0, 0], grad_down)
    out_parts = [None] * experts
    back_parts = [None] * experts
    for place, act, both_grad in zip(arrival, acts, both_grads):
        act, both_grad = after((act, both_grad), down_new)
        out_parts[place] = (
            jnp.dot(act, weight_down, preferred_element_type=jnp.float32) * scale_hidden
        )
        back_parts[place] = (
            lax.dot_general(both_grad, weight_both, inner_dims, preferred_element_type=jnp.float32)
            * scale_in
        )
    out_parts = [lax.optimization_barrier(part) for part in out_parts]
    back_parts = [lax.optimization_barrier(part) for part in back_parts]
    first = experts // 2
    grad_both_pre = after(grad_both_pre, out_parts[first], back_parts[first])
    grad_both = (
        lax.dot_general(rows_in, grad_both_pre, outer_dims, preferred_element_type=jnp.float32)
        * scale_in
    )
    both_new, both_moment = momentum_step(weight_both, mom_both, grad_both)
    gate_moment = both_moment[:, :hidden_width]
    up_moment = both_moment[:, hidden_width:]

    far = bit_count - 1
    down_far = swap(down_new, far)
    both_far = swap(both_new, far)
    down_near = [swap(down_new, bit_index) for bit_index in range(far)]
    both_near = [swap(both_new, bit_index, down_far) for bit_index in range(far)]

    def gate(step, forward, backward):
        if step == 3:
            return (both_new, down_near)
        if step == 2:
            return (down_far,)
        return ()

    parts = [
        jnp.concatenate([out_part, back_part], axis=0)
        for out_part, back_part in zip(out_parts, back_parts)
    ]
    returns = ring_scatter(parts, experts, gate)
    layer_out, token_grad = returns[:tok_rows], returns[tok_rows:]

    new_down = averaged(down_new, down_near + [down_far])
    both_base = with_near(both_new, both_near)
    new_gate = with_far(both_base[:, :hidden_width], both_far[:, :hidden_width])
    new_up = with_far(both_base[:, hidden_width:], both_far[:, hidden_width:])
    return (
        layer_out,
        token_grad,
        new_gate[None, None],
        new_up[None, None],
        new_down[None, None],
        gate_moment[None, None],
        up_moment[None, None],
        down_moment[None, None],
    )


def per_device(tokens, routing, *others):
    if routing.shape[1] == lax.axis_size("expert"):
        return per_device_dense(tokens, routing, *others)
    return per_device_routed(tokens, routing, *others)


def solution(mesh):
    placed = (
        P(("replica", "expert"), None),
        P(("replica", "expert"), None),
        P(("replica", "expert"), None),
        P(("replica", "expert"), None),
        P("replica", "expert", None, None),
        P("replica", "expert", None, None),
        P("replica", "expert", None, None),
        P("replica", "expert", None, None),
        P("replica", "expert", None, None),
        P("replica", "expert", None, None),
        P("expert"),
    )
    return jax.shard_map(
        per_device,
        mesh=mesh,
        in_specs=placed,
        out_specs=(
            P(("replica", "expert"), None),
            P(("replica", "expert"), None),
            P("replica", "expert", None, None),
            P("replica", "expert", None, None),
            P("replica", "expert", None, None),
            P("replica", "expert", None, None),
            P("replica", "expert", None, None),
            P("replica", "expert", None, None),
        ),
        check_vma=False,
    )
```

```python
import jax
import jax.numpy as jnp
from jax import lax
from jax.sharding import PartitionSpec as P

momentum_beta = 0.9
learn_rate = 0.1


def partner_2(value, axis, stride):
    mask = 2**stride
    pairs = [(source, source ^ mask) for source in range(lax.axis_size(axis))]
    return lax.ppermute(value, axis, pairs)


def expert_forward(rows_in, weight_gate, weight_up, weight_down):
    scale_in = rows_in.shape[1] ** (-0.5)
    scale_hidden = weight_gate.shape[1] ** (-0.5)
    gate_pre = jnp.dot(rows_in, weight_gate, preferred_element_type=jnp.float32) * scale_in
    up_pre = jnp.dot(rows_in, weight_up, preferred_element_type=jnp.float32) * scale_in
    sigmoid_gate = jax.nn.sigmoid(gate_pre)
    activation = (gate_pre * sigmoid_gate * up_pre).astype(jnp.bfloat16)
    produced = (
        jnp.dot(activation, weight_down, preferred_element_type=jnp.float32) * scale_hidden
    ).astype(jnp.bfloat16)
    return (gate_pre, up_pre, sigmoid_gate, activation, produced)


def expert_backward(
    rows_in,
    rows_grad,
    weight_gate,
    weight_up,
    weight_down,
    gate_pre,
    up_pre,
    sigmoid_gate,
    activation,
):
    scale_in = rows_in.shape[1] ** (-0.5)
    scale_hidden = weight_gate.shape[1] ** (-0.5)
    inner_dims = (((1,), (1,)), ((), ()))
    outer_dims = (((0,), (0,)), ((), ()))
    grad_act = (
        lax.dot_general(rows_grad, weight_down, inner_dims, preferred_element_type=jnp.float32)
        * scale_hidden
    )
    grad_gate_pre = (
        grad_act * up_pre * sigmoid_gate * (1.0 + gate_pre * (1.0 - sigmoid_gate))
    ).astype(jnp.bfloat16)
    grad_up_pre = (grad_act * gate_pre * sigmoid_gate).astype(jnp.bfloat16)
    grad_down = (
        lax.dot_general(activation, rows_grad, outer_dims, preferred_element_type=jnp.float32)
        * scale_hidden
    )
    grad_gate = (
        lax.dot_general(rows_in, grad_gate_pre, outer_dims, preferred_element_type=jnp.float32)
        * scale_in
    )
    grad_up = (
        lax.dot_general(rows_in, grad_up_pre, outer_dims, preferred_element_type=jnp.float32)
        * scale_in
    )
    back_sum = lax.dot_general(
        grad_gate_pre, weight_gate, inner_dims, preferred_element_type=jnp.float32
    )
    back_sum = back_sum + lax.dot_general(
        grad_up_pre, weight_up, inner_dims, preferred_element_type=jnp.float32
    )
    rows_back = (back_sum * scale_in).astype(jnp.bfloat16)
    return (rows_back, grad_gate, grad_up, grad_down)


def momentum_step(weight, moment, gradient):
    moment_new = momentum_beta * moment.astype(jnp.float32) + gradient
    weight_new = (weight.astype(jnp.float32) - learn_rate * moment_new).astype(jnp.bfloat16)
    return (weight_new, moment_new.astype(jnp.bfloat16))


def per_device_routed(
    tokens,
    routing,
    gate_scores,
    cotangent,
    w_gate,
    w_up,
    w_down,
    mom_gate,
    mom_up,
    mom_down,
    gossip_round,
):
    tok_rows, feature_width = tokens.shape
    top_count = routing.shape[1]
    experts = lax.axis_size("expert")
    capacity = max(2, min(tok_rows, tok_rows * top_count // experts + 8))
    gate_share = gate_scores / jnp.sum(gate_scores, axis=1, keepdims=True)
    expert_ids = routing.reshape(-1)
    member = (expert_ids[:, None] == jnp.arange(experts, dtype=jnp.int32)[None, :]).astype(
        jnp.int32
    )
    earlier = jnp.sum((jnp.cumsum(member, axis=0) - member) * member, axis=1)
    target = expert_ids * capacity + earlier
    source = jnp.arange(expert_ids.shape[0], dtype=jnp.int32) // top_count
    send_rows = (
        jnp.zeros((experts * capacity, feature_width), jnp.bfloat16).at[target].set(tokens[source])
    )
    weighted = (gate_share.reshape(-1)[:, None] * cotangent[source].astype(jnp.float32)).astype(
        jnp.bfloat16
    )
    send_grad = (
        jnp.zeros((experts * capacity, feature_width), jnp.bfloat16).at[target].set(weighted)
    )
    arrived = lax.all_to_all(
        send_rows.reshape(experts, capacity, feature_width),
        "expert",
        split_axis=0,
        concat_axis=0,
        tiled=True,
    ).reshape(-1, feature_width)
    arrived_grad = lax.all_to_all(
        send_grad.reshape(experts, capacity, feature_width),
        "expert",
        split_axis=0,
        concat_axis=0,
        tiled=True,
    ).reshape(-1, feature_width)
    weight_gate = w_gate[0, 0]
    weight_up = w_up[0, 0]
    weight_down = w_down[0, 0]
    gate_pre, up_pre, sigmoid_gate, activation, produced = expert_forward(
        arrived, weight_gate, weight_up, weight_down
    )
    returned = lax.all_to_all(
        produced.reshape(experts, capacity, feature_width),
        "expert",
        split_axis=0,
        concat_axis=0,
        tiled=True,
    ).reshape(-1, feature_width)
    picked = returned[target].astype(jnp.float32) * gate_share.reshape(-1)[:, None]
    layer_out = jnp.sum(picked.reshape(tok_rows, top_count, feature_width), axis=1).astype(
        jnp.bfloat16
    )
    rows_back, grad_gate, grad_up, grad_down = expert_backward(
        arrived,
        arrived_grad,
        weight_gate,
        weight_up,
        weight_down,
        gate_pre,
        up_pre,
        sigmoid_gate,
        activation,
    )
    returned_grad = lax.all_to_all(
        rows_back.reshape(experts, capacity, feature_width),
        "expert",
        split_axis=0,
        concat_axis=0,
        tiled=True,
    ).reshape(-1, feature_width)
    picked_back = returned_grad[target].astype(jnp.float32)
    token_grad = jnp.sum(picked_back.reshape(tok_rows, top_count, feature_width), axis=1).astype(
        jnp.bfloat16
    )
    gate_new, gate_moment = momentum_step(weight_gate, mom_gate[0, 0], grad_gate)
    up_new, up_moment = momentum_step(weight_up, mom_up[0, 0], grad_up)
    down_new, down_moment = momentum_step(weight_down, mom_down[0, 0], grad_down)
    hidden_width = weight_gate.shape[1]
    stacked = jnp.stack([gate_new, up_new, down_new.reshape(feature_width, hidden_width)], axis=0)
    bit_count = lax.axis_size("replica").bit_length() - 1
    bit_now = gossip_round[0] % bit_count
    partner = stacked
    for bit_index in range(bit_count):
        swapped = partner_2(stacked, "replica", bit_index)
        partner = jnp.where(bit_now == bit_index, swapped, partner)
    averaged = ((stacked.astype(jnp.float32) + partner.astype(jnp.float32)) * 0.5).astype(
        jnp.bfloat16
    )
    new_gate = averaged[0][None, None]
    new_up = averaged[1][None, None]
    new_down = averaged[2].reshape(hidden_width, feature_width)[None, None]
    return (
        layer_out,
        token_grad,
        new_gate,
        new_up,
        new_down,
        gate_moment[None, None],
        up_moment[None, None],
        down_moment[None, None],
    )


def ring_order(experts):
    return list(range(0, experts, 2)) + list(range(experts - 1, 0, -2))


def ring_hop(value, experts, step):
    order = ring_order(experts)
    pairs = [(order[i], order[(i + step) % experts]) for i in range(experts)]
    return lax.ppermute(value, "expert", pairs)


def after(value, *others):
    return lax.optimization_barrier((value,) + others)[0]


def ring_gather_pair(first, second, experts):
    last = experts // 2
    blocks = [[None] * experts, [None] * experts]
    moving = [(first, first), (second, second)]
    for which, own in enumerate((first, second)):
        blocks[which][0] = own
    for step in range(1, last):
        for which in range(2):
            behind, ahead = moving[which]
            behind = ring_hop(behind, experts, 1)
            ahead = ring_hop(ahead, experts, -1)
            moving[which] = after((behind, ahead), moving[0]) if which else (behind, ahead)
            moving[which] = lax.optimization_barrier(moving[which])
            blocks[which][experts - step], blocks[which][step] = moving[which]
    blocks[0][last] = ring_hop(moving[0][0], experts, 1)
    blocks[1][last] = ring_hop(moving[1][1], experts, -1)
    return blocks


def ring_scatter(parts, experts, gate):
    half = parts[0].shape[0] // 2
    last = experts // 2
    f32 = jnp.float32
    forward = ring_hop(parts[last][:half].astype(jnp.bfloat16), experts, 1)
    backward = ring_hop(parts[last][half:].astype(jnp.bfloat16), experts, -1)
    for step in range(last - 1, 0, -1):
        mine_f, mine_b = parts[step], parts[experts - step]
        if step == last - 1:
            add_f = jnp.concatenate([mine_f[:half] + forward.astype(f32), mine_f[half:]], axis=0)
            add_b = jnp.concatenate([mine_b[:half], mine_b[half:] + backward.astype(f32)], axis=0)
        else:
            add_f = mine_f + forward.astype(f32)
            add_b = mine_b + backward.astype(f32)
        add_f, add_b = add_f.astype(jnp.bfloat16), add_b.astype(jnp.bfloat16)
        add_f, add_b = after((add_f, add_b), gate(step, forward, backward))
        forward = ring_hop(add_f, experts, 1)
        backward = ring_hop(add_b, experts, -1)
    total = parts[0] + forward.astype(f32) + backward.astype(f32)
    return total.astype(jnp.bfloat16)


def own_shares(routing, gate_share, experts, mark):
    me = lax.axis_index("expert")
    ids = jnp.arange(experts, dtype=jnp.int32)
    order = ring_order(experts)
    ahead = [[order[(order.index(e) + j) % experts] for j in range(experts)] for e in range(experts)]
    names = routing[:, None, :] == ids[None, :, None]
    table = jnp.sum(jnp.where(names, gate_share[:, None, :], 0.0), axis=2).T
    mine = lax.all_to_all(table, "expert", split_axis=0, concat_axis=0, tiled=True)
    mine = after(mine, mark)
    picks = jnp.array(ahead, dtype=jnp.int32)[me]
    rows = jnp.sum(jnp.where(picks[:, None, None] == ids[None, :, None], mine[None], 0.0), axis=1)
    return [rows[j][:, None] for j in range(experts)]


def per_device_dense(
    tokens,
    routing,
    gate_scores,
    cotangent,
    w_gate,
    w_up,
    w_down,
    mom_gate,
    mom_up,
    mom_down,
    gossip_round,
):
    tok_rows, feature_width = tokens.shape
    experts = lax.axis_size("expert")
    weight_gate = w_gate[0, 0]
    weight_up = w_up[0, 0]
    weight_down = w_down[0, 0]
    hidden_width = weight_gate.shape[1]
    scale_in = feature_width ** (-0.5)
    scale_hidden = hidden_width ** (-0.5)
    inner_dims = (((1,), (1,)), ((), ()))
    outer_dims = (((0,), (0,)), ((), ()))
    gate_share = gate_scores / jnp.sum(gate_scores, axis=1, keepdims=True)
    tok_blocks, cot_blocks = ring_gather_pair(tokens, cotangent, experts)
    mark = tok_blocks[min(2, experts // 2)]
    share_blocks = own_shares(routing, gate_share, experts, mark)
    weight_both = jnp.concatenate([weight_gate, weight_up], axis=1)
    mom_both = jnp.concatenate([mom_gate[0, 0], mom_up[0, 0]], axis=1)

    arrival = [0]
    for step in range(1, experts // 2):
        arrival = arrival + [step, experts - step]
    arrival.append(experts // 2)

    acts, gate_grads, up_grads = [], [], []
    for place in arrival:
        block, cot, share = tok_blocks[place], cot_blocks[place], share_blocks[place]
        both_pre = jnp.dot(block, weight_both, preferred_element_type=jnp.float32) * scale_in
        gate_pre = both_pre[:, :hidden_width]
        up_pre = both_pre[:, hidden_width:]
        sigmoid_gate = jax.nn.sigmoid(gate_pre)
        acts.append((gate_pre * sigmoid_gate * up_pre * share).astype(jnp.bfloat16))
        grad_act = lax.dot_general(
            cot, weight_down, inner_dims, preferred_element_type=jnp.float32
        ) * (share * scale_hidden)
        gate_grads.append(
            (grad_act * up_pre * sigmoid_gate * (1.0 + gate_pre * (1.0 - sigmoid_gate))).astype(
                jnp.bfloat16
            )
        )
        up_grads.append((grad_act * gate_pre * sigmoid_gate).astype(jnp.bfloat16))
    rows_in = jnp.concatenate([tok_blocks[place] for place in arrival], axis=0)
    rows_cot = jnp.concatenate([cot_blocks[place] for place in arrival], axis=0)
    activation = jnp.concatenate(acts, axis=0)
    both_grads = [jnp.concatenate(pair, axis=1) for pair in zip(gate_grads, up_grads)]
    grad_both_pre = jnp.concatenate(both_grads, axis=0)

    bit_count = lax.axis_size("replica").bit_length() - 1
    bit_now = gossip_round[0] % bit_count

    def swap(local, bit_index, *others):
        return partner_2(after(local, *others) if others else local, "replica", bit_index)

    def mean(one, other):
        total = one.astype(jnp.float32) + other.astype(jnp.float32)
        return (total * 0.5).astype(jnp.bfloat16)

    def with_near(local, swapped):
        result = local
        for bit_index, value in enumerate(swapped):
            result = jnp.where(bit_now == bit_index, mean(local, value), result)
        return lax.optimization_barrier(result)

    def with_far(base, value):
        return jnp.where(bit_now == bit_count - 1, mean(base, value), base)

    def averaged(local, swapped):
        return with_far(with_near(local, swapped[:-1]), swapped[-1])

    grad_down = (
        lax.dot_general(activation, rows_cot, outer_dims, preferred_element_type=jnp.float32)
        * scale_hidden
    )
    down_new, down_moment = momentum_step(weight_down, mom_down[0, 0], grad_down)
    out_parts = [None] * experts
    back_parts = [None] * experts
    for place, act, both_grad in zip(arrival, acts, both_grads):
        act, both_grad = after((act, both_grad), down_new)
        out_parts[place] = (
            jnp.dot(act, weight_down, preferred_element_type=jnp.float32) * scale_hidden
        )
        back_parts[place] = (
            lax.dot_general(both_grad, weight_both, inner_dims, preferred_element_type=jnp.float32)
            * scale_in
        )
    out_parts = [lax.optimization_barrier(part) for part in out_parts]
    back_parts = [lax.optimization_barrier(part) for part in back_parts]
    first = experts // 2
    grad_both_pre = after(grad_both_pre, out_parts[first], back_parts[first])
    grad_both = (
        lax.dot_general(rows_in, grad_both_pre, outer_dims, preferred_element_type=jnp.float32)
        * scale_in
    )
    both_new, both_moment = momentum_step(weight_both, mom_both, grad_both)
    gate_moment = both_moment[:, :hidden_width]
    up_moment = both_moment[:, hidden_width:]

    far = bit_count - 1
    down_far = swap(down_new, far)
    both_far = swap(both_new, far)
    down_near = [swap(down_new, bit_index) for bit_index in range(far)]
    both_near = [swap(both_new, bit_index, down_far) for bit_index in range(far)]

    def gate(step, forward, backward):
        if step == 3:
            return (both_new, down_near)
        if step == 2:
            return (down_far,)
        return ()

    parts = [
        jnp.concatenate([out_part, back_part], axis=0)
        for out_part, back_part in zip(out_parts, back_parts)
    ]
    returns = ring_scatter(parts, experts, gate)
    layer_out, token_grad = returns[:tok_rows], returns[tok_rows:]

    new_down = averaged(down_new, down_near + [down_far])
    both_base = with_near(both_new, both_near)
    new_gate = with_far(both_base[:, :hidden_width], both_far[:, :hidden_width])
    new_up = with_far(both_base[:, hidden_width:], both_far[:, hidden_width:])
    return (
        layer_out,
        token_grad,
        new_gate[None, None],
        new_up[None, None],
        new_down[None, None],
        gate_moment[None, None],
        up_moment[None, None],
        down_moment[None, None],
    )


def per_device(tokens, routing, *others):
    if routing.shape[1] == lax.axis_size("expert"):
        return per_device_dense(tokens, routing, *others)
    return per_device_routed(tokens, routing, *others)


def solution(mesh):
    placed = (
        P(("replica", "expert"), None),
        P(("replica", "expert"), None),
        P(("replica", "expert"), None),
        P(("replica", "expert"), None),
        P("replica", "expert", None, None),
        P("replica", "expert", None, None),
        P("replica", "expert", None, None),
        P("replica", "expert", None, None),
        P("replica", "expert", None, None),
        P("replica", "expert", None, None),
        P("expert"),
    )
    return jax.shard_map(
        per_device,
        mesh=mesh,
        in_specs=placed,
        out_specs=(
            P(("replica", "expert"), None),
            P(("replica", "expert"), None),
            P("replica", "expert", None, None),
            P("replica", "expert", None, None),
            P("replica", "expert", None, None),
            P("replica", "expert", None, None),
            P("replica", "expert", None, None),
            P("replica", "expert", None, None),
        ),
        check_vma=False,
    )
```

```python
import jax
import jax.numpy as jnp
from jax import lax
from jax.sharding import PartitionSpec as P

momentum_beta = 0.9
learn_rate = 0.1


def partner_2(value, axis, stride):
    mask = 2**stride
    pairs = [(source, source ^ mask) for source in range(lax.axis_size(axis))]
    return lax.ppermute(value, axis, pairs)


def expert_forward(rows_in, weight_gate, weight_up, weight_down):
    scale_in = rows_in.shape[1] ** (-0.5)
    scale_hidden = weight_gate.shape[1] ** (-0.5)
    gate_pre = jnp.dot(rows_in, weight_gate, preferred_element_type=jnp.float32) * scale_in
    up_pre = jnp.dot(rows_in, weight_up, preferred_element_type=jnp.float32) * scale_in
    sigmoid_gate = jax.nn.sigmoid(gate_pre)
    activation = (gate_pre * sigmoid_gate * up_pre).astype(jnp.bfloat16)
    produced = (
        jnp.dot(activation, weight_down, preferred_element_type=jnp.float32) * scale_hidden
    ).astype(jnp.bfloat16)
    return (gate_pre, up_pre, sigmoid_gate, activation, produced)


def expert_backward(
    rows_in,
    rows_grad,
    weight_gate,
    weight_up,
    weight_down,
    gate_pre,
    up_pre,
    sigmoid_gate,
    activation,
):
    scale_in = rows_in.shape[1] ** (-0.5)
    scale_hidden = weight_gate.shape[1] ** (-0.5)
    inner_dims = (((1,), (1,)), ((), ()))
    outer_dims = (((0,), (0,)), ((), ()))
    grad_act = (
        lax.dot_general(rows_grad, weight_down, inner_dims, preferred_element_type=jnp.float32)
        * scale_hidden
    )
    grad_gate_pre = (
        grad_act * up_pre * sigmoid_gate * (1.0 + gate_pre * (1.0 - sigmoid_gate))
    ).astype(jnp.bfloat16)
    grad_up_pre = (grad_act * gate_pre * sigmoid_gate).astype(jnp.bfloat16)
    grad_down = (
        lax.dot_general(activation, rows_grad, outer_dims, preferred_element_type=jnp.float32)
        * scale_hidden
    )
    grad_gate = (
        lax.dot_general(rows_in, grad_gate_pre, outer_dims, preferred_element_type=jnp.float32)
        * scale_in
    )
    grad_up = (
        lax.dot_general(rows_in, grad_up_pre, outer_dims, preferred_element_type=jnp.float32)
        * scale_in
    )
    back_sum = lax.dot_general(
        grad_gate_pre, weight_gate, inner_dims, preferred_element_type=jnp.float32
    )
    back_sum = back_sum + lax.dot_general(
        grad_up_pre, weight_up, inner_dims, preferred_element_type=jnp.float32
    )
    rows_back = (back_sum * scale_in).astype(jnp.bfloat16)
    return (rows_back, grad_gate, grad_up, grad_down)


def momentum_step(weight, moment, gradient):
    moment_new = momentum_beta * moment.astype(jnp.float32) + gradient
    weight_new = (weight.astype(jnp.float32) - learn_rate * moment_new).astype(jnp.bfloat16)
    return (weight_new, moment_new.astype(jnp.bfloat16))


def per_device_routed(
    tokens,
    routing,
    gate_scores,
    cotangent,
    w_gate,
    w_up,
    w_down,
    mom_gate,
    mom_up,
    mom_down,
    gossip_round,
):
    tok_rows, feature_width = tokens.shape
    top_count = routing.shape[1]
    experts = lax.axis_size("expert")
    capacity = max(2, min(tok_rows, tok_rows * top_count // experts + 8))
    gate_share = gate_scores / jnp.sum(gate_scores, axis=1, keepdims=True)
    expert_ids = routing.reshape(-1)
    member = (expert_ids[:, None] == jnp.arange(experts, dtype=jnp.int32)[None, :]).astype(
        jnp.int32
    )
    earlier = jnp.sum((jnp.cumsum(member, axis=0) - member) * member, axis=1)
    target = expert_ids * capacity + earlier
    source = jnp.arange(expert_ids.shape[0], dtype=jnp.int32) // top_count
    send_rows = (
        jnp.zeros((experts * capacity, feature_width), jnp.bfloat16).at[target].set(tokens[source])
    )
    weighted = (gate_share.reshape(-1)[:, None] * cotangent[source].astype(jnp.float32)).astype(
        jnp.bfloat16
    )
    send_grad = (
        jnp.zeros((experts * capacity, feature_width), jnp.bfloat16).at[target].set(weighted)
    )
    arrived = lax.all_to_all(
        send_rows.reshape(experts, capacity, feature_width),
        "expert",
        split_axis=0,
        concat_axis=0,
        tiled=True,
    ).reshape(-1, feature_width)
    arrived_grad = lax.all_to_all(
        send_grad.reshape(experts, capacity, feature_width),
        "expert",
        split_axis=0,
        concat_axis=0,
        tiled=True,
    ).reshape(-1, feature_width)
    weight_gate = w_gate[0, 0]
    weight_up = w_up[0, 0]
    weight_down = w_down[0, 0]
    gate_pre, up_pre, sigmoid_gate, activation, produced = expert_forward(
        arrived, weight_gate, weight_up, weight_down
    )
    returned = lax.all_to_all(
        produced.reshape(experts, capacity, feature_width),
        "expert",
        split_axis=0,
        concat_axis=0,
        tiled=True,
    ).reshape(-1, feature_width)
    picked = returned[target].astype(jnp.float32) * gate_share.reshape(-1)[:, None]
    layer_out = jnp.sum(picked.reshape(tok_rows, top_count, feature_width), axis=1).astype(
        jnp.bfloat16
    )
    rows_back, grad_gate, grad_up, grad_down = expert_backward(
        arrived,
        arrived_grad,
        weight_gate,
        weight_up,
        weight_down,
        gate_pre,
        up_pre,
        sigmoid_gate,
        activation,
    )
    returned_grad = lax.all_to_all(
        rows_back.reshape(experts, capacity, feature_width),
        "expert",
        split_axis=0,
        concat_axis=0,
        tiled=True,
    ).reshape(-1, feature_width)
    picked_back = returned_grad[target].astype(jnp.float32)
    token_grad = jnp.sum(picked_back.reshape(tok_rows, top_count, feature_width), axis=1).astype(
        jnp.bfloat16
    )
    gate_new, gate_moment = momentum_step(weight_gate, mom_gate[0, 0], grad_gate)
    up_new, up_moment = momentum_step(weight_up, mom_up[0, 0], grad_up)
    down_new, down_moment = momentum_step(weight_down, mom_down[0, 0], grad_down)
    hidden_width = weight_gate.shape[1]
    stacked = jnp.stack([gate_new, up_new, down_new.reshape(feature_width, hidden_width)], axis=0)
    bit_count = lax.axis_size("replica").bit_length() - 1
    bit_now = gossip_round[0] % bit_count
    partner = stacked
    for bit_index in range(bit_count):
        swapped = partner_2(stacked, "replica", bit_index)
        partner = jnp.where(bit_now == bit_index, swapped, partner)
    averaged = ((stacked.astype(jnp.float32) + partner.astype(jnp.float32)) * 0.5).astype(
        jnp.bfloat16
    )
    new_gate = averaged[0][None, None]
    new_up = averaged[1][None, None]
    new_down = averaged[2].reshape(hidden_width, feature_width)[None, None]
    return (
        layer_out,
        token_grad,
        new_gate,
        new_up,
        new_down,
        gate_moment[None, None],
        up_moment[None, None],
        down_moment[None, None],
    )


def ring_order(experts):
    return list(range(0, experts, 2)) + list(range(experts - 1, 0, -2))


def ring_hop(value, experts, step):
    order = ring_order(experts)
    pairs = [(order[i], order[(i + step) % experts]) for i in range(experts)]
    return lax.ppermute(value, "expert", pairs)


def after(value, *others):
    return lax.optimization_barrier((value,) + others)[0]


def ring_gather_pair(first, second, experts):
    last = experts // 2
    blocks = [[None] * experts, [None] * experts]
    moving = [(first, first), (second, second)]
    for which, own in enumerate((first, second)):
        blocks[which][0] = own
    for step in range(1, last):
        for which in range(2):
            behind, ahead = moving[which]
            behind = ring_hop(behind, experts, 1)
            ahead = ring_hop(ahead, experts, -1)
            moving[which] = after((behind, ahead), moving[0]) if which else (behind, ahead)
            moving[which] = lax.optimization_barrier(moving[which])
            blocks[which][experts - step], blocks[which][step] = moving[which]
    blocks[0][last] = ring_hop(moving[0][0], experts, 1)
    blocks[1][last] = ring_hop(moving[1][1], experts, -1)
    return blocks


def ring_scatter(parts, experts, gate):
    half = parts[0].shape[0] // 2
    last = experts // 2
    f32 = jnp.float32
    forward = ring_hop(parts[last][:half].astype(jnp.bfloat16), experts, 1)
    backward = ring_hop(parts[last][half:].astype(jnp.bfloat16), experts, -1)
    for step in range(last - 1, 0, -1):
        mine_f, mine_b = parts[step], parts[experts - step]
        if step == last - 1:
            add_f = jnp.concatenate([mine_f[:half] + forward.astype(f32), mine_f[half:]], axis=0)
            add_b = jnp.concatenate([mine_b[:half], mine_b[half:] + backward.astype(f32)], axis=0)
        else:
            add_f = mine_f + forward.astype(f32)
            add_b = mine_b + backward.astype(f32)
        add_f, add_b = add_f.astype(jnp.bfloat16), add_b.astype(jnp.bfloat16)
        add_f, add_b = after((add_f, add_b), gate(step, forward, backward))
        forward = ring_hop(add_f, experts, 1)
        backward = ring_hop(add_b, experts, -1)
    total = parts[0] + forward.astype(f32) + backward.astype(f32)
    return total.astype(jnp.bfloat16)


def own_shares(routing, gate_share, experts, marks):
    me = lax.axis_index("expert")
    ids = jnp.arange(experts, dtype=jnp.int32)
    order = ring_order(experts)
    away = [[order[(order.index(e) + j) % experts] ^ e for j in range(experts)] for e in range(experts)]
    names = routing[:, None, :] == ids[None, :, None]
    table = jnp.sum(jnp.where(names, gate_share[:, None, :], 0.0), axis=2).T
    table = table[None]
    bit = 1
    turn = 0
    while bit < experts:
        pairs = [(e, e ^ bit) for e in range(experts)]
        other = lax.ppermute(table, "expert", pairs)
        table = jnp.concatenate([table, after(other, marks[turn % len(marks)])], axis=0)
        bit = bit * 2
        turn = turn + 1
    mine = jnp.sum(jnp.where((ids == me)[None, :, None], table, 0.0), axis=1)
    picks = jnp.array(away, dtype=jnp.int32)[me]
    rows = jnp.sum(jnp.where(picks[:, None, None] == ids[None, :, None], mine[None], 0.0), axis=1)
    return [rows[j][:, None] for j in range(experts)]


def per_device_dense(
    tokens,
    routing,
    gate_scores,
    cotangent,
    w_gate,
    w_up,
    w_down,
    mom_gate,
    mom_up,
    mom_down,
    gossip_round,
):
    tok_rows, feature_width = tokens.shape
    experts = lax.axis_size("expert")
    weight_gate = w_gate[0, 0]
    weight_up = w_up[0, 0]
    weight_down = w_down[0, 0]
    hidden_width = weight_gate.shape[1]
    scale_in = feature_width ** (-0.5)
    scale_hidden = hidden_width ** (-0.5)
    inner_dims = (((1,), (1,)), ((), ()))
    outer_dims = (((0,), (0,)), ((), ()))
    gate_share = gate_scores / jnp.sum(gate_scores, axis=1, keepdims=True)
    tok_blocks, cot_blocks = ring_gather_pair(tokens, cotangent, experts)
    marks = (cot_blocks[1], tok_blocks[min(2, experts // 2)], tok_blocks[experts // 2 - 1])
    share_blocks = own_shares(routing, gate_share, experts, marks)
    weight_both = jnp.concatenate([weight_gate, weight_up], axis=1)
    mom_both = jnp.concatenate([mom_gate[0, 0], mom_up[0, 0]], axis=1)

    arrival = [0]
    for step in range(1, experts // 2):
        arrival = arrival + [step, experts - step]
    arrival.append(experts // 2)

    acts, gate_grads, up_grads = [], [], []
    for place in arrival:
        block, cot, share = tok_blocks[place], cot_blocks[place], share_blocks[place]
        both_pre = jnp.dot(block, weight_both, preferred_element_type=jnp.float32) * scale_in
        gate_pre = both_pre[:, :hidden_width]
        up_pre = both_pre[:, hidden_width:]
        sigmoid_gate = jax.nn.sigmoid(gate_pre)
        acts.append((gate_pre * sigmoid_gate * up_pre * share).astype(jnp.bfloat16))
        grad_act = lax.dot_general(
            cot, weight_down, inner_dims, preferred_element_type=jnp.float32
        ) * (share * scale_hidden)
        gate_grads.append(
            (grad_act * up_pre * sigmoid_gate * (1.0 + gate_pre * (1.0 - sigmoid_gate))).astype(
                jnp.bfloat16
            )
        )
        up_grads.append((grad_act * gate_pre * sigmoid_gate).astype(jnp.bfloat16))
    rows_in = jnp.concatenate([tok_blocks[place] for place in arrival], axis=0)
    rows_cot = jnp.concatenate([cot_blocks[place] for place in arrival], axis=0)
    activation = jnp.concatenate(acts, axis=0)
    both_grads = [jnp.concatenate(pair, axis=1) for pair in zip(gate_grads, up_grads)]
    grad_both_pre = jnp.concatenate(both_grads, axis=0)

    bit_count = lax.axis_size("replica").bit_length() - 1
    bit_now = gossip_round[0] % bit_count

    def swap(local, bit_index, *others):
        return partner_2(after(local, *others) if others else local, "replica", bit_index)

    def mean(one, other):
        total = one.astype(jnp.float32) + other.astype(jnp.float32)
        return (total * 0.5).astype(jnp.bfloat16)

    def with_near(local, swapped):
        result = local
        for bit_index, value in enumerate(swapped):
            result = jnp.where(bit_now == bit_index, mean(local, value), result)
        return lax.optimization_barrier(result)

    def with_far(base, value):
        return jnp.where(bit_now == bit_count - 1, mean(base, value), base)

    def averaged(local, swapped):
        return with_far(with_near(local, swapped[:-1]), swapped[-1])

    grad_down = (
        lax.dot_general(activation, rows_cot, outer_dims, preferred_element_type=jnp.float32)
        * scale_hidden
    )
    down_new, down_moment = momentum_step(weight_down, mom_down[0, 0], grad_down)
    out_parts = [None] * experts
    back_parts = [None] * experts
    for place, act, both_grad in zip(arrival, acts, both_grads):
        act, both_grad = after((act, both_grad), down_new)
        out_parts[place] = (
            jnp.dot(act, weight_down, preferred_element_type=jnp.float32) * scale_hidden
        )
        back_parts[place] = (
            lax.dot_general(both_grad, weight_both, inner_dims, preferred_element_type=jnp.float32)
            * scale_in
        )
    out_parts = [lax.optimization_barrier(part) for part in out_parts]
    back_parts = [lax.optimization_barrier(part) for part in back_parts]
    first = experts // 2
    grad_both_pre = after(grad_both_pre, out_parts[first], back_parts[first])
    grad_both = (
        lax.dot_general(rows_in, grad_both_pre, outer_dims, preferred_element_type=jnp.float32)
        * scale_in
    )
    both_new, both_moment = momentum_step(weight_both, mom_both, grad_both)
    gate_moment = both_moment[:, :hidden_width]
    up_moment = both_moment[:, hidden_width:]

    far = bit_count - 1
    down_far = swap(down_new, far)
    both_far = swap(both_new, far)
    down_near = [swap(down_new, bit_index) for bit_index in range(far)]
    both_near = [swap(both_new, bit_index, down_far) for bit_index in range(far)]

    def gate(step, forward, backward):
        if step == 3:
            return (both_new, down_near)
        if step == 2:
            return (down_far,)
        return ()

    parts = [
        jnp.concatenate([out_part, back_part], axis=0)
        for out_part, back_part in zip(out_parts, back_parts)
    ]
    returns = ring_scatter(parts, experts, gate)
    layer_out, token_grad = returns[:tok_rows], returns[tok_rows:]

    new_down = averaged(down_new, down_near + [down_far])
    both_base = with_near(both_new, both_near)
    new_gate = with_far(both_base[:, :hidden_width], both_far[:, :hidden_width])
    new_up = with_far(both_base[:, hidden_width:], both_far[:, hidden_width:])
    return (
        layer_out,
        token_grad,
        new_gate[None, None],
        new_up[None, None],
        new_down[None, None],
        gate_moment[None, None],
        up_moment[None, None],
        down_moment[None, None],
    )


def per_device(tokens, routing, *others):
    if routing.shape[1] == lax.axis_size("expert"):
        return per_device_dense(tokens, routing, *others)
    return per_device_routed(tokens, routing, *others)


def solution(mesh):
    placed = (
        P(("replica", "expert"), None),
        P(("replica", "expert"), None),
        P(("replica", "expert"), None),
        P(("replica", "expert"), None),
        P("replica", "expert", None, None),
        P("replica", "expert", None, None),
        P("replica", "expert", None, None),
        P("replica", "expert", None, None),
        P("replica", "expert", None, None),
        P("replica", "expert", None, None),
        P("expert"),
    )
    return jax.shard_map(
        per_device,
        mesh=mesh,
        in_specs=placed,
        out_specs=(
            P(("replica", "expert"), None),
            P(("replica", "expert"), None),
            P("replica", "expert", None, None),
            P("replica", "expert", None, None),
            P("replica", "expert", None, None),
            P("replica", "expert", None, None),
            P("replica", "expert", None, None),
            P("replica", "expert", None, None),
        ),
        check_vma=False,
    )
```

```python
import jax
import jax.numpy as jnp
from jax import lax
from jax.sharding import PartitionSpec as P

momentum_beta = 0.9
learn_rate = 0.1


def partner_2(value, axis, stride):
    mask = 2**stride
    pairs = [(source, source ^ mask) for source in range(lax.axis_size(axis))]
    return lax.ppermute(value, axis, pairs)


def expert_forward(rows_in, weight_gate, weight_up, weight_down):
    scale_in = rows_in.shape[1] ** (-0.5)
    scale_hidden = weight_gate.shape[1] ** (-0.5)
    gate_pre = jnp.dot(rows_in, weight_gate, preferred_element_type=jnp.float32) * scale_in
    up_pre = jnp.dot(rows_in, weight_up, preferred_element_type=jnp.float32) * scale_in
    sigmoid_gate = jax.nn.sigmoid(gate_pre)
    activation = (gate_pre * sigmoid_gate * up_pre).astype(jnp.bfloat16)
    produced = (
        jnp.dot(activation, weight_down, preferred_element_type=jnp.float32) * scale_hidden
    ).astype(jnp.bfloat16)
    return (gate_pre, up_pre, sigmoid_gate, activation, produced)


def expert_backward(
    rows_in,
    rows_grad,
    weight_gate,
    weight_up,
    weight_down,
    gate_pre,
    up_pre,
    sigmoid_gate,
    activation,
):
    scale_in = rows_in.shape[1] ** (-0.5)
    scale_hidden = weight_gate.shape[1] ** (-0.5)
    inner_dims = (((1,), (1,)), ((), ()))
    outer_dims = (((0,), (0,)), ((), ()))
    grad_act = (
        lax.dot_general(rows_grad, weight_down, inner_dims, preferred_element_type=jnp.float32)
        * scale_hidden
    )
    grad_gate_pre = (
        grad_act * up_pre * sigmoid_gate * (1.0 + gate_pre * (1.0 - sigmoid_gate))
    ).astype(jnp.bfloat16)
    grad_up_pre = (grad_act * gate_pre * sigmoid_gate).astype(jnp.bfloat16)
    grad_down = (
        lax.dot_general(activation, rows_grad, outer_dims, preferred_element_type=jnp.float32)
        * scale_hidden
    )
    grad_gate = (
        lax.dot_general(rows_in, grad_gate_pre, outer_dims, preferred_element_type=jnp.float32)
        * scale_in
    )
    grad_up = (
        lax.dot_general(rows_in, grad_up_pre, outer_dims, preferred_element_type=jnp.float32)
        * scale_in
    )
    back_sum = lax.dot_general(
        grad_gate_pre, weight_gate, inner_dims, preferred_element_type=jnp.float32
    )
    back_sum = back_sum + lax.dot_general(
        grad_up_pre, weight_up, inner_dims, preferred_element_type=jnp.float32
    )
    rows_back = (back_sum * scale_in).astype(jnp.bfloat16)
    return (rows_back, grad_gate, grad_up, grad_down)


def momentum_step(weight, moment, gradient):
    moment_new = momentum_beta * moment.astype(jnp.float32) + gradient
    weight_new = (weight.astype(jnp.float32) - learn_rate * moment_new).astype(jnp.bfloat16)
    return (weight_new, moment_new.astype(jnp.bfloat16))


def per_device_routed(
    tokens,
    routing,
    gate_scores,
    cotangent,
    w_gate,
    w_up,
    w_down,
    mom_gate,
    mom_up,
    mom_down,
    gossip_round,
):
    tok_rows, feature_width = tokens.shape
    top_count = routing.shape[1]
    experts = lax.axis_size("expert")
    capacity = max(2, min(tok_rows, tok_rows * top_count // experts + 8))
    gate_share = gate_scores / jnp.sum(gate_scores, axis=1, keepdims=True)
    expert_ids = routing.reshape(-1)
    member = (expert_ids[:, None] == jnp.arange(experts, dtype=jnp.int32)[None, :]).astype(
        jnp.int32
    )
    earlier = jnp.sum((jnp.cumsum(member, axis=0) - member) * member, axis=1)
    target = expert_ids * capacity + earlier
    source = jnp.arange(expert_ids.shape[0], dtype=jnp.int32) // top_count
    send_rows = (
        jnp.zeros((experts * capacity, feature_width), jnp.bfloat16).at[target].set(tokens[source])
    )
    weighted = (gate_share.reshape(-1)[:, None] * cotangent[source].astype(jnp.float32)).astype(
        jnp.bfloat16
    )
    send_grad = (
        jnp.zeros((experts * capacity, feature_width), jnp.bfloat16).at[target].set(weighted)
    )
    arrived = lax.all_to_all(
        send_rows.reshape(experts, capacity, feature_width),
        "expert",
        split_axis=0,
        concat_axis=0,
        tiled=True,
    ).reshape(-1, feature_width)
    arrived_grad = lax.all_to_all(
        send_grad.reshape(experts, capacity, feature_width),
        "expert",
        split_axis=0,
        concat_axis=0,
        tiled=True,
    ).reshape(-1, feature_width)
    weight_gate = w_gate[0, 0]
    weight_up = w_up[0, 0]
    weight_down = w_down[0, 0]
    gate_pre, up_pre, sigmoid_gate, activation, produced = expert_forward(
        arrived, weight_gate, weight_up, weight_down
    )
    returned = lax.all_to_all(
        produced.reshape(experts, capacity, feature_width),
        "expert",
        split_axis=0,
        concat_axis=0,
        tiled=True,
    ).reshape(-1, feature_width)
    picked = returned[target].astype(jnp.float32) * gate_share.reshape(-1)[:, None]
    layer_out = jnp.sum(picked.reshape(tok_rows, top_count, feature_width), axis=1).astype(
        jnp.bfloat16
    )
    rows_back, grad_gate, grad_up, grad_down = expert_backward(
        arrived,
        arrived_grad,
        weight_gate,
        weight_up,
        weight_down,
        gate_pre,
        up_pre,
        sigmoid_gate,
        activation,
    )
    returned_grad = lax.all_to_all(
        rows_back.reshape(experts, capacity, feature_width),
        "expert",
        split_axis=0,
        concat_axis=0,
        tiled=True,
    ).reshape(-1, feature_width)
    picked_back = returned_grad[target].astype(jnp.float32)
    token_grad = jnp.sum(picked_back.reshape(tok_rows, top_count, feature_width), axis=1).astype(
        jnp.bfloat16
    )
    gate_new, gate_moment = momentum_step(weight_gate, mom_gate[0, 0], grad_gate)
    up_new, up_moment = momentum_step(weight_up, mom_up[0, 0], grad_up)
    down_new, down_moment = momentum_step(weight_down, mom_down[0, 0], grad_down)
    hidden_width = weight_gate.shape[1]
    stacked = jnp.stack([gate_new, up_new, down_new.reshape(feature_width, hidden_width)], axis=0)
    bit_count = lax.axis_size("replica").bit_length() - 1
    bit_now = gossip_round[0] % bit_count
    partner = stacked
    for bit_index in range(bit_count):
        swapped = partner_2(stacked, "replica", bit_index)
        partner = jnp.where(bit_now == bit_index, swapped, partner)
    averaged = ((stacked.astype(jnp.float32) + partner.astype(jnp.float32)) * 0.5).astype(
        jnp.bfloat16
    )
    new_gate = averaged[0][None, None]
    new_up = averaged[1][None, None]
    new_down = averaged[2].reshape(hidden_width, feature_width)[None, None]
    return (
        layer_out,
        token_grad,
        new_gate,
        new_up,
        new_down,
        gate_moment[None, None],
        up_moment[None, None],
        down_moment[None, None],
    )


def ring_order(experts):
    return list(range(0, experts, 2)) + list(range(experts - 1, 0, -2))


def ring_hop(value, experts, step):
    order = ring_order(experts)
    pairs = [(order[i], order[(i + step) % experts]) for i in range(experts)]
    return lax.ppermute(value, "expert", pairs)


def after(value, *others):
    return lax.optimization_barrier((value,) + others)[0]


def ring_gather_pair(first, second, experts):
    last = experts // 2
    blocks = [[None] * experts, [None] * experts]
    moving = [(first, first), (second, second)]
    for which, own in enumerate((first, second)):
        blocks[which][0] = own
    for step in range(1, last):
        for which in range(2):
            behind, ahead = moving[which]
            behind = ring_hop(behind, experts, 1)
            ahead = ring_hop(ahead, experts, -1)
            moving[which] = after((behind, ahead), moving[0]) if which else (behind, ahead)
            moving[which] = lax.optimization_barrier(moving[which])
            blocks[which][experts - step], blocks[which][step] = moving[which]
    blocks[0][last] = ring_hop(moving[0][0], experts, 1)
    blocks[1][last] = ring_hop(moving[1][1], experts, -1)
    return blocks


def ring_scatter(parts, experts, gate):
    half = parts[0].shape[0] // 2
    last = experts // 2
    f32 = jnp.float32
    forward = ring_hop(parts[last][:half].astype(jnp.bfloat16), experts, 1)
    backward = ring_hop(parts[last][half:].astype(jnp.bfloat16), experts, -1)
    for step in range(last - 1, 0, -1):
        mine_f, mine_b = parts[step], parts[experts - step]
        if step == last - 1:
            add_f = jnp.concatenate([mine_f[:half] + forward.astype(f32), mine_f[half:]], axis=0)
            add_b = jnp.concatenate([mine_b[:half], mine_b[half:] + backward.astype(f32)], axis=0)
        else:
            add_f = mine_f + forward.astype(f32)
            add_b = mine_b + backward.astype(f32)
        add_f, add_b = add_f.astype(jnp.bfloat16), add_b.astype(jnp.bfloat16)
        add_f, add_b = after((add_f, add_b), gate(step, forward, backward))
        forward = ring_hop(add_f, experts, 1)
        backward = ring_hop(add_b, experts, -1)
    total = parts[0] + forward.astype(f32) + backward.astype(f32)
    return total.astype(jnp.bfloat16)


def own_shares(routing, gate_share, experts, marks):
    me = lax.axis_index("expert")
    ids = jnp.arange(experts, dtype=jnp.int32)
    order = ring_order(experts)
    away = [[order[(order.index(e) + j) % experts] ^ e for j in range(experts)] for e in range(experts)]
    names = routing[:, None, :] == ids[None, :, None]
    table = jnp.sum(jnp.where(names, gate_share[:, None, :], 0.0), axis=2).T
    table = table[None]
    bit = 1
    turn = 0
    while bit < experts:
        pairs = [(e, e ^ bit) for e in range(experts)]
        other = lax.ppermute(table, "expert", pairs)
        table = jnp.concatenate([table, after(other, marks[turn % len(marks)])], axis=0)
        bit = bit * 2
        turn = turn + 1
    mine = jnp.sum(jnp.where((ids == me)[None, :, None], table, 0.0), axis=1)
    picks = jnp.array(away, dtype=jnp.int32)[me]
    rows = jnp.sum(jnp.where(picks[:, None, None] == ids[None, :, None], mine[None], 0.0), axis=1)
    return [rows[j][:, None] for j in range(experts)]


def per_device_dense(
    tokens,
    routing,
    gate_scores,
    cotangent,
    w_gate,
    w_up,
    w_down,
    mom_gate,
    mom_up,
    mom_down,
    gossip_round,
):
    tok_rows, feature_width = tokens.shape
    experts = lax.axis_size("expert")
    weight_gate = w_gate[0, 0]
    weight_up = w_up[0, 0]
    weight_down = w_down[0, 0]
    hidden_width = weight_gate.shape[1]
    scale_in = feature_width ** (-0.5)
    scale_hidden = hidden_width ** (-0.5)
    inner_dims = (((1,), (1,)), ((), ()))
    outer_dims = (((0,), (0,)), ((), ()))
    gate_share = gate_scores / jnp.sum(gate_scores, axis=1, keepdims=True)
    tok_blocks, cot_blocks = ring_gather_pair(tokens, cotangent, experts)
    marks = (tok_blocks[1], cot_blocks[1], tok_blocks[min(2, experts // 2)])
    share_blocks = own_shares(routing, gate_share, experts, marks)
    weight_both = jnp.concatenate([weight_gate, weight_up], axis=1)
    mom_both = jnp.concatenate([mom_gate[0, 0], mom_up[0, 0]], axis=1)

    arrival = [0]
    for step in range(1, experts // 2):
        arrival = arrival + [step, experts - step]
    arrival.append(experts // 2)

    groups = [[0]] + [[step, experts - step] for step in range(1, experts // 2)] + [[experts // 2]]

    def rows_of(blocks, group):
        return jnp.concatenate([blocks[place] for place in group], axis=0)

    acts, both_grads = {}, {}
    for group in groups:
        block, cot = rows_of(tok_blocks, group), rows_of(cot_blocks, group)
        share = rows_of(share_blocks, group)
        both_pre = jnp.dot(block, weight_both, preferred_element_type=jnp.float32) * scale_in
        gate_pre = both_pre[:, :hidden_width]
        up_pre = both_pre[:, hidden_width:]
        sigmoid_gate = jax.nn.sigmoid(gate_pre)
        act = (gate_pre * sigmoid_gate * up_pre * share).astype(jnp.bfloat16)
        grad_act = lax.dot_general(
            cot, weight_down, inner_dims, preferred_element_type=jnp.float32
        ) * (share * scale_hidden)
        slope = sigmoid_gate * (1.0 + gate_pre * (1.0 - sigmoid_gate))
        gate_grad = (grad_act * up_pre * slope).astype(jnp.bfloat16)
        up_grad = (grad_act * gate_pre * sigmoid_gate).astype(jnp.bfloat16)
        both_grad = jnp.concatenate([gate_grad, up_grad], axis=1)
        for at, place in enumerate(group):
            acts[place] = act[at * tok_rows : (at + 1) * tok_rows]
            both_grads[place] = both_grad[at * tok_rows : (at + 1) * tok_rows]
    rows_in = jnp.concatenate([tok_blocks[place] for place in arrival], axis=0)
    rows_cot = jnp.concatenate([cot_blocks[place] for place in arrival], axis=0)
    activation = jnp.concatenate([acts[place] for place in arrival], axis=0)
    grad_both_pre = jnp.concatenate([both_grads[place] for place in arrival], axis=0)

    bit_count = lax.axis_size("replica").bit_length() - 1
    bit_now = gossip_round[0] % bit_count

    def swap(local, bit_index, *others):
        return partner_2(after(local, *others) if others else local, "replica", bit_index)

    def mean(one, other):
        total = one.astype(jnp.float32) + other.astype(jnp.float32)
        return (total * 0.5).astype(jnp.bfloat16)

    def with_near(local, swapped):
        result = local
        for bit_index, value in enumerate(swapped):
            result = jnp.where(bit_now == bit_index, mean(local, value), result)
        return lax.optimization_barrier(result)

    def with_far(base, value):
        return jnp.where(bit_now == bit_count - 1, mean(base, value), base)

    def averaged(local, swapped):
        return with_far(with_near(local, swapped[:-1]), swapped[-1])

    grad_down = (
        lax.dot_general(activation, rows_cot, outer_dims, preferred_element_type=jnp.float32)
        * scale_hidden
    )
    down_new, down_moment = momentum_step(weight_down, mom_down[0, 0], grad_down)
    out_parts = [None] * experts
    back_parts = [None] * experts
    for place in arrival:
        act, both_grad = after((acts[place], both_grads[place]), down_new)
        out_parts[place] = (
            jnp.dot(act, weight_down, preferred_element_type=jnp.float32) * scale_hidden
        )
        back_parts[place] = (
            lax.dot_general(both_grad, weight_both, inner_dims, preferred_element_type=jnp.float32)
            * scale_in
        )
    out_parts = [lax.optimization_barrier(part) for part in out_parts]
    back_parts = [lax.optimization_barrier(part) for part in back_parts]
    first = experts // 2
    grad_both_pre = after(grad_both_pre, out_parts[first], back_parts[first])
    grad_both = (
        lax.dot_general(rows_in, grad_both_pre, outer_dims, preferred_element_type=jnp.float32)
        * scale_in
    )
    both_new, both_moment = momentum_step(weight_both, mom_both, grad_both)
    gate_moment = both_moment[:, :hidden_width]
    up_moment = both_moment[:, hidden_width:]

    far = bit_count - 1
    down_far = swap(down_new, far)
    both_far = swap(both_new, far)
    down_near = [swap(down_new, bit_index) for bit_index in range(far)]
    both_near = [swap(both_new, bit_index, down_far) for bit_index in range(far)]

    def gate(step, forward, backward):
        if step == 3:
            return (both_new, down_near)
        if step == 2:
            return (down_far,)
        return ()

    parts = [
        jnp.concatenate([out_part, back_part], axis=0)
        for out_part, back_part in zip(out_parts, back_parts)
    ]
    returns = ring_scatter(parts, experts, gate)
    layer_out, token_grad = returns[:tok_rows], returns[tok_rows:]

    new_down = averaged(down_new, down_near + [down_far])
    both_base = with_near(both_new, both_near)
    new_gate = with_far(both_base[:, :hidden_width], both_far[:, :hidden_width])
    new_up = with_far(both_base[:, hidden_width:], both_far[:, hidden_width:])
    return (
        layer_out,
        token_grad,
        new_gate[None, None],
        new_up[None, None],
        new_down[None, None],
        gate_moment[None, None],
        up_moment[None, None],
        down_moment[None, None],
    )


def per_device(tokens, routing, *others):
    if routing.shape[1] == lax.axis_size("expert"):
        return per_device_dense(tokens, routing, *others)
    return per_device_routed(tokens, routing, *others)


def solution(mesh):
    placed = (
        P(("replica", "expert"), None),
        P(("replica", "expert"), None),
        P(("replica", "expert"), None),
        P(("replica", "expert"), None),
        P("replica", "expert", None, None),
        P("replica", "expert", None, None),
        P("replica", "expert", None, None),
        P("replica", "expert", None, None),
        P("replica", "expert", None, None),
        P("replica", "expert", None, None),
        P("expert"),
    )
    return jax.shard_map(
        per_device,
        mesh=mesh,
        in_specs=placed,
        out_specs=(
            P(("replica", "expert"), None),
            P(("replica", "expert"), None),
            P("replica", "expert", None, None),
            P("replica", "expert", None, None),
            P("replica", "expert", None, None),
            P("replica", "expert", None, None),
            P("replica", "expert", None, None),
            P("replica", "expert", None, None),
        ),
        check_vma=False,
    )
```

```python
import jax
import jax.numpy as jnp
from jax import lax
from jax.sharding import PartitionSpec as P

momentum_beta = 0.9
learn_rate = 0.1


def partner_2(value, axis, stride):
    mask = 2**stride
    pairs = [(source, source ^ mask) for source in range(lax.axis_size(axis))]
    return lax.ppermute(value, axis, pairs)


def expert_forward(rows_in, weight_gate, weight_up, weight_down):
    scale_in = rows_in.shape[1] ** (-0.5)
    scale_hidden = weight_gate.shape[1] ** (-0.5)
    gate_pre = jnp.dot(rows_in, weight_gate, preferred_element_type=jnp.float32) * scale_in
    up_pre = jnp.dot(rows_in, weight_up, preferred_element_type=jnp.float32) * scale_in
    sigmoid_gate = jax.nn.sigmoid(gate_pre)
    activation = (gate_pre * sigmoid_gate * up_pre).astype(jnp.bfloat16)
    produced = (
        jnp.dot(activation, weight_down, preferred_element_type=jnp.float32) * scale_hidden
    ).astype(jnp.bfloat16)
    return (gate_pre, up_pre, sigmoid_gate, activation, produced)


def expert_backward(
    rows_in,
    rows_grad,
    weight_gate,
    weight_up,
    weight_down,
    gate_pre,
    up_pre,
    sigmoid_gate,
    activation,
):
    scale_in = rows_in.shape[1] ** (-0.5)
    scale_hidden = weight_gate.shape[1] ** (-0.5)
    inner_dims = (((1,), (1,)), ((), ()))
    outer_dims = (((0,), (0,)), ((), ()))
    grad_act = (
        lax.dot_general(rows_grad, weight_down, inner_dims, preferred_element_type=jnp.float32)
        * scale_hidden
    )
    grad_gate_pre = (
        grad_act * up_pre * sigmoid_gate * (1.0 + gate_pre * (1.0 - sigmoid_gate))
    ).astype(jnp.bfloat16)
    grad_up_pre = (grad_act * gate_pre * sigmoid_gate).astype(jnp.bfloat16)
    grad_down = (
        lax.dot_general(activation, rows_grad, outer_dims, preferred_element_type=jnp.float32)
        * scale_hidden
    )
    grad_gate = (
        lax.dot_general(rows_in, grad_gate_pre, outer_dims, preferred_element_type=jnp.float32)
        * scale_in
    )
    grad_up = (
        lax.dot_general(rows_in, grad_up_pre, outer_dims, preferred_element_type=jnp.float32)
        * scale_in
    )
    back_sum = lax.dot_general(
        grad_gate_pre, weight_gate, inner_dims, preferred_element_type=jnp.float32
    )
    back_sum = back_sum + lax.dot_general(
        grad_up_pre, weight_up, inner_dims, preferred_element_type=jnp.float32
    )
    rows_back = (back_sum * scale_in).astype(jnp.bfloat16)
    return (rows_back, grad_gate, grad_up, grad_down)


def momentum_step(weight, moment, gradient):
    moment_new = momentum_beta * moment.astype(jnp.float32) + gradient
    weight_new = (weight.astype(jnp.float32) - learn_rate * moment_new).astype(jnp.bfloat16)
    return (weight_new, moment_new.astype(jnp.bfloat16))


def per_device_routed(
    tokens,
    routing,
    gate_scores,
    cotangent,
    w_gate,
    w_up,
    w_down,
    mom_gate,
    mom_up,
    mom_down,
    gossip_round,
):
    tok_rows, feature_width = tokens.shape
    top_count = routing.shape[1]
    experts = lax.axis_size("expert")
    capacity = max(2, min(tok_rows, tok_rows * top_count // experts + 8))
    gate_share = gate_scores / jnp.sum(gate_scores, axis=1, keepdims=True)
    expert_ids = routing.reshape(-1)
    member = (expert_ids[:, None] == jnp.arange(experts, dtype=jnp.int32)[None, :]).astype(
        jnp.int32
    )
    earlier = jnp.sum((jnp.cumsum(member, axis=0) - member) * member, axis=1)
    target = expert_ids * capacity + earlier
    source = jnp.arange(expert_ids.shape[0], dtype=jnp.int32) // top_count
    send_rows = (
        jnp.zeros((experts * capacity, feature_width), jnp.bfloat16).at[target].set(tokens[source])
    )
    weighted = (gate_share.reshape(-1)[:, None] * cotangent[source].astype(jnp.float32)).astype(
        jnp.bfloat16
    )
    send_grad = (
        jnp.zeros((experts * capacity, feature_width), jnp.bfloat16).at[target].set(weighted)
    )
    arrived = lax.all_to_all(
        send_rows.reshape(experts, capacity, feature_width),
        "expert",
        split_axis=0,
        concat_axis=0,
        tiled=True,
    ).reshape(-1, feature_width)
    arrived_grad = lax.all_to_all(
        send_grad.reshape(experts, capacity, feature_width),
        "expert",
        split_axis=0,
        concat_axis=0,
        tiled=True,
    ).reshape(-1, feature_width)
    weight_gate = w_gate[0, 0]
    weight_up = w_up[0, 0]
    weight_down = w_down[0, 0]
    gate_pre, up_pre, sigmoid_gate, activation, produced = expert_forward(
        arrived, weight_gate, weight_up, weight_down
    )
    returned = lax.all_to_all(
        produced.reshape(experts, capacity, feature_width),
        "expert",
        split_axis=0,
        concat_axis=0,
        tiled=True,
    ).reshape(-1, feature_width)
    picked = returned[target].astype(jnp.float32) * gate_share.reshape(-1)[:, None]
    layer_out = jnp.sum(picked.reshape(tok_rows, top_count, feature_width), axis=1).astype(
        jnp.bfloat16
    )
    rows_back, grad_gate, grad_up, grad_down = expert_backward(
        arrived,
        arrived_grad,
        weight_gate,
        weight_up,
        weight_down,
        gate_pre,
        up_pre,
        sigmoid_gate,
        activation,
    )
    returned_grad = lax.all_to_all(
        rows_back.reshape(experts, capacity, feature_width),
        "expert",
        split_axis=0,
        concat_axis=0,
        tiled=True,
    ).reshape(-1, feature_width)
    picked_back = returned_grad[target].astype(jnp.float32)
    token_grad = jnp.sum(picked_back.reshape(tok_rows, top_count, feature_width), axis=1).astype(
        jnp.bfloat16
    )
    gate_new, gate_moment = momentum_step(weight_gate, mom_gate[0, 0], grad_gate)
    up_new, up_moment = momentum_step(weight_up, mom_up[0, 0], grad_up)
    down_new, down_moment = momentum_step(weight_down, mom_down[0, 0], grad_down)
    hidden_width = weight_gate.shape[1]
    stacked = jnp.stack([gate_new, up_new, down_new.reshape(feature_width, hidden_width)], axis=0)
    bit_count = lax.axis_size("replica").bit_length() - 1
    bit_now = gossip_round[0] % bit_count
    partner = stacked
    for bit_index in range(bit_count):
        swapped = partner_2(stacked, "replica", bit_index)
        partner = jnp.where(bit_now == bit_index, swapped, partner)
    averaged = ((stacked.astype(jnp.float32) + partner.astype(jnp.float32)) * 0.5).astype(
        jnp.bfloat16
    )
    new_gate = averaged[0][None, None]
    new_up = averaged[1][None, None]
    new_down = averaged[2].reshape(hidden_width, feature_width)[None, None]
    return (
        layer_out,
        token_grad,
        new_gate,
        new_up,
        new_down,
        gate_moment[None, None],
        up_moment[None, None],
        down_moment[None, None],
    )


def ring_order(experts):
    return list(range(0, experts, 2)) + list(range(experts - 1, 0, -2))


def ring_hop(value, experts, step):
    order = ring_order(experts)
    pairs = [(order[i], order[(i + step) % experts]) for i in range(experts)]
    return lax.ppermute(value, "expert", pairs)


def after(value, *others):
    return lax.optimization_barrier((value,) + others)[0]


def ring_gather_pair(first, second, experts):
    last = experts // 2
    blocks = [[None] * experts, [None] * experts]
    moving = [(first, first), (second, second)]
    for which, own in enumerate((first, second)):
        blocks[which][0] = own
    for step in range(1, last):
        for which in range(2):
            behind, ahead = moving[which]
            behind = ring_hop(behind, experts, 1)
            ahead = ring_hop(ahead, experts, -1)
            moving[which] = after((behind, ahead), moving[0]) if which else (behind, ahead)
            moving[which] = lax.optimization_barrier(moving[which])
            blocks[which][experts - step], blocks[which][step] = moving[which]
    blocks[0][last] = ring_hop(moving[0][0], experts, 1)
    blocks[1][last] = ring_hop(moving[1][1], experts, -1)
    return blocks


def ring_scatter(parts, experts, gate):
    half = parts[0].shape[0] // 2
    last = experts // 2
    f32 = jnp.float32
    forward = ring_hop(parts[last][:half].astype(jnp.bfloat16), experts, 1)
    backward = ring_hop(parts[last][half:].astype(jnp.bfloat16), experts, -1)
    for step in range(last - 1, 0, -1):
        mine_f, mine_b = parts[step], parts[experts - step]
        if step == last - 1:
            add_f = jnp.concatenate([mine_f[:half] + forward.astype(f32), mine_f[half:]], axis=0)
            add_b = jnp.concatenate([mine_b[:half], mine_b[half:] + backward.astype(f32)], axis=0)
        else:
            add_f = mine_f + forward.astype(f32)
            add_b = mine_b + backward.astype(f32)
        add_f, add_b = add_f.astype(jnp.bfloat16), add_b.astype(jnp.bfloat16)
        add_f, add_b = after((add_f, add_b), gate(step, forward, backward))
        forward = ring_hop(add_f, experts, 1)
        backward = ring_hop(add_b, experts, -1)
    total = parts[0] + forward.astype(f32) + backward.astype(f32)
    return total.astype(jnp.bfloat16)


def own_shares(routing, gate_share, experts, marks):
    me = lax.axis_index("expert")
    ids = jnp.arange(experts, dtype=jnp.int32)
    order = ring_order(experts)
    away = [[order[(order.index(e) + j) % experts] ^ e for j in range(experts)] for e in range(experts)]
    names = routing[:, None, :] == ids[None, :, None]
    table = jnp.sum(jnp.where(names, gate_share[:, None, :], 0.0), axis=2).T
    table = table[None]
    bit = 1
    turn = 0
    while bit < experts:
        pairs = [(e, e ^ bit) for e in range(experts)]
        other = lax.ppermute(table, "expert", pairs)
        table = jnp.concatenate([table, after(other, marks[turn % len(marks)])], axis=0)
        bit = bit * 2
        turn = turn + 1
    mine = jnp.sum(jnp.where((ids == me)[None, :, None], table, 0.0), axis=1)
    picks = jnp.array(away, dtype=jnp.int32)[me]
    rows = jnp.sum(jnp.where(picks[:, None, None] == ids[None, :, None], mine[None], 0.0), axis=1)
    return [rows[j][:, None] for j in range(experts)]


def per_device_dense(
    tokens,
    routing,
    gate_scores,
    cotangent,
    w_gate,
    w_up,
    w_down,
    mom_gate,
    mom_up,
    mom_down,
    gossip_round,
):
    tok_rows, feature_width = tokens.shape
    experts = lax.axis_size("expert")
    weight_gate = w_gate[0, 0]
    weight_up = w_up[0, 0]
    weight_down = w_down[0, 0]
    hidden_width = weight_gate.shape[1]
    scale_in = feature_width ** (-0.5)
    scale_hidden = hidden_width ** (-0.5)
    inner_dims = (((1,), (1,)), ((), ()))
    outer_dims = (((0,), (0,)), ((), ()))
    gate_share = gate_scores / jnp.sum(gate_scores, axis=1, keepdims=True)
    tok_blocks, cot_blocks = ring_gather_pair(tokens, cotangent, experts)
    marks = (tok_blocks[1], cot_blocks[1], tok_blocks[min(2, experts // 2)])
    share_blocks = own_shares(routing, gate_share, experts, marks)
    weight_both = jnp.concatenate([weight_gate, weight_up], axis=1)

    arrival = [0]
    for step in range(1, experts // 2):
        arrival = arrival + [step, experts - step]
    arrival.append(experts // 2)

    acts, gate_grads, up_grads = [], [], []
    for place in arrival:
        block, cot, share = tok_blocks[place], cot_blocks[place], share_blocks[place]
        both_pre = jnp.dot(block, weight_both, preferred_element_type=jnp.float32) * scale_in
        gate_pre = both_pre[:, :hidden_width]
        up_pre = both_pre[:, hidden_width:]
        sigmoid_gate = jax.nn.sigmoid(gate_pre)
        acts.append((gate_pre * sigmoid_gate * up_pre * share).astype(jnp.bfloat16))
        grad_act = lax.dot_general(
            cot, weight_down, inner_dims, preferred_element_type=jnp.float32
        ) * (share * scale_hidden)
        gate_grads.append(
            (grad_act * up_pre * sigmoid_gate * (1.0 + gate_pre * (1.0 - sigmoid_gate))).astype(
                jnp.bfloat16
            )
        )
        up_grads.append((grad_act * gate_pre * sigmoid_gate).astype(jnp.bfloat16))
    rows_in = jnp.concatenate([tok_blocks[place] for place in arrival], axis=0)
    rows_cot = jnp.concatenate([cot_blocks[place] for place in arrival], axis=0)
    activation = jnp.concatenate(acts, axis=0)
    both_grads = [jnp.concatenate(pair, axis=1) for pair in zip(gate_grads, up_grads)]
    grad_gate_pre = jnp.concatenate(gate_grads, axis=0)
    grad_up_pre = jnp.concatenate(up_grads, axis=0)

    bit_count = lax.axis_size("replica").bit_length() - 1
    bit_now = gossip_round[0] % bit_count

    def swap(local, bit_index, *others):
        return partner_2(after(local, *others) if others else local, "replica", bit_index)

    def mean(one, other):
        total = one.astype(jnp.float32) + other.astype(jnp.float32)
        return (total * 0.5).astype(jnp.bfloat16)

    def with_near(local, swapped):
        result = local
        for bit_index, value in enumerate(swapped):
            result = jnp.where(bit_now == bit_index, mean(local, value), result)
        return lax.optimization_barrier(result)

    def with_far(base, value):
        return jnp.where(bit_now == bit_count - 1, mean(base, value), base)

    def averaged(local, swapped):
        return with_far(with_near(local, swapped[:-1]), swapped[-1])

    grad_down = (
        lax.dot_general(activation, rows_cot, outer_dims, preferred_element_type=jnp.float32)
        * scale_hidden
    )
    down_new, down_moment = momentum_step(weight_down, mom_down[0, 0], grad_down)
    out_parts = [None] * experts
    back_parts = [None] * experts
    for place, act, both_grad in zip(arrival, acts, both_grads):
        act, both_grad = after((act, both_grad), down_new)
        out_parts[place] = (
            jnp.dot(act, weight_down, preferred_element_type=jnp.float32) * scale_hidden
        )
        back_parts[place] = (
            lax.dot_general(both_grad, weight_both, inner_dims, preferred_element_type=jnp.float32)
            * scale_in
        )
    out_parts = [lax.optimization_barrier(part) for part in out_parts]
    back_parts = [lax.optimization_barrier(part) for part in back_parts]
    first = experts // 2
    grad_gate_pre, grad_up_pre = after(
        (grad_gate_pre, grad_up_pre), out_parts[first], back_parts[first]
    )
    grad_gate = (
        lax.dot_general(rows_in, grad_gate_pre, outer_dims, preferred_element_type=jnp.float32)
        * scale_in
    )
    grad_up = (
        lax.dot_general(rows_in, grad_up_pre, outer_dims, preferred_element_type=jnp.float32)
        * scale_in
    )
    gate_new, gate_moment = momentum_step(weight_gate, mom_gate[0, 0], grad_gate)
    up_new, up_moment = momentum_step(weight_up, mom_up[0, 0], grad_up)
    both_new = jnp.concatenate([gate_new, up_new], axis=0)

    far = bit_count - 1
    down_far = swap(down_new, far)
    both_far = swap(both_new, far)
    down_near = [swap(down_new, bit_index) for bit_index in range(far)]
    both_near = [swap(both_new, bit_index, down_far) for bit_index in range(far)]

    def gate(step, forward, backward):
        if step == 3:
            return (both_new, down_near)
        if step == 2:
            return (down_far,)
        return ()

    parts = [
        jnp.concatenate([out_part, back_part], axis=0)
        for out_part, back_part in zip(out_parts, back_parts)
    ]
    returns = ring_scatter(parts, experts, gate)
    layer_out, token_grad = returns[:tok_rows], returns[tok_rows:]

    new_down = averaged(down_new, down_near + [down_far])
    both_base = with_near(both_new, both_near)
    new_gate = with_far(both_base[:feature_width], both_far[:feature_width])
    new_up = with_far(both_base[feature_width:], both_far[feature_width:])
    return (
        layer_out,
        token_grad,
        new_gate[None, None],
        new_up[None, None],
        new_down[None, None],
        gate_moment[None, None],
        up_moment[None, None],
        down_moment[None, None],
    )


def per_device(tokens, routing, *others):
    if routing.shape[1] == lax.axis_size("expert"):
        return per_device_dense(tokens, routing, *others)
    return per_device_routed(tokens, routing, *others)


def solution(mesh):
    placed = (
        P(("replica", "expert"), None),
        P(("replica", "expert"), None),
        P(("replica", "expert"), None),
        P(("replica", "expert"), None),
        P("replica", "expert", None, None),
        P("replica", "expert", None, None),
        P("replica", "expert", None, None),
        P("replica", "expert", None, None),
        P("replica", "expert", None, None),
        P("replica", "expert", None, None),
        P("expert"),
    )
    return jax.shard_map(
        per_device,
        mesh=mesh,
        in_specs=placed,
        out_specs=(
            P(("replica", "expert"), None),
            P(("replica", "expert"), None),
            P("replica", "expert", None, None),
            P("replica", "expert", None, None),
            P("replica", "expert", None, None),
            P("replica", "expert", None, None),
            P("replica", "expert", None, None),
            P("replica", "expert", None, None),
        ),
        check_vma=False,
    )
```

```python
import jax
import jax.numpy as jnp
from jax import lax
from jax.sharding import PartitionSpec as P

momentum_beta = 0.9
learn_rate = 0.1


def partner_2(value, axis, stride):
    mask = 2**stride
    pairs = [(source, source ^ mask) for source in range(lax.axis_size(axis))]
    return lax.ppermute(value, axis, pairs)


def expert_forward(rows_in, weight_gate, weight_up, weight_down):
    scale_in = rows_in.shape[1] ** (-0.5)
    scale_hidden = weight_gate.shape[1] ** (-0.5)
    gate_pre = jnp.dot(rows_in, weight_gate, preferred_element_type=jnp.float32) * scale_in
    up_pre = jnp.dot(rows_in, weight_up, preferred_element_type=jnp.float32) * scale_in
    sigmoid_gate = jax.nn.sigmoid(gate_pre)
    activation = (gate_pre * sigmoid_gate * up_pre).astype(jnp.bfloat16)
    produced = (
        jnp.dot(activation, weight_down, preferred_element_type=jnp.float32) * scale_hidden
    ).astype(jnp.bfloat16)
    return (gate_pre, up_pre, sigmoid_gate, activation, produced)


def expert_backward(
    rows_in,
    rows_grad,
    weight_gate,
    weight_up,
    weight_down,
    gate_pre,
    up_pre,
    sigmoid_gate,
    activation,
):
    scale_in = rows_in.shape[1] ** (-0.5)
    scale_hidden = weight_gate.shape[1] ** (-0.5)
    inner_dims = (((1,), (1,)), ((), ()))
    outer_dims = (((0,), (0,)), ((), ()))
    grad_act = (
        lax.dot_general(rows_grad, weight_down, inner_dims, preferred_element_type=jnp.float32)
        * scale_hidden
    )
    grad_gate_pre = (
        grad_act * up_pre * sigmoid_gate * (1.0 + gate_pre * (1.0 - sigmoid_gate))
    ).astype(jnp.bfloat16)
    grad_up_pre = (grad_act * gate_pre * sigmoid_gate).astype(jnp.bfloat16)
    grad_down = (
        lax.dot_general(activation, rows_grad, outer_dims, preferred_element_type=jnp.float32)
        * scale_hidden
    )
    grad_gate = (
        lax.dot_general(rows_in, grad_gate_pre, outer_dims, preferred_element_type=jnp.float32)
        * scale_in
    )
    grad_up = (
        lax.dot_general(rows_in, grad_up_pre, outer_dims, preferred_element_type=jnp.float32)
        * scale_in
    )
    back_sum = lax.dot_general(
        grad_gate_pre, weight_gate, inner_dims, preferred_element_type=jnp.float32
    )
    back_sum = back_sum + lax.dot_general(
        grad_up_pre, weight_up, inner_dims, preferred_element_type=jnp.float32
    )
    rows_back = (back_sum * scale_in).astype(jnp.bfloat16)
    return (rows_back, grad_gate, grad_up, grad_down)


def momentum_step(weight, moment, gradient):
    moment_new = momentum_beta * moment.astype(jnp.float32) + gradient
    weight_new = (weight.astype(jnp.float32) - learn_rate * moment_new).astype(jnp.bfloat16)
    return (weight_new, moment_new.astype(jnp.bfloat16))


def per_device_routed(
    tokens,
    routing,
    gate_scores,
    cotangent,
    w_gate,
    w_up,
    w_down,
    mom_gate,
    mom_up,
    mom_down,
    gossip_round,
):
    tok_rows, feature_width = tokens.shape
    top_count = routing.shape[1]
    experts = lax.axis_size("expert")
    capacity = max(2, min(tok_rows, tok_rows * top_count // experts + 8))
    gate_share = gate_scores / jnp.sum(gate_scores, axis=1, keepdims=True)
    expert_ids = routing.reshape(-1)
    member = (expert_ids[:, None] == jnp.arange(experts, dtype=jnp.int32)[None, :]).astype(
        jnp.int32
    )
    earlier = jnp.sum((jnp.cumsum(member, axis=0) - member) * member, axis=1)
    target = expert_ids * capacity + earlier
    source = jnp.arange(expert_ids.shape[0], dtype=jnp.int32) // top_count
    send_rows = (
        jnp.zeros((experts * capacity, feature_width), jnp.bfloat16).at[target].set(tokens[source])
    )
    weighted = (gate_share.reshape(-1)[:, None] * cotangent[source].astype(jnp.float32)).astype(
        jnp.bfloat16
    )
    send_grad = (
        jnp.zeros((experts * capacity, feature_width), jnp.bfloat16).at[target].set(weighted)
    )
    arrived = lax.all_to_all(
        send_rows.reshape(experts, capacity, feature_width),
        "expert",
        split_axis=0,
        concat_axis=0,
        tiled=True,
    ).reshape(-1, feature_width)
    arrived_grad = lax.all_to_all(
        send_grad.reshape(experts, capacity, feature_width),
        "expert",
        split_axis=0,
        concat_axis=0,
        tiled=True,
    ).reshape(-1, feature_width)
    weight_gate = w_gate[0, 0]
    weight_up = w_up[0, 0]
    weight_down = w_down[0, 0]
    gate_pre, up_pre, sigmoid_gate, activation, produced = expert_forward(
        arrived, weight_gate, weight_up, weight_down
    )
    returned = lax.all_to_all(
        produced.reshape(experts, capacity, feature_width),
        "expert",
        split_axis=0,
        concat_axis=0,
        tiled=True,
    ).reshape(-1, feature_width)
    picked = returned[target].astype(jnp.float32) * gate_share.reshape(-1)[:, None]
    layer_out = jnp.sum(picked.reshape(tok_rows, top_count, feature_width), axis=1).astype(
        jnp.bfloat16
    )
    rows_back, grad_gate, grad_up, grad_down = expert_backward(
        arrived,
        arrived_grad,
        weight_gate,
        weight_up,
        weight_down,
        gate_pre,
        up_pre,
        sigmoid_gate,
        activation,
    )
    returned_grad = lax.all_to_all(
        rows_back.reshape(experts, capacity, feature_width),
        "expert",
        split_axis=0,
        concat_axis=0,
        tiled=True,
    ).reshape(-1, feature_width)
    picked_back = returned_grad[target].astype(jnp.float32)
    token_grad = jnp.sum(picked_back.reshape(tok_rows, top_count, feature_width), axis=1).astype(
        jnp.bfloat16
    )
    gate_new, gate_moment = momentum_step(weight_gate, mom_gate[0, 0], grad_gate)
    up_new, up_moment = momentum_step(weight_up, mom_up[0, 0], grad_up)
    down_new, down_moment = momentum_step(weight_down, mom_down[0, 0], grad_down)
    hidden_width = weight_gate.shape[1]
    stacked = jnp.stack([gate_new, up_new, down_new.reshape(feature_width, hidden_width)], axis=0)
    bit_count = lax.axis_size("replica").bit_length() - 1
    bit_now = gossip_round[0] % bit_count
    partner = stacked
    for bit_index in range(bit_count):
        swapped = partner_2(stacked, "replica", bit_index)
        partner = jnp.where(bit_now == bit_index, swapped, partner)
    averaged = ((stacked.astype(jnp.float32) + partner.astype(jnp.float32)) * 0.5).astype(
        jnp.bfloat16
    )
    new_gate = averaged[0][None, None]
    new_up = averaged[1][None, None]
    new_down = averaged[2].reshape(hidden_width, feature_width)[None, None]
    return (
        layer_out,
        token_grad,
        new_gate,
        new_up,
        new_down,
        gate_moment[None, None],
        up_moment[None, None],
        down_moment[None, None],
    )


def ring_order(experts):
    return list(range(0, experts, 2)) + list(range(experts - 1, 0, -2))


def ring_hop(value, experts, step):
    order = ring_order(experts)
    pairs = [(order[i], order[(i + step) % experts]) for i in range(experts)]
    return lax.ppermute(value, "expert", pairs)


def after(value, *others):
    return lax.optimization_barrier((value,) + others)[0]


def ring_gather_pair(first, second, table, experts):
    half = first.shape[0] // 2
    last = experts // 2
    blocks = [[None] * experts, [None] * experts]
    moving = [(first, first), (second, second)]
    table = table[None]
    for which, own in enumerate((first, second)):
        blocks[which][0] = own
    for step in range(1, last):
        swapped = None
        if table.shape[0] < experts:
            bit = table.shape[0]
            pairs = [(e, e ^ bit) for e in range(experts)]
            swapped = lax.ppermute(table, "expert", pairs)
        for which in range(2):
            behind, ahead = moving[which]
            behind = ring_hop(behind, experts, 1)
            ahead = ring_hop(ahead, experts, -1)
            if which == 0:
                moving[0] = lax.optimization_barrier((behind, ahead))
                if swapped is not None:
                    table = jnp.concatenate([table, after(swapped, moving[0])], axis=0)
            else:
                moving[1] = after((behind, ahead), moving[0], table)
            blocks[which][experts - step], blocks[which][step] = moving[which]
    for which in range(2):
        behind, ahead = moving[which]
        top = ring_hop(behind[:half], experts, 1)
        bottom = ring_hop(ahead[half:], experts, -1)
        blocks[which][last] = jnp.concatenate([top, bottom], axis=0)
    while table.shape[0] < experts:
        bit = table.shape[0]
        pairs = [(e, e ^ bit) for e in range(experts)]
        table = jnp.concatenate([table, lax.ppermute(table, "expert", pairs)], axis=0)
    return blocks, table


def ring_scatter(parts, experts, gate):
    half = parts[0].shape[0] // 2
    last = experts // 2
    f32 = jnp.float32
    forward = ring_hop(parts[last][:half].astype(jnp.bfloat16), experts, 1)
    backward = ring_hop(parts[last][half:].astype(jnp.bfloat16), experts, -1)
    for step in range(last - 1, 0, -1):
        mine_f, mine_b = parts[step], parts[experts - step]
        if step == last - 1:
            add_f = jnp.concatenate([mine_f[:half] + forward.astype(f32), mine_f[half:]], axis=0)
            add_b = jnp.concatenate([mine_b[:half], mine_b[half:] + backward.astype(f32)], axis=0)
        else:
            add_f = mine_f + forward.astype(f32)
            add_b = mine_b + backward.astype(f32)
        add_f, add_b = add_f.astype(jnp.bfloat16), add_b.astype(jnp.bfloat16)
        add_f, add_b = after((add_f, add_b), gate(step, forward, backward))
        forward = ring_hop(add_f, experts, 1)
        backward = ring_hop(add_b, experts, -1)
    total = parts[0] + forward.astype(f32) + backward.astype(f32)
    return total.astype(jnp.bfloat16)


def share_table(routing, gate_share, experts):
    ids = jnp.arange(experts, dtype=jnp.int32)
    names = routing[:, None, :] == ids[None, :, None]
    return jnp.sum(jnp.where(names, gate_share[:, None, :], 0.0), axis=2).T


def own_shares(tables, experts):
    me = lax.axis_index("expert")
    ids = jnp.arange(experts, dtype=jnp.int32)
    order = ring_order(experts)
    away = [[order[(order.index(e) + j) % experts] ^ e for j in range(experts)] for e in range(experts)]
    mine = jnp.sum(jnp.where((ids == me)[None, :, None], tables, 0.0), axis=1)
    picks = jnp.array(away, dtype=jnp.int32)[me]
    rows = jnp.sum(jnp.where(picks[:, None, None] == ids[None, :, None], mine[None], 0.0), axis=1)
    return [rows[j][:, None] for j in range(experts)]


def per_device_dense(
    tokens,
    routing,
    gate_scores,
    cotangent,
    w_gate,
    w_up,
    w_down,
    mom_gate,
    mom_up,
    mom_down,
    gossip_round,
):
    tok_rows, feature_width = tokens.shape
    experts = lax.axis_size("expert")
    weight_gate = w_gate[0, 0]
    weight_up = w_up[0, 0]
    weight_down = w_down[0, 0]
    hidden_width = weight_gate.shape[1]
    scale_in = feature_width ** (-0.5)
    scale_hidden = hidden_width ** (-0.5)
    inner_dims = (((1,), (1,)), ((), ()))
    outer_dims = (((0,), (0,)), ((), ()))
    gate_share = gate_scores / jnp.sum(gate_scores, axis=1, keepdims=True)
    table = share_table(routing, gate_share, experts)
    blocks, tables = ring_gather_pair(tokens, cotangent, table, experts)
    tok_blocks, cot_blocks = blocks
    share_blocks = own_shares(after(tables, tok_blocks[experts // 2]), experts)
    weight_both = jnp.concatenate([weight_gate, weight_up], axis=1)

    arrival = [0]
    for step in range(1, experts // 2):
        arrival = arrival + [step, experts - step]
    arrival.append(experts // 2)

    acts, gate_grads, up_grads = [], [], []
    for place in arrival:
        block, cot, share = tok_blocks[place], cot_blocks[place], share_blocks[place]
        both_pre = jnp.dot(block, weight_both, preferred_element_type=jnp.float32) * scale_in
        gate_pre = both_pre[:, :hidden_width]
        up_pre = both_pre[:, hidden_width:]
        sigmoid_gate = jax.nn.sigmoid(gate_pre)
        acts.append((gate_pre * sigmoid_gate * up_pre * share).astype(jnp.bfloat16))
        grad_act = lax.dot_general(
            cot, weight_down, inner_dims, preferred_element_type=jnp.float32
        ) * (share * scale_hidden)
        gate_grads.append(
            (grad_act * up_pre * sigmoid_gate * (1.0 + gate_pre * (1.0 - sigmoid_gate))).astype(
                jnp.bfloat16
            )
        )
        up_grads.append((grad_act * gate_pre * sigmoid_gate).astype(jnp.bfloat16))
    rows_in = jnp.concatenate([tok_blocks[place] for place in arrival], axis=0)
    rows_cot = jnp.concatenate([cot_blocks[place] for place in arrival], axis=0)
    activation = jnp.concatenate(acts, axis=0)
    both_grads = [jnp.concatenate(pair, axis=1) for pair in zip(gate_grads, up_grads)]
    grad_gate_pre = jnp.concatenate(gate_grads, axis=0)
    grad_up_pre = jnp.concatenate(up_grads, axis=0)

    bit_count = lax.axis_size("replica").bit_length() - 1
    bit_now = gossip_round[0] % bit_count

    def swap(local, bit_index, *others):
        return partner_2(after(local, *others) if others else local, "replica", bit_index)

    def mean(one, other):
        total = one.astype(jnp.float32) + other.astype(jnp.float32)
        return (total * 0.5).astype(jnp.bfloat16)

    def with_near(local, swapped):
        result = local
        for bit_index, value in enumerate(swapped):
            result = jnp.where(bit_now == bit_index, mean(local, value), result)
        return lax.optimization_barrier(result)

    def with_far(base, value):
        return jnp.where(bit_now == bit_count - 1, mean(base, value), base)

    def averaged(local, swapped):
        return with_far(with_near(local, swapped[:-1]), swapped[-1])

    grad_down = (
        lax.dot_general(activation, rows_cot, outer_dims, preferred_element_type=jnp.float32)
        * scale_hidden
    )
    down_new, down_moment = momentum_step(weight_down, mom_down[0, 0], grad_down)
    def parts_of(place, *others):
        act, both_grad = after((acts_of[place], both_grads_of[place]), *others)
        out_part = jnp.dot(act, weight_down, preferred_element_type=jnp.float32) * scale_hidden
        back_part = (
            lax.dot_general(both_grad, weight_both, inner_dims, preferred_element_type=jnp.float32)
            * scale_in
        )
        return lax.optimization_barrier(out_part), lax.optimization_barrier(back_part)

    acts_of = dict(zip(arrival, acts))
    both_grads_of = dict(zip(arrival, both_grads))
    first = experts // 2
    out_parts = [None] * experts
    back_parts = [None] * experts
    out_parts[first], back_parts[first] = parts_of(first, down_new)
    grad_gate_pre, grad_up_pre = after(
        (grad_gate_pre, grad_up_pre), out_parts[first], back_parts[first]
    )
    grad_gate = (
        lax.dot_general(rows_in, grad_gate_pre, outer_dims, preferred_element_type=jnp.float32)
        * scale_in
    )
    grad_up = (
        lax.dot_general(rows_in, grad_up_pre, outer_dims, preferred_element_type=jnp.float32)
        * scale_in
    )
    gate_new, gate_moment = momentum_step(weight_gate, mom_gate[0, 0], grad_gate)
    up_new, up_moment = momentum_step(weight_up, mom_up[0, 0], grad_up)
    both_new = jnp.concatenate([gate_new, up_new], axis=0)
    for place in arrival:
        if place != first:
            out_parts[place], back_parts[place] = parts_of(place, down_new, out_parts[first], back_parts[first])

    far = bit_count - 1
    down_far = swap(down_new, far)
    both_far = swap(both_new, far)
    down_near = [swap(down_new, bit_index) for bit_index in range(far)]
    both_near = [swap(both_new, bit_index, down_far) for bit_index in range(far)]

    def gate(step, forward, backward):
        if step == 3:
            return (both_new, down_near)
        if step == 2:
            return (down_far,)
        return ()

    parts = [
        jnp.concatenate([out_part, back_part], axis=0)
        for out_part, back_part in zip(out_parts, back_parts)
    ]
    returns = ring_scatter(parts, experts, gate)
    layer_out, token_grad = returns[:tok_rows], returns[tok_rows:]

    new_down = averaged(down_new, down_near + [down_far])
    both_base = with_near(both_new, both_near)
    new_gate = with_far(both_base[:feature_width], both_far[:feature_width])
    new_up = with_far(both_base[feature_width:], both_far[feature_width:])
    return (
        layer_out,
        token_grad,
        new_gate[None, None],
        new_up[None, None],
        new_down[None, None],
        gate_moment[None, None],
        up_moment[None, None],
        down_moment[None, None],
    )


def per_device(tokens, routing, *others):
    if routing.shape[1] == lax.axis_size("expert"):
        return per_device_dense(tokens, routing, *others)
    return per_device_routed(tokens, routing, *others)


def solution(mesh):
    placed = (
        P(("replica", "expert"), None),
        P(("replica", "expert"), None),
        P(("replica", "expert"), None),
        P(("replica", "expert"), None),
        P("replica", "expert", None, None),
        P("replica", "expert", None, None),
        P("replica", "expert", None, None),
        P("replica", "expert", None, None),
        P("replica", "expert", None, None),
        P("replica", "expert", None, None),
        P("expert"),
    )
    return jax.shard_map(
        per_device,
        mesh=mesh,
        in_specs=placed,
        out_specs=(
            P(("replica", "expert"), None),
            P(("replica", "expert"), None),
            P("replica", "expert", None, None),
            P("replica", "expert", None, None),
            P("replica", "expert", None, None),
            P("replica", "expert", None, None),
            P("replica", "expert", None, None),
            P("replica", "expert", None, None),
        ),
        check_vma=False,
    )
```

```python
import jax
import jax.numpy as jnp
from jax import lax
from jax.sharding import PartitionSpec as P

momentum_beta = 0.9
learn_rate = 0.1


def partner_2(value, axis, stride):
    mask = 2**stride
    pairs = [(source, source ^ mask) for source in range(lax.axis_size(axis))]
    return lax.ppermute(value, axis, pairs)


def expert_forward(rows_in, weight_gate, weight_up, weight_down):
    scale_in = rows_in.shape[1] ** (-0.5)
    scale_hidden = weight_gate.shape[1] ** (-0.5)
    gate_pre = jnp.dot(rows_in, weight_gate, preferred_element_type=jnp.float32) * scale_in
    up_pre = jnp.dot(rows_in, weight_up, preferred_element_type=jnp.float32) * scale_in
    sigmoid_gate = jax.nn.sigmoid(gate_pre)
    activation = (gate_pre * sigmoid_gate * up_pre).astype(jnp.bfloat16)
    produced = (
        jnp.dot(activation, weight_down, preferred_element_type=jnp.float32) * scale_hidden
    ).astype(jnp.bfloat16)
    return (gate_pre, up_pre, sigmoid_gate, activation, produced)


def expert_backward(
    rows_in,
    rows_grad,
    weight_gate,
    weight_up,
    weight_down,
    gate_pre,
    up_pre,
    sigmoid_gate,
    activation,
):
    scale_in = rows_in.shape[1] ** (-0.5)
    scale_hidden = weight_gate.shape[1] ** (-0.5)
    inner_dims = (((1,), (1,)), ((), ()))
    outer_dims = (((0,), (0,)), ((), ()))
    grad_act = (
        lax.dot_general(rows_grad, weight_down, inner_dims, preferred_element_type=jnp.float32)
        * scale_hidden
    )
    grad_gate_pre = (
        grad_act * up_pre * sigmoid_gate * (1.0 + gate_pre * (1.0 - sigmoid_gate))
    ).astype(jnp.bfloat16)
    grad_up_pre = (grad_act * gate_pre * sigmoid_gate).astype(jnp.bfloat16)
    grad_down = (
        lax.dot_general(activation, rows_grad, outer_dims, preferred_element_type=jnp.float32)
        * scale_hidden
    )
    grad_gate = (
        lax.dot_general(rows_in, grad_gate_pre, outer_dims, preferred_element_type=jnp.float32)
        * scale_in
    )
    grad_up = (
        lax.dot_general(rows_in, grad_up_pre, outer_dims, preferred_element_type=jnp.float32)
        * scale_in
    )
    back_sum = lax.dot_general(
        grad_gate_pre, weight_gate, inner_dims, preferred_element_type=jnp.float32
    )
    back_sum = back_sum + lax.dot_general(
        grad_up_pre, weight_up, inner_dims, preferred_element_type=jnp.float32
    )
    rows_back = (back_sum * scale_in).astype(jnp.bfloat16)
    return (rows_back, grad_gate, grad_up, grad_down)


def momentum_step(weight, moment, gradient):
    moment_new = momentum_beta * moment.astype(jnp.float32) + gradient
    weight_new = (weight.astype(jnp.float32) - learn_rate * moment_new).astype(jnp.bfloat16)
    return (weight_new, moment_new.astype(jnp.bfloat16))


def per_device_routed(
    tokens,
    routing,
    gate_scores,
    cotangent,
    w_gate,
    w_up,
    w_down,
    mom_gate,
    mom_up,
    mom_down,
    gossip_round,
):
    tok_rows, feature_width = tokens.shape
    top_count = routing.shape[1]
    experts = lax.axis_size("expert")
    capacity = max(2, min(tok_rows, tok_rows * top_count // experts + 8))
    gate_share = gate_scores / jnp.sum(gate_scores, axis=1, keepdims=True)
    expert_ids = routing.reshape(-1)
    member = (expert_ids[:, None] == jnp.arange(experts, dtype=jnp.int32)[None, :]).astype(
        jnp.int32
    )
    earlier = jnp.sum((jnp.cumsum(member, axis=0) - member) * member, axis=1)
    target = expert_ids * capacity + earlier
    source = jnp.arange(expert_ids.shape[0], dtype=jnp.int32) // top_count
    send_rows = (
        jnp.zeros((experts * capacity, feature_width), jnp.bfloat16).at[target].set(tokens[source])
    )
    weighted = (gate_share.reshape(-1)[:, None] * cotangent[source].astype(jnp.float32)).astype(
        jnp.bfloat16
    )
    send_grad = (
        jnp.zeros((experts * capacity, feature_width), jnp.bfloat16).at[target].set(weighted)
    )
    arrived = lax.all_to_all(
        send_rows.reshape(experts, capacity, feature_width),
        "expert",
        split_axis=0,
        concat_axis=0,
        tiled=True,
    ).reshape(-1, feature_width)
    arrived_grad = lax.all_to_all(
        send_grad.reshape(experts, capacity, feature_width),
        "expert",
        split_axis=0,
        concat_axis=0,
        tiled=True,
    ).reshape(-1, feature_width)
    weight_gate = w_gate[0, 0]
    weight_up = w_up[0, 0]
    weight_down = w_down[0, 0]
    gate_pre, up_pre, sigmoid_gate, activation, produced = expert_forward(
        arrived, weight_gate, weight_up, weight_down
    )
    returned = lax.all_to_all(
        produced.reshape(experts, capacity, feature_width),
        "expert",
        split_axis=0,
        concat_axis=0,
        tiled=True,
    ).reshape(-1, feature_width)
    picked = returned[target].astype(jnp.float32) * gate_share.reshape(-1)[:, None]
    layer_out = jnp.sum(picked.reshape(tok_rows, top_count, feature_width), axis=1).astype(
        jnp.bfloat16
    )
    rows_back, grad_gate, grad_up, grad_down = expert_backward(
        arrived,
        arrived_grad,
        weight_gate,
        weight_up,
        weight_down,
        gate_pre,
        up_pre,
        sigmoid_gate,
        activation,
    )
    returned_grad = lax.all_to_all(
        rows_back.reshape(experts, capacity, feature_width),
        "expert",
        split_axis=0,
        concat_axis=0,
        tiled=True,
    ).reshape(-1, feature_width)
    picked_back = returned_grad[target].astype(jnp.float32)
    token_grad = jnp.sum(picked_back.reshape(tok_rows, top_count, feature_width), axis=1).astype(
        jnp.bfloat16
    )
    gate_new, gate_moment = momentum_step(weight_gate, mom_gate[0, 0], grad_gate)
    up_new, up_moment = momentum_step(weight_up, mom_up[0, 0], grad_up)
    down_new, down_moment = momentum_step(weight_down, mom_down[0, 0], grad_down)
    hidden_width = weight_gate.shape[1]
    stacked = jnp.stack([gate_new, up_new, down_new.reshape(feature_width, hidden_width)], axis=0)
    bit_count = lax.axis_size("replica").bit_length() - 1
    bit_now = gossip_round[0] % bit_count
    partner = stacked
    for bit_index in range(bit_count):
        swapped = partner_2(stacked, "replica", bit_index)
        partner = jnp.where(bit_now == bit_index, swapped, partner)
    averaged = ((stacked.astype(jnp.float32) + partner.astype(jnp.float32)) * 0.5).astype(
        jnp.bfloat16
    )
    new_gate = averaged[0][None, None]
    new_up = averaged[1][None, None]
    new_down = averaged[2].reshape(hidden_width, feature_width)[None, None]
    return (
        layer_out,
        token_grad,
        new_gate,
        new_up,
        new_down,
        gate_moment[None, None],
        up_moment[None, None],
        down_moment[None, None],
    )


def ring_order(experts):
    return list(range(0, experts, 2)) + list(range(experts - 1, 0, -2))


def ring_hop(value, experts, step):
    order = ring_order(experts)
    pairs = [(order[i], order[(i + step) % experts]) for i in range(experts)]
    return lax.ppermute(value, "expert", pairs)


def after(value, *others):
    return lax.optimization_barrier((value,) + others)[0]


def ring_gather_pair(first, second, table, experts):
    last = experts // 2
    blocks = [[None] * experts, [None] * experts]
    moving = [(first, first), (second, second)]
    table = table[None]
    for which, own in enumerate((first, second)):
        blocks[which][0] = own
    for step in range(1, last):
        swapped = None
        if table.shape[0] < experts:
            bit = table.shape[0]
            pairs = [(e, e ^ bit) for e in range(experts)]
            swapped = lax.ppermute(table, "expert", pairs)
        for which in range(2):
            behind, ahead = moving[which]
            behind = ring_hop(behind, experts, 1)
            ahead = ring_hop(ahead, experts, -1)
            if which == 0:
                moving[0] = lax.optimization_barrier((behind, ahead))
                if swapped is not None:
                    table = jnp.concatenate([table, after(swapped, moving[0])], axis=0)
            else:
                moving[1] = after((behind, ahead), moving[0], table)
            blocks[which][experts - step], blocks[which][step] = moving[which]
    blocks[0][last] = ring_hop(moving[0][0], experts, 1)
    blocks[1][last] = ring_hop(moving[1][1], experts, -1)
    while table.shape[0] < experts:
        bit = table.shape[0]
        pairs = [(e, e ^ bit) for e in range(experts)]
        table = jnp.concatenate([table, lax.ppermute(table, "expert", pairs)], axis=0)
    return blocks, table


def ring_scatter(parts, experts, gate):
    half = parts[0].shape[0] // 2
    last = experts // 2
    f32 = jnp.float32
    forward = ring_hop(parts[last][:half].astype(jnp.bfloat16), experts, 1)
    backward = ring_hop(parts[last][half:].astype(jnp.bfloat16), experts, -1)
    for step in range(last - 1, 0, -1):
        mine_f, mine_b = parts[step], parts[experts - step]
        if step == last - 1:
            add_f = jnp.concatenate([mine_f[:half] + forward.astype(f32), mine_f[half:]], axis=0)
            add_b = jnp.concatenate([mine_b[:half], mine_b[half:] + backward.astype(f32)], axis=0)
        else:
            add_f = mine_f + forward.astype(f32)
            add_b = mine_b + backward.astype(f32)
        add_f, add_b = add_f.astype(jnp.bfloat16), add_b.astype(jnp.bfloat16)
        add_f, add_b = after((add_f, add_b), gate(step, forward, backward))
        forward = ring_hop(add_f, experts, 1)
        backward = ring_hop(add_b, experts, -1)
    total = parts[0] + forward.astype(f32) + backward.astype(f32)
    return total.astype(jnp.bfloat16)


def share_table(routing, gate_share, experts):
    ids = jnp.arange(experts, dtype=jnp.int32)
    names = routing[:, None, :] == ids[None, :, None]
    return jnp.sum(jnp.where(names, gate_share[:, None, :], 0.0), axis=2).T


def own_shares(tables, experts):
    me = lax.axis_index("expert")
    ids = jnp.arange(experts, dtype=jnp.int32)
    order = ring_order(experts)
    away = [[order[(order.index(e) + j) % experts] ^ e for j in range(experts)] for e in range(experts)]
    mine = jnp.sum(jnp.where((ids == me)[None, :, None], tables, 0.0), axis=1)
    picks = jnp.array(away, dtype=jnp.int32)[me]
    rows = jnp.sum(jnp.where(picks[:, None, None] == ids[None, :, None], mine[None], 0.0), axis=1)
    return [rows[j][:, None] for j in range(experts)]


def per_device_dense(
    tokens,
    routing,
    gate_scores,
    cotangent,
    w_gate,
    w_up,
    w_down,
    mom_gate,
    mom_up,
    mom_down,
    gossip_round,
):
    tok_rows, feature_width = tokens.shape
    experts = lax.axis_size("expert")
    weight_gate = w_gate[0, 0]
    weight_up = w_up[0, 0]
    weight_down = w_down[0, 0]
    hidden_width = weight_gate.shape[1]
    scale_in = feature_width ** (-0.5)
    scale_hidden = hidden_width ** (-0.5)
    inner_dims = (((1,), (1,)), ((), ()))
    outer_dims = (((0,), (0,)), ((), ()))
    gate_share = gate_scores / jnp.sum(gate_scores, axis=1, keepdims=True)
    table = share_table(routing, gate_share, experts)
    blocks, tables = ring_gather_pair(tokens, cotangent, table, experts)
    tok_blocks, cot_blocks = blocks
    share_blocks = own_shares(tables, experts)
    weight_both = jnp.concatenate([weight_gate, weight_up], axis=1)

    arrival = [0]
    for step in range(1, experts // 2):
        arrival = arrival + [step, experts - step]
    arrival.append(experts // 2)

    acts, gate_grads, up_grads = [], [], []
    for place in arrival:
        block, cot, share = tok_blocks[place], cot_blocks[place], share_blocks[place]
        both_pre = jnp.dot(block, weight_both, preferred_element_type=jnp.float32) * scale_in
        gate_pre = both_pre[:, :hidden_width]
        up_pre = both_pre[:, hidden_width:]
        sigmoid_gate = jax.nn.sigmoid(gate_pre)
        acts.append((gate_pre * sigmoid_gate * up_pre * share).astype(jnp.bfloat16))
        grad_act = lax.dot_general(
            cot, weight_down, inner_dims, preferred_element_type=jnp.float32
        ) * (share * scale_hidden)
        gate_grads.append(
            (grad_act * up_pre * sigmoid_gate * (1.0 + gate_pre * (1.0 - sigmoid_gate))).astype(
                jnp.bfloat16
            )
        )
        up_grads.append((grad_act * gate_pre * sigmoid_gate).astype(jnp.bfloat16))
    rows_in = jnp.concatenate([tok_blocks[place] for place in arrival], axis=0)
    rows_cot = jnp.concatenate([cot_blocks[place] for place in arrival], axis=0)
    activation = jnp.concatenate(acts, axis=0)
    both_grads = [jnp.concatenate(pair, axis=1) for pair in zip(gate_grads, up_grads)]
    grad_gate_pre = jnp.concatenate(gate_grads, axis=0)
    grad_up_pre = jnp.concatenate(up_grads, axis=0)

    bit_count = lax.axis_size("replica").bit_length() - 1
    bit_now = gossip_round[0] % bit_count

    def swap(local, bit_index, *others):
        return partner_2(after(local, *others) if others else local, "replica", bit_index)

    def mean(one, other):
        total = one.astype(jnp.float32) + other.astype(jnp.float32)
        return (total * 0.5).astype(jnp.bfloat16)

    def with_near(local, swapped):
        result = local
        for bit_index, value in enumerate(swapped):
            result = jnp.where(bit_now == bit_index, mean(local, value), result)
        return lax.optimization_barrier(result)

    def with_far(base, value):
        return jnp.where(bit_now == bit_count - 1, mean(base, value), base)

    def averaged(local, swapped):
        return with_far(with_near(local, swapped[:-1]), swapped[-1])

    grad_down = (
        lax.dot_general(activation, rows_cot, outer_dims, preferred_element_type=jnp.float32)
        * scale_hidden
    )
    down_new, down_moment = momentum_step(weight_down, mom_down[0, 0], grad_down)
    def parts_of(place, *others):
        act, both_grad = after((acts_of[place], both_grads_of[place]), *others)
        out_part = jnp.dot(act, weight_down, preferred_element_type=jnp.float32) * scale_hidden
        back_part = (
            lax.dot_general(both_grad, weight_both, inner_dims, preferred_element_type=jnp.float32)
            * scale_in
        )
        return lax.optimization_barrier(out_part), lax.optimization_barrier(back_part)

    acts_of = dict(zip(arrival, acts))
    both_grads_of = dict(zip(arrival, both_grads))
    first = experts // 2
    out_parts = [None] * experts
    back_parts = [None] * experts
    out_parts[first], back_parts[first] = parts_of(first, down_new)
    grad_gate_pre, grad_up_pre = after(
        (grad_gate_pre, grad_up_pre), out_parts[first], back_parts[first]
    )
    grad_gate = (
        lax.dot_general(rows_in, grad_gate_pre, outer_dims, preferred_element_type=jnp.float32)
        * scale_in
    )
    grad_up = (
        lax.dot_general(rows_in, grad_up_pre, outer_dims, preferred_element_type=jnp.float32)
        * scale_in
    )
    gate_new, gate_moment = momentum_step(weight_gate, mom_gate[0, 0], grad_gate)
    up_new, up_moment = momentum_step(weight_up, mom_up[0, 0], grad_up)
    both_new = jnp.concatenate([gate_new, up_new], axis=0)
    for place in arrival:
        if place != first:
            out_parts[place], back_parts[place] = parts_of(place, down_new, out_parts[first], back_parts[first])

    far = bit_count - 1
    down_far = swap(down_new, far)
    both_far = swap(both_new, far)
    down_near = [swap(down_new, bit_index) for bit_index in range(far)]
    both_near = [swap(both_new, bit_index, down_far) for bit_index in range(far)]

    def gate(step, forward, backward):
        if step == 3:
            return (both_new, down_near)
        if step == 2:
            return (down_far,)
        return ()

    parts = [
        jnp.concatenate([out_part, back_part], axis=0)
        for out_part, back_part in zip(out_parts, back_parts)
    ]
    returns = ring_scatter(parts, experts, gate)
    layer_out, token_grad = returns[:tok_rows], returns[tok_rows:]

    new_down = averaged(down_new, down_near + [down_far])
    both_base = with_near(both_new, both_near)
    new_gate = with_far(both_base[:feature_width], both_far[:feature_width])
    new_up = with_far(both_base[feature_width:], both_far[feature_width:])
    return (
        layer_out,
        token_grad,
        new_gate[None, None],
        new_up[None, None],
        new_down[None, None],
        gate_moment[None, None],
        up_moment[None, None],
        down_moment[None, None],
    )


def per_device(tokens, routing, *others):
    if routing.shape[1] == lax.axis_size("expert"):
        return per_device_dense(tokens, routing, *others)
    return per_device_routed(tokens, routing, *others)


def solution(mesh):
    placed = (
        P(("replica", "expert"), None),
        P(("replica", "expert"), None),
        P(("replica", "expert"), None),
        P(("replica", "expert"), None),
        P("replica", "expert", None, None),
        P("replica", "expert", None, None),
        P("replica", "expert", None, None),
        P("replica", "expert", None, None),
        P("replica", "expert", None, None),
        P("replica", "expert", None, None),
        P("expert"),
    )
    return jax.shard_map(
        per_device,
        mesh=mesh,
        in_specs=placed,
        out_specs=(
            P(("replica", "expert"), None),
            P(("replica", "expert"), None),
            P("replica", "expert", None, None),
            P("replica", "expert", None, None),
            P("replica", "expert", None, None),
            P("replica", "expert", None, None),
            P("replica", "expert", None, None),
            P("replica", "expert", None, None),
        ),
        check_vma=False,
    )
```

```python
import jax
import jax.numpy as jnp
from jax import lax
from jax.sharding import PartitionSpec as P

momentum_beta = 0.9
learn_rate = 0.1


def partner_2(value, axis, stride):
    mask = 2**stride
    pairs = [(source, source ^ mask) for source in range(lax.axis_size(axis))]
    return lax.ppermute(value, axis, pairs)


def expert_forward(rows_in, weight_gate, weight_up, weight_down):
    scale_in = rows_in.shape[1] ** (-0.5)
    scale_hidden = weight_gate.shape[1] ** (-0.5)
    gate_pre = jnp.dot(rows_in, weight_gate, preferred_element_type=jnp.float32) * scale_in
    up_pre = jnp.dot(rows_in, weight_up, preferred_element_type=jnp.float32) * scale_in
    sigmoid_gate = jax.nn.sigmoid(gate_pre)
    activation = (gate_pre * sigmoid_gate * up_pre).astype(jnp.bfloat16)
    produced = (
        jnp.dot(activation, weight_down, preferred_element_type=jnp.float32) * scale_hidden
    ).astype(jnp.bfloat16)
    return (gate_pre, up_pre, sigmoid_gate, activation, produced)


def expert_backward(
    rows_in,
    rows_grad,
    weight_gate,
    weight_up,
    weight_down,
    gate_pre,
    up_pre,
    sigmoid_gate,
    activation,
):
    scale_in = rows_in.shape[1] ** (-0.5)
    scale_hidden = weight_gate.shape[1] ** (-0.5)
    inner_dims = (((1,), (1,)), ((), ()))
    outer_dims = (((0,), (0,)), ((), ()))
    grad_act = (
        lax.dot_general(rows_grad, weight_down, inner_dims, preferred_element_type=jnp.float32)
        * scale_hidden
    )
    grad_gate_pre = (
        grad_act * up_pre * sigmoid_gate * (1.0 + gate_pre * (1.0 - sigmoid_gate))
    ).astype(jnp.bfloat16)
    grad_up_pre = (grad_act * gate_pre * sigmoid_gate).astype(jnp.bfloat16)
    grad_down = (
        lax.dot_general(activation, rows_grad, outer_dims, preferred_element_type=jnp.float32)
        * scale_hidden
    )
    grad_gate = (
        lax.dot_general(rows_in, grad_gate_pre, outer_dims, preferred_element_type=jnp.float32)
        * scale_in
    )
    grad_up = (
        lax.dot_general(rows_in, grad_up_pre, outer_dims, preferred_element_type=jnp.float32)
        * scale_in
    )
    back_sum = lax.dot_general(
        grad_gate_pre, weight_gate, inner_dims, preferred_element_type=jnp.float32
    )
    back_sum = back_sum + lax.dot_general(
        grad_up_pre, weight_up, inner_dims, preferred_element_type=jnp.float32
    )
    rows_back = (back_sum * scale_in).astype(jnp.bfloat16)
    return (rows_back, grad_gate, grad_up, grad_down)


def momentum_step(weight, moment, gradient):
    moment_new = momentum_beta * moment.astype(jnp.float32) + gradient
    weight_new = (weight.astype(jnp.float32) - learn_rate * moment_new).astype(jnp.bfloat16)
    return (weight_new, moment_new.astype(jnp.bfloat16))


def per_device_routed(
    tokens,
    routing,
    gate_scores,
    cotangent,
    w_gate,
    w_up,
    w_down,
    mom_gate,
    mom_up,
    mom_down,
    gossip_round,
):
    tok_rows, feature_width = tokens.shape
    top_count = routing.shape[1]
    experts = lax.axis_size("expert")
    capacity = max(2, min(tok_rows, tok_rows * top_count // experts + 8))
    gate_share = gate_scores / jnp.sum(gate_scores, axis=1, keepdims=True)
    expert_ids = routing.reshape(-1)
    member = (expert_ids[:, None] == jnp.arange(experts, dtype=jnp.int32)[None, :]).astype(
        jnp.int32
    )
    earlier = jnp.sum((jnp.cumsum(member, axis=0) - member) * member, axis=1)
    target = expert_ids * capacity + earlier
    source = jnp.arange(expert_ids.shape[0], dtype=jnp.int32) // top_count
    send_rows = (
        jnp.zeros((experts * capacity, feature_width), jnp.bfloat16).at[target].set(tokens[source])
    )
    weighted = (gate_share.reshape(-1)[:, None] * cotangent[source].astype(jnp.float32)).astype(
        jnp.bfloat16
    )
    send_grad = (
        jnp.zeros((experts * capacity, feature_width), jnp.bfloat16).at[target].set(weighted)
    )
    arrived = lax.all_to_all(
        send_rows.reshape(experts, capacity, feature_width),
        "expert",
        split_axis=0,
        concat_axis=0,
        tiled=True,
    ).reshape(-1, feature_width)
    arrived_grad = lax.all_to_all(
        send_grad.reshape(experts, capacity, feature_width),
        "expert",
        split_axis=0,
        concat_axis=0,
        tiled=True,
    ).reshape(-1, feature_width)
    weight_gate = w_gate[0, 0]
    weight_up = w_up[0, 0]
    weight_down = w_down[0, 0]
    gate_pre, up_pre, sigmoid_gate, activation, produced = expert_forward(
        arrived, weight_gate, weight_up, weight_down
    )
    returned = lax.all_to_all(
        produced.reshape(experts, capacity, feature_width),
        "expert",
        split_axis=0,
        concat_axis=0,
        tiled=True,
    ).reshape(-1, feature_width)
    picked = returned[target].astype(jnp.float32) * gate_share.reshape(-1)[:, None]
    layer_out = jnp.sum(picked.reshape(tok_rows, top_count, feature_width), axis=1).astype(
        jnp.bfloat16
    )
    rows_back, grad_gate, grad_up, grad_down = expert_backward(
        arrived,
        arrived_grad,
        weight_gate,
        weight_up,
        weight_down,
        gate_pre,
        up_pre,
        sigmoid_gate,
        activation,
    )
    returned_grad = lax.all_to_all(
        rows_back.reshape(experts, capacity, feature_width),
        "expert",
        split_axis=0,
        concat_axis=0,
        tiled=True,
    ).reshape(-1, feature_width)
    picked_back = returned_grad[target].astype(jnp.float32)
    token_grad = jnp.sum(picked_back.reshape(tok_rows, top_count, feature_width), axis=1).astype(
        jnp.bfloat16
    )
    gate_new, gate_moment = momentum_step(weight_gate, mom_gate[0, 0], grad_gate)
    up_new, up_moment = momentum_step(weight_up, mom_up[0, 0], grad_up)
    down_new, down_moment = momentum_step(weight_down, mom_down[0, 0], grad_down)
    hidden_width = weight_gate.shape[1]
    stacked = jnp.stack([gate_new, up_new, down_new.reshape(feature_width, hidden_width)], axis=0)
    bit_count = lax.axis_size("replica").bit_length() - 1
    bit_now = gossip_round[0] % bit_count
    partner = stacked
    for bit_index in range(bit_count):
        swapped = partner_2(stacked, "replica", bit_index)
        partner = jnp.where(bit_now == bit_index, swapped, partner)
    averaged = ((stacked.astype(jnp.float32) + partner.astype(jnp.float32)) * 0.5).astype(
        jnp.bfloat16
    )
    new_gate = averaged[0][None, None]
    new_up = averaged[1][None, None]
    new_down = averaged[2].reshape(hidden_width, feature_width)[None, None]
    return (
        layer_out,
        token_grad,
        new_gate,
        new_up,
        new_down,
        gate_moment[None, None],
        up_moment[None, None],
        down_moment[None, None],
    )


def ring_order(experts):
    return list(range(0, experts, 2)) + list(range(experts - 1, 0, -2))


def ring_hop(value, experts, step):
    order = ring_order(experts)
    pairs = [(order[i], order[(i + step) % experts]) for i in range(experts)]
    return lax.ppermute(value, "expert", pairs)


def after(value, *others):
    return lax.optimization_barrier((value,) + others)[0]


def ring_gather_pair(first, second, table, experts):
    last = experts // 2
    blocks = [[None] * experts, [None] * experts]
    moving = [(first, first), (second, second)]
    table = table[None]
    for which, own in enumerate((first, second)):
        blocks[which][0] = own
    for step in range(1, last):
        swapped = None
        if table.shape[0] < experts:
            bit = table.shape[0]
            pairs = [(e, e ^ bit) for e in range(experts)]
            swapped = lax.ppermute(table, "expert", pairs)
        for which in range(2):
            behind, ahead = moving[which]
            behind = ring_hop(behind, experts, 1)
            ahead = ring_hop(ahead, experts, -1)
            if which == 0:
                moving[0] = lax.optimization_barrier((behind, ahead))
                if swapped is not None:
                    table = jnp.concatenate([table, after(swapped, moving[0])], axis=0)
            else:
                moving[1] = (after(behind, moving[0], table), after(ahead, moving[0], table))
            blocks[which][experts - step], blocks[which][step] = moving[which]
    blocks[0][last] = ring_hop(moving[0][0], experts, 1)
    blocks[1][last] = ring_hop(moving[1][1], experts, -1)
    while table.shape[0] < experts:
        bit = table.shape[0]
        pairs = [(e, e ^ bit) for e in range(experts)]
        table = jnp.concatenate([table, lax.ppermute(table, "expert", pairs)], axis=0)
    return blocks, table


def ring_scatter(parts, experts, gate):
    half = parts[0].shape[0] // 2
    last = experts // 2
    f32 = jnp.float32
    forward = ring_hop(parts[last][:half].astype(jnp.bfloat16), experts, 1)
    backward = ring_hop(parts[last][half:].astype(jnp.bfloat16), experts, -1)
    for step in range(last - 1, 0, -1):
        mine_f, mine_b = parts[step], parts[experts - step]
        if step == last - 1:
            add_f = jnp.concatenate([mine_f[:half] + forward.astype(f32), mine_f[half:]], axis=0)
            add_b = jnp.concatenate([mine_b[:half], mine_b[half:] + backward.astype(f32)], axis=0)
        else:
            add_f = mine_f + forward.astype(f32)
            add_b = mine_b + backward.astype(f32)
        add_f, add_b = add_f.astype(jnp.bfloat16), add_b.astype(jnp.bfloat16)
        add_f, add_b = after((add_f, add_b), gate(step, forward, backward))
        forward = ring_hop(add_f, experts, 1)
        backward = ring_hop(add_b, experts, -1)
    total = parts[0] + forward.astype(f32) + backward.astype(f32)
    return total.astype(jnp.bfloat16)


def share_table(routing, gate_share, experts):
    ids = jnp.arange(experts, dtype=jnp.int32)
    names = routing[:, None, :] == ids[None, :, None]
    return jnp.sum(jnp.where(names, gate_share[:, None, :], 0.0), axis=2).T


def own_shares(tables, experts):
    me = lax.axis_index("expert")
    ids = jnp.arange(experts, dtype=jnp.int32)
    order = ring_order(experts)
    away = [[order[(order.index(e) + j) % experts] ^ e for j in range(experts)] for e in range(experts)]
    mine = jnp.sum(jnp.where((ids == me)[None, :, None], tables, 0.0), axis=1)
    picks = jnp.array(away, dtype=jnp.int32)[me]
    rows = jnp.sum(jnp.where(picks[:, None, None] == ids[None, :, None], mine[None], 0.0), axis=1)
    return [rows[j][:, None] for j in range(experts)]


def per_device_dense(
    tokens,
    routing,
    gate_scores,
    cotangent,
    w_gate,
    w_up,
    w_down,
    mom_gate,
    mom_up,
    mom_down,
    gossip_round,
):
    tok_rows, feature_width = tokens.shape
    experts = lax.axis_size("expert")
    weight_gate = w_gate[0, 0]
    weight_up = w_up[0, 0]
    weight_down = w_down[0, 0]
    hidden_width = weight_gate.shape[1]
    scale_in = feature_width ** (-0.5)
    scale_hidden = hidden_width ** (-0.5)
    inner_dims = (((1,), (1,)), ((), ()))
    outer_dims = (((0,), (0,)), ((), ()))
    gate_share = gate_scores / jnp.sum(gate_scores, axis=1, keepdims=True)
    table = share_table(routing, gate_share, experts)
    blocks, tables = ring_gather_pair(tokens, cotangent, table, experts)
    tok_blocks, cot_blocks = blocks
    share_blocks = own_shares(tables, experts)
    weight_both = jnp.concatenate([weight_gate, weight_up], axis=1)

    arrival = [0]
    for step in range(1, experts // 2):
        arrival = arrival + [step, experts - step]
    arrival.append(experts // 2)

    acts, gate_grads, up_grads = [], [], []
    for place in arrival:
        block, cot, share = tok_blocks[place], cot_blocks[place], share_blocks[place]
        both_pre = jnp.dot(block, weight_both, preferred_element_type=jnp.float32) * scale_in
        gate_pre = both_pre[:, :hidden_width]
        up_pre = both_pre[:, hidden_width:]
        sigmoid_gate = jax.nn.sigmoid(gate_pre)
        acts.append((gate_pre * sigmoid_gate * up_pre * share).astype(jnp.bfloat16))
        grad_act = lax.dot_general(
            cot, weight_down, inner_dims, preferred_element_type=jnp.float32
        ) * (share * scale_hidden)
        gate_grads.append(
            (grad_act * up_pre * sigmoid_gate * (1.0 + gate_pre * (1.0 - sigmoid_gate))).astype(
                jnp.bfloat16
            )
        )
        up_grads.append((grad_act * gate_pre * sigmoid_gate).astype(jnp.bfloat16))
    rows_in = jnp.concatenate([tok_blocks[place] for place in arrival], axis=0)
    rows_cot = jnp.concatenate([cot_blocks[place] for place in arrival], axis=0)
    activation = jnp.concatenate(acts, axis=0)
    both_grads = [jnp.concatenate(pair, axis=1) for pair in zip(gate_grads, up_grads)]
    grad_gate_pre = jnp.concatenate(gate_grads, axis=0)
    grad_up_pre = jnp.concatenate(up_grads, axis=0)

    bit_count = lax.axis_size("replica").bit_length() - 1
    bit_now = gossip_round[0] % bit_count

    def swap(local, bit_index, *others):
        return partner_2(after(local, *others) if others else local, "replica", bit_index)

    def mean(one, other):
        total = one.astype(jnp.float32) + other.astype(jnp.float32)
        return (total * 0.5).astype(jnp.bfloat16)

    def with_near(local, swapped):
        result = local
        for bit_index, value in enumerate(swapped):
            result = jnp.where(bit_now == bit_index, mean(local, value), result)
        return lax.optimization_barrier(result)

    def with_far(base, value):
        return jnp.where(bit_now == bit_count - 1, mean(base, value), base)

    def averaged(local, swapped):
        return with_far(with_near(local, swapped[:-1]), swapped[-1])

    grad_down = (
        lax.dot_general(activation, rows_cot, outer_dims, preferred_element_type=jnp.float32)
        * scale_hidden
    )
    down_new, down_moment = momentum_step(weight_down, mom_down[0, 0], grad_down)
    def parts_of(place, *others):
        act, both_grad = after((acts_of[place], both_grads_of[place]), *others)
        out_part = jnp.dot(act, weight_down, preferred_element_type=jnp.float32) * scale_hidden
        back_part = (
            lax.dot_general(both_grad, weight_both, inner_dims, preferred_element_type=jnp.float32)
            * scale_in
        )
        return lax.optimization_barrier(out_part), lax.optimization_barrier(back_part)

    acts_of = dict(zip(arrival, acts))
    both_grads_of = dict(zip(arrival, both_grads))
    first = experts // 2
    out_parts = [None] * experts
    back_parts = [None] * experts
    out_parts[first], back_parts[first] = parts_of(first, down_new)
    grad_gate_pre, grad_up_pre = after(
        (grad_gate_pre, grad_up_pre), out_parts[first], back_parts[first]
    )
    grad_gate = (
        lax.dot_general(rows_in, grad_gate_pre, outer_dims, preferred_element_type=jnp.float32)
        * scale_in
    )
    grad_up = (
        lax.dot_general(rows_in, grad_up_pre, outer_dims, preferred_element_type=jnp.float32)
        * scale_in
    )
    gate_new, gate_moment = momentum_step(weight_gate, mom_gate[0, 0], grad_gate)
    up_new, up_moment = momentum_step(weight_up, mom_up[0, 0], grad_up)
    both_new = jnp.concatenate([gate_new, up_new], axis=0)
    for place in arrival:
        if place != first:
            out_parts[place], back_parts[place] = parts_of(place, down_new, out_parts[first], back_parts[first])

    far = bit_count - 1
    down_far = swap(down_new, far)
    both_far = swap(both_new, far)
    down_near = [swap(down_new, bit_index) for bit_index in range(far)]
    both_near = [swap(both_new, bit_index, down_far) for bit_index in range(far)]

    def gate(step, forward, backward):
        if step == 3:
            return (both_new, down_near)
        if step == 2:
            return (down_far,)
        return ()

    parts = [
        jnp.concatenate([out_part, back_part], axis=0)
        for out_part, back_part in zip(out_parts, back_parts)
    ]
    returns = ring_scatter(parts, experts, gate)
    layer_out, token_grad = returns[:tok_rows], returns[tok_rows:]

    new_down = averaged(down_new, down_near + [down_far])
    both_base = with_near(both_new, both_near)
    new_gate = with_far(both_base[:feature_width], both_far[:feature_width])
    new_up = with_far(both_base[feature_width:], both_far[feature_width:])
    return (
        layer_out,
        token_grad,
        new_gate[None, None],
        new_up[None, None],
        new_down[None, None],
        gate_moment[None, None],
        up_moment[None, None],
        down_moment[None, None],
    )


def per_device(tokens, routing, *others):
    if routing.shape[1] == lax.axis_size("expert"):
        return per_device_dense(tokens, routing, *others)
    return per_device_routed(tokens, routing, *others)


def solution(mesh):
    placed = (
        P(("replica", "expert"), None),
        P(("replica", "expert"), None),
        P(("replica", "expert"), None),
        P(("replica", "expert"), None),
        P("replica", "expert", None, None),
        P("replica", "expert", None, None),
        P("replica", "expert", None, None),
        P("replica", "expert", None, None),
        P("replica", "expert", None, None),
        P("replica", "expert", None, None),
        P("expert"),
    )
    return jax.shard_map(
        per_device,
        mesh=mesh,
        in_specs=placed,
        out_specs=(
            P(("replica", "expert"), None),
            P(("replica", "expert"), None),
            P("replica", "expert", None, None),
            P("replica", "expert", None, None),
            P("replica", "expert", None, None),
            P("replica", "expert", None, None),
            P("replica", "expert", None, None),
            P("replica", "expert", None, None),
        ),
        check_vma=False,
    )
```
